32 devices in a mesh: rad: 4 (over z), azi: 2 (over y), ax: 4 (over x, core).
Axes of the slice: x: 2, y: 2, z: 4, core: 2. Of those that a mesh axis runs over, the one named last changes fastest.
Arguments:
- primal: float32 [5, 64, 64, 512], P(None, 'rad', 'azi', 'ax'), may hold values from -1 to 4, as said below
- adjoint: float32 [5, 64, 64, 512], P(None, 'rad', 'azi', 'ax'), may hold values from -6 to 6
- refine_flag: int32 [4, 4, 32], P('rad', 'azi', 'ax'), may hold values 0 or 1
- owner_map: int32 [4, 4, 32], P('rad', 'azi', 'ax'), may hold values from 0 to 31
- migrate_weight: int32 [4, 4, 32], P('rad', 'azi', 'ax'), may hold values from 1 to 16
- neighbor_list: int32 [4, 4, 32, 6], P('rad', 'azi', 'ax'), may hold values from 0 to 511
Outputs:
- indicator: float32 [64, 64, 512], P('rad', 'azi', 'ax')
- block_cost: float32 [4, 4, 32], P('rad', 'azi', 'ax')
- owner_load: float32 [4, 2, 4], P('rad', 'azi', 'ax')
The draws below stay inside these ranges and needn't reach their ends.
Inputs may be any that keep to these rules, and one draw needn't show every extreme that they name: `primal`: density (field 0) lies in [0.5, 2], momenta (fields 1 to 3) in [-1, 1], energy (field 4) in [2, 4].
All inputs are finite; a program needn't handle non-finite values. No bound on the sum of `refine_flag` on one device may be relied on, other than what follows from the above.
Results may differ from the reference program's by a relative error of at most 0.00002.
Values sent between devices are 32-bit elements; how exact they have to be, the bound alone decides.
No kernel may reach another device: no remote copies, remote signals or barrier semaphores. Data moves between devices by JAX's collectives and lax.ppermute only.
A program may use at most 64 MiB of HBM per device.

```python
import math
import jax
import jax.numpy as jnp
import numpy as np
from jax import lax

FIELDS = 5
BLK = 16
CR = 16
CA = 32
CX = 128
NR = 64
NA = 64
NX = 512
NBR = 4
NBA = 4
NBX = 32
NBLK = 512
N_RAD = 4
N_AZI = 2
N_AX = 4


def draw_primal(key, part):
    keys = jax.random.split(key, 3)
    shape = (NR, NA, NX)
    first = jax.random.uniform(keys[0], shape, jnp.float32)
    rough = jax.random.uniform(keys[1], (3, NR, NA, NX), jnp.float32, -1.0, 1.0)
    third = jax.random.uniform(keys[2], shape, jnp.float32)
    density = 0.5 + 1.5 * first
    momenta = rough
    energy = 2.0 + 2.0 * third
    return jnp.concatenate([density[None], momenta, energy[None]], axis=0).astype(jnp.float32)


def set_ends(result, key, smallest, high):
    longest = result.shape.index(max(result.shape))
    spots = []
    for shift in (0, 1):
        where = [jax.random.randint(jax.random.fold_in(key, axis), (), 0, length) for axis, length in enumerate(result.shape)]
        where[longest] = (where[longest] + shift) % result.shape[longest]
        spots.append(tuple(where))
    return result.at[spots[0]].set(smallest).at[spots[1]].set(high)


def block_levels(key, extent, shards, smallest, top_value):
    gain = 1.0
    for axis_at, parts in shards:
        heights = jax.random.uniform(jax.random.fold_in(jax.random.fold_in(key, 6), axis_at), (parts,), jnp.float32, smallest / len(shards), top_value / len(shards))
        gain = gain * jnp.repeat(jnp.exp(heights), extent[axis_at] // parts).reshape((-1,) + (1,) * (len(extent) - 1 - axis_at))
    return gain


def cumulative_ranks(count, slope):
    portions = [(1 << 20) // math.isqrt(rank ** slope) + 1 for rank in range(1, count + 1)]
    spread = 1 + sum(portions) // (1 << 30)
    return np.cumsum(np.array([max(1, weight // spread) for weight in portions]))


def ranked_ids(own_key, extent, count, slope):
    table = cumulative_ranks(count, slope)
    pick = jax.random.randint(jax.random.fold_in(own_key, 1), extent, 0, int(table[count - 1]))
    rank = jnp.searchsorted(jnp.asarray(table, jnp.int32), pick, side="right")
    return jax.random.permutation(jax.random.fold_in(own_key, 2), count)[rank].astype(jnp.int32)


def gaussian(rng, dims, scale, limit, shards=(), kind=jnp.bfloat16):
    loudness = block_levels(rng, dims, shards, -0.22, 0.18) if shards else 1.0
    values = jax.random.normal(rng, dims, jnp.float32) * scale * loudness
    return jnp.minimum(jnp.maximum(values, -limit), limit).astype(kind)


def setup_inputs(seed: int = 0) -> dict:
    streams_of = jax.random.split(jax.random.key(seed), 7)
    primal = draw_primal(jax.random.fold_in(streams_of[6], 71), 0)
    adjoint = gaussian(streams_of[1], (FIELDS, NR, NA, NX), 1.0, 6.0, ((1, 4), (2, 2), (3, 4)), jnp.float32)
    refine_flag = set_ends((jax.random.randint(streams_of[2], (NBR, NBA, NBX), 0, 4) < 1).astype(jnp.int32), jax.random.fold_in(streams_of[2], 1), 0, 1)
    owner_map = set_ends(ranked_ids(streams_of[3], (NBR, NBA, NBX), N_RAD * N_AZI * N_AX, 2), jax.random.fold_in(streams_of[3], 3), 0, (N_RAD * N_AZI * N_AX) - 1).astype(jnp.int32)
    migrate_weight = set_ends(jax.random.randint(streams_of[4], (NBR, NBA, NBX), 1, 17), jax.random.fold_in(streams_of[4], 1), 1, 16).astype(jnp.int32)
    neighbor_list = set_ends(jax.random.randint(streams_of[5], (NBR, NBA, NBX, 6), 0, NBLK), jax.random.fold_in(streams_of[5], 1), 0, NBLK - 1).astype(jnp.int32)
    return {"primal": primal, "adjoint": adjoint, "refine_flag": refine_flag, "owner_map": owner_map, "migrate_weight": migrate_weight, "neighbor_list": neighbor_list}


def euler_flux(face_state, along):
    density = face_state[0]
    momenta = face_state[1:4]
    energy = face_state[4]
    velocity = momenta[along] / density
    kinetic = 0.5 * (momenta[0] * momenta[0] + momenta[1] * momenta[1] + momenta[2] * momenta[2]) / density
    pressure = 0.4 * (energy - kinetic)
    columns = [momenta[along], momenta[0] * velocity, momenta[1] * velocity, momenta[2] * velocity, (energy + pressure) * velocity]
    columns[1 + along] = columns[1 + along] + pressure
    return jnp.stack(columns)


def window(extended, along, start, count, padded_axes):
    pieces = [slice(None)] * 4
    for spatial in padded_axes:
        pieces[spatial] = slice(2, extended.shape[spatial] - 2)
    pieces[along] = slice(start, start + count)
    return extended[tuple(pieces)]


def axis_terms(ext_primal, ext_adjoint, along, padded_axes):
    length = ext_primal.shape[along] - 4
    high = (7.0 * window(ext_primal, along, 1, length + 1, padded_axes) - window(ext_primal, along, 0, length + 1, padded_axes)) / 12.0
    low = (7.0 * window(ext_primal, along, 2, length + 1, padded_axes) - window(ext_primal, along, 3, length + 1, padded_axes)) / 12.0
    fluxes = euler_flux(high + low, along - 1)
    balance = lax.slice_in_dim(fluxes, 1, length + 1, axis=along) - lax.slice_in_dim(fluxes, 0, length, axis=along)
    fourth = (window(ext_adjoint, along, 0, length, padded_axes) - 4.0 * window(ext_adjoint, along, 1, length, padded_axes)
              + 6.0 * window(ext_adjoint, along, 2, length, padded_axes) - 4.0 * window(ext_adjoint, along, 3, length, padded_axes)
              + window(ext_adjoint, along, 4, length, padded_axes)) / 12.0
    return balance, fourth


def extend(fields):
    wrapped = jnp.concatenate([fields[:, :, -2:], fields, fields[:, :, :2]], axis=2)
    return jnp.pad(wrapped, ((0, 0), (2, 2), (0, 0), (2, 2)))


def reference(primal, adjoint, refine_flag, owner_map, migrate_weight, neighbor_list):
    ext_primal = extend(primal)
    ext_adjoint = extend(adjoint)
    balance = jnp.zeros(primal.shape, jnp.float32)
    weight = jnp.zeros(primal.shape, jnp.float32)
    for along in (1, 2, 3):
        part_balance, part_weight = axis_terms(ext_primal, ext_adjoint, along, (1, 2, 3))
        balance = balance + part_balance
        weight = weight + part_weight
    indicator = jnp.abs(jnp.sum(weight * balance, axis=0))
    block_mean = indicator.reshape(NBR, BLK, NBA, BLK, NBX, BLK).mean(axis=(1, 3, 5))
    beside_all = jnp.mean(jnp.take(block_mean.reshape(-1), neighbor_list), axis=-1)
    smooth = 0.5 * block_mean + 0.5 * beside_all
    per_rad = CR // BLK
    per_azi = CA // BLK
    per_ax = CX // BLK
    rad_home = (jnp.arange(NBR, dtype=jnp.int32) // per_rad)[:, None, None]
    azi_home = (jnp.arange(NBA, dtype=jnp.int32) // per_azi)[None, :, None]
    ax_home = (jnp.arange(NBX, dtype=jnp.int32) // per_ax)[None, None, :]
    home = (rad_home * N_AZI + azi_home) * N_AX + ax_home
    moved = (owner_map != home).astype(jnp.float32)
    block_cost = smooth * (1.0 + 7.0 * refine_flag.astype(jnp.float32)) + 0.25 * migrate_weight.astype(jnp.float32) * moved
    devices = N_RAD * N_AZI * N_AX
    totals = jax.ops.segment_sum(block_cost.reshape(-1), owner_map.reshape(-1), num_segments=devices)
    owner_load = (totals / (NBLK // devices)).reshape(N_RAD, N_AZI, N_AX)
    return indicator, block_cost, owner_load
```

```python
import functools

import jax
import jax.numpy as jnp
from jax import lax
from jax.experimental import pallas as pl
from jax.experimental.pallas import tpu as pltpu
from jax.sharding import PartitionSpec as P

BLK = 16
F = 5
LO = 16
AXES = ("rad", "azi", "ax")


def line_pairs(count, first):
    pairs = []
    for i in range(first, count - 1, 2):
        pairs += [(i, i + 1), (i + 1, i)]
    return pairs


def ring(count, step):
    return [(i, (i + step) % count) for i in range(count)]


def pack_kernel(dims, prim, adj, rad_a, rad_b, azi_s, ax_s, buf, sems):
    nr, na, nx = dims
    odd = lax.rem(lax.axis_index("rad"), 2)
    first = jnp.where(odd == 0, nr - 2, 0)
    copies = []
    for t, src in enumerate((prim, adj)):
        rows = pl.ds(t * F, F)
        for i, (a, b) in enumerate(
            (
                (src.at[:, pl.ds(first, 2)], rad_a.at[rows]),
                (src.at[:, pl.ds(nr - 2 - first, 2)], rad_b.at[rows]),
                (src.at[:, :, pl.ds(0, 2)], azi_s.at[rows, :, pl.ds(0, 2)]),
                (src.at[:, :, pl.ds(na - 2, 2)], azi_s.at[rows, :, pl.ds(2, 2)]),
            )
        ):
            copies.append(pltpu.make_async_copy(a, b, sems.at[t, i]))
    loads = []
    for t, src in enumerate((prim, adj)):
        for f in range(F):
            loads.append(pltpu.make_async_copy(src.at[f], buf.at[t * F + f], sems.at[2 + t, f]))
    for c in copies + loads:
        c.start()
    slot = lax.broadcasted_iota(jnp.int32, (8, nx), 1) // 4
    tiles = na // 8
    per = nx // 4
    for f in range(2 * F):
        loads[f].wait()
        for h in range(nr * tiles // per):
            acc = jnp.zeros((8, nx), jnp.float32)
            for j in range(per):
                k = h * per + j
                x = buf[f, k // tiles, pl.ds(8 * (k % tiles), 8), :]
                y = pltpu.roll(x, (4 * j + 2) % nx, 1)
                acc = jnp.where(slot == j, y, acc)
            ax_s[f, h] = acc
    for c in copies:
        c.wait()


def flux(s, along):
    inv = 1.0 / s[0]
    v = s[1 + along] * inv
    kin = (s[1] * s[1] + s[2] * s[2] + s[3] * s[3]) * inv
    p = 0.4 * s[4] - 0.2 * kin
    out = [s[1 + along], s[1] * v, s[2] * v, s[3] * v, (s[4] + p) * v]
    out[1 + along] = out[1 + along] + p
    return out


def face(m1, c, p1, p2):
    return 7.0 * (c + p1) - (m1 + p2)


def main_kernel(
    dims, shape, prim, adj, rad_a, rad_b, azi_l, azi_r, ax_a, ax_b, ax_s, row,
    ind, send, ext, got, fm, frad, fazi, sems,
):
    nr, na, nx = dims
    n_rad, n_azi, n_ax = shape
    i_rad = lax.axis_index("rad")
    i_ax = lax.axis_index("ax")
    odd = lax.rem(i_rad, 2)
    tiles = na // 8
    per = nx // 4
    cells = pl.ds(LO, na)
    copies = []
    for t, src in enumerate((prim, adj)):
        fs = pl.ds(t * F, F)
        at_a = jnp.where(odd == 0, nr + 2, 0)
        for i, (a, b) in enumerate(
            (
                (src, ext.at[fs, pl.ds(2, nr), cells]),
                (rad_a.at[fs], ext.at[fs, pl.ds(at_a, 2), cells]),
                (rad_b.at[fs], ext.at[fs, pl.ds(nr + 2 - at_a, 2), cells]),
                (azi_l.at[fs, :, pl.ds(2, 2)], ext.at[fs, pl.ds(2, nr), pl.ds(LO - 2, 2)]),
                (azi_r.at[fs, :, pl.ds(0, 2)], ext.at[fs, pl.ds(2, nr), pl.ds(LO + na, 2)]),
            )
        ):
            copies.append(pltpu.make_async_copy(a, b, sems.at[t, i]))
    for c in copies:
        c.start()

    lane = lax.broadcasted_iota(jnp.int32, (8, nx), 1)
    part = lane % 4
    even_ax = lax.rem(i_ax, 2) == 0
    halves = nr * tiles // per
    for h in range(halves):
        face_in = []
        for f in range(2 * F):
            a, b = ax_a[f, h], ax_b[f, h]
            left = jnp.where(even_ax, b, a)
            right = jnp.where(even_ax, a, b)
            left = jnp.where(i_ax == 0, 0.0, left)
            right = jnp.where(i_ax == n_ax - 1, 0.0, right)
            got[f, h] = jnp.where(part < 2, left, right)
            if f < F:
                q = jnp.where(part < 2, left, ax_s[f, h])
                face_in.append(
                    face(pltpu.roll(q, 1, 1), q, pltpu.roll(q, nx - 1, 1), pltpu.roll(q, nx - 2, 1))
                )
        ok = part == 1
        face_in[0] = jnp.where(ok, face_in[0], 1.0)
        for f, x in enumerate(flux(face_in, 2)):
            fm[f, h] = x
    for c in copies:
        c.wait()

    zero = jnp.zeros((2 * F, 2, na, nx), jnp.float32)

    @pl.when(i_rad == 0)
    def _():
        ext[:, 0:2, LO:LO + na, :] = zero

    @pl.when(i_rad == n_rad - 1)
    def _():
        ext[:, nr + 2:nr + 4, LO:LO + na, :] = zero

    def rad_flux(r, a):
        rows = pl.ds(LO + 8 * a, 8)
        s = [face(*(ext[f, r + o, rows, :] for o in range(4))) for f in range(F)]
        return flux(s, 0)

    for a in range(tiles):
        for f, x in enumerate(rad_flux(0, a)):
            frad[f, a] = x

    def azi_flux(r, a):
        s = [face(*(ext[f, r + 2, pl.ds(LO + 8 * a + o, 8), :] for o in (-1, 0, 1, 2))) for f in range(F)]
        return flux(s, 1)

    def body(r, sums):
        for a in range(-1, tiles):
            for f, x in enumerate(azi_flux(r, a)):
                fazi[f, pl.ds(LO + 8 * a, 8), :] = x
        out = []
        for a in range(tiles):
            rows = pl.ds(LO + 8 * a, 8)
            k = r * tiles + a
            h = k // per
            j = lax.rem(k, per)
            turn = lax.rem(2 * nx - (4 * j + 2), nx)
            turn_f = lax.rem(2 * nx - (4 * j + 2), nx)
            up = rad_flux(r + 1, a)
            bal = []
            for f in range(F):
                bal.append(up[f] - frad[f, a])
                frad[f, a] = up[f]
            for f in range(F):
                bal[f] = bal[f] + (fazi[f, rows, :] - fazi[f, pl.ds(LO + 8 * a - 1, 8), :])
            s = []
            for f in range(F):
                x = ext[f, r + 2, rows, :]
                hal = pltpu.roll(got[f, h], turn, 1)
                s.append(
                    face(
                        pltpu.roll(jnp.where(lane == nx - 1, hal, x), 1, 1),
                        x,
                        pltpu.roll(jnp.where(lane == 0, hal, x), nx - 1, 1),
                        pltpu.roll(jnp.where(lane < 2, hal, x), nx - 2, 1),
                    )
                )
            for f, x in enumerate(flux(s, 2)):
                edge = pltpu.roll(fm[f, h], turn_f, 1)
                low = pltpu.roll(jnp.where(lane == nx - 1, edge, x), 1, 1)
                bal[f] = bal[f] + (x - low)
            total = None
            for f in range(F):
                g = F + f
                z = ext[g, r + 2, rows, :]
                hal = pltpu.roll(got[g, h], turn, 1)
                up1 = pltpu.roll(jnp.where(lane == 0, hal, z), nx - 1, 1)
                up2 = pltpu.roll(jnp.where(lane < 2, hal, z), nx - 2, 1)
                dn1 = pltpu.roll(jnp.where(lane == nx - 1, hal, z), 1, 1)
                dn2 = pltpu.roll(jnp.where(lane >= nx - 2, hal, z), 2, 1)
                two = (
                    (ext[g, r, rows, :] + ext[g, r + 4, rows, :])
                    + (ext[g, r + 2, pl.ds(LO + 8 * a - 2, 8), :] + ext[g, r + 2, pl.ds(LO + 8 * a + 2, 8), :])
                    + (dn2 + up2)
                )
                one = (
                    (ext[g, r + 1, rows, :] + ext[g, r + 3, rows, :])
                    + (ext[g, r + 2, pl.ds(LO + 8 * a - 1, 8), :] + ext[g, r + 2, pl.ds(LO + 8 * a + 1, 8), :])
                    + (dn1 + up1)
                )
                w = (two - 4.0 * one + 18.0 * z) * bal[f]
                total = w if total is None else total + w
            total = jnp.abs(total) * (1.0 / 144.0)
            ind[r, pl.ds(8 * a, 8), :] = total
            out.append(sums[a] + total)
        return tuple(out)

    sums = lax.fori_loop(0, nr, body, tuple(jnp.zeros((8, nx), jnp.float32) for _ in range(tiles)))

    groups = nx // BLK
    halves_a = na // BLK
    per_tile = BLK // 8
    means = jnp.zeros((8, nx), jnp.float32)
    for b in range(halves_a):
        t = sums[b * per_tile]
        for i in range(1, per_tile):
            t = t + sums[b * per_tile + i]
        t = jnp.broadcast_to(jnp.sum(t, axis=0, keepdims=True), (8, nx))
        for sh in (8, 4, 2, 1):
            t = t + pltpu.roll(t, nx - sh, 1)
        t = jnp.take_along_axis(t, (lane % groups) * BLK, axis=1)
        means = jnp.where(lane // groups == b, t, means)
    means = means * (1.0 / BLK**3)
    head = jnp.broadcast_to(row[:, 0:nx], (8, nx))
    head = jnp.where(lane < groups * halves_a, means, head)
    tail = jnp.broadcast_to(row[:, nx:2 * nx], (8, nx))
    for d in range(send.shape[0] // 8):
        send[pl.ds(8 * d, 8), 0:nx] = head
        send[pl.ds(8 * d, 8), nx:2 * nx] = tail


def final_kernel(n_loc, per_ax, data, cost, load):
    n_dev = data.shape[0]
    nx = data.shape[1] // 2
    me = (lax.axis_index("rad") * lax.axis_size("azi") + lax.axis_index("azi")) * lax.axis_size(
        "ax"
    ) + lax.axis_index("ax")
    lane = lax.broadcasted_iota(jnp.int32, (8, nx), 1)
    sub = lax.broadcasted_iota(jnp.int32, (8, nx), 0)

    def group(g, carry):
        acc_load, acc_cost = carry
        rows = pl.ds(pl.multiple_of(8 * g, 8), 8)
        head = data[rows, 0:nx]
        tail = data[rows, nx:2 * nx]
        spot = head.astype(jnp.int32)
        dev = spot // n_loc
        pos = spot - dev * n_loc

        def look(d8, acc):
            table = data[pl.ds(pl.multiple_of(8 * d8, 8), 8), 0:nx]
            for i in range(8):
                t = jnp.broadcast_to(table[i:i + 1, :], (8, nx))
                v = jnp.take_along_axis(t, pos, axis=1)
                acc = jnp.where(dev == d8 * 8 + i, v, acc)
            return acc

        val = lax.fori_loop(0, n_dev // 8, look, jnp.zeros((8, nx), jnp.float32), unroll=n_dev <= 32)
        beside = None
        for j in range(6):
            x = pltpu.roll(val, nx - n_loc * (1 + j), 1)
            beside = x if beside is None else beside + x
        smooth = 0.5 * head + (0.5 / 6.0) * beside
        refine = pltpu.roll(head, nx - 7 * n_loc, 1)
        owner = tail.astype(jnp.int32)
        weight = pltpu.roll(tail, nx - n_loc, 1)
        home = sub + 8 * g
        c = smooth * (1.0 + 7.0 * refine) + jnp.where(owner != home, 0.25 * weight, 0.0)
        ok = lane < n_loc
        acc_load = acc_load + jnp.where(ok & (owner == me), c, 0.0)
        acc_cost = acc_cost + jnp.where(home == me, c, 0.0)
        return acc_load, acc_cost

    zero = jnp.zeros((8, nx), jnp.float32)
    acc_load, acc_cost = lax.fori_loop(0, n_dev // 8, group, (zero, zero), unroll=n_dev <= 32)
    own = jnp.sum(acc_cost, axis=0, keepdims=True)
    for b in range(n_loc // per_ax):
        x = own if b == 0 else pltpu.roll(own, nx - b * per_ax, 1)
        cost[0, pl.ds(b, 1), :] = x[:, 0:per_ax]
    total = jnp.sum(jnp.sum(acc_load, axis=0, keepdims=True), axis=1, keepdims=True) * (1.0 / n_loc)
    load[0] = total


def on_device(primal, adjoint, refine_flag, owner_map, migrate_weight, neighbor_list):
    _, nr, na, nx = primal.shape
    dims = (nr, na, nx)
    n_rad, n_azi, n_ax = (lax.axis_size(a) for a in AXES)
    n_dev = n_rad * n_azi * n_ax
    tiles = na // 8
    halves = nr * tiles // (nx // 4)
    f32 = functools.partial(jax.ShapeDtypeStruct, dtype=jnp.float32)
    anyspec = pl.BlockSpec(memory_space=pl.ANY)
    hbm = pl.BlockSpec(memory_space=pltpu.HBM)
    vmem = pl.BlockSpec(memory_space=pltpu.VMEM)

    rad_a, rad_b, azi_s, ax_s = pl.pallas_call(
        functools.partial(pack_kernel, dims),
        out_shape=(
            f32((2 * F, 2, na, nx)),
            f32((2 * F, 2, na, nx)),
            f32((2 * F, nr, 4, nx)),
            f32((2 * F, halves, 8, nx)),
        ),
        in_specs=[hbm, hbm],
        out_specs=(anyspec, anyspec, anyspec, vmem),
        scratch_shapes=[
            pltpu.VMEM((2 * F, nr, na, nx), jnp.float32),
            pltpu.SemaphoreType.DMA((4, F)),
        ],
        compiler_params=pltpu.CompilerParams(vmem_limit_bytes=16 << 20),
        name="pack",
    )(primal, adjoint)

    ax_a = lax.ppermute(ax_s, "ax", line_pairs(n_ax, 0))
    ax_b = lax.ppermute(ax_s, "ax", line_pairs(n_ax, 1))
    azi_l = lax.ppermute(azi_s, "azi", ring(n_azi, 1))
    azi_r = azi_l if n_azi == 2 else lax.ppermute(azi_s, "azi", ring(n_azi, -1))
    rad_a = lax.ppermute(rad_a, "rad", line_pairs(n_rad, 0))
    rad_b = lax.ppermute(rad_b, "rad", line_pairs(n_rad, 1))

    per_rad, per_azi, per_ax = nr // BLK, na // BLK, nx // BLK
    n_loc = per_rad * per_azi * per_ax
    blocks_azi, blocks_ax = per_azi * n_azi, per_ax * n_ax
    b_rad = neighbor_list // (blocks_azi * blocks_ax)
    b_azi = neighbor_list // blocks_ax % blocks_azi
    b_ax = neighbor_list % blocks_ax
    device = (b_rad // per_rad * n_azi + b_azi // per_azi) * n_ax + b_ax // per_ax
    local = (b_rad % per_rad * per_azi + b_azi % per_azi) * per_ax + b_ax % per_ax
    spot = (device * n_loc + local).reshape(n_loc, 6).T.reshape(-1)
    row = jnp.concatenate(
        [
            jnp.zeros((n_loc,), jnp.int32),
            spot,
            refine_flag.reshape(-1),
            owner_map.reshape(-1),
            migrate_weight.reshape(-1),
        ]
    ).astype(jnp.float32)
    row = jnp.pad(row, (0, 2 * nx - row.shape[0]))[None]

    indicator, send = pl.pallas_call(
        functools.partial(main_kernel, dims, (n_rad, n_azi, n_ax)),
        out_shape=(f32(dims), f32((n_dev, 2 * nx))),
        in_specs=[hbm] * 2 + [anyspec] * 4 + [vmem] * 4,
        out_specs=(vmem, vmem),
        scratch_shapes=[
            pltpu.VMEM((2 * F, nr + 4, LO + na + 8, nx), jnp.float32),
            pltpu.VMEM((2 * F, halves, 8, nx), jnp.float32),
            pltpu.VMEM((F, halves, 8, nx), jnp.float32),
            pltpu.VMEM((F, tiles, 8, nx), jnp.float32),
            pltpu.VMEM((F, LO + na, nx), jnp.float32),
            pltpu.SemaphoreType.DMA((2, 5)),
        ],
        compiler_params=pltpu.CompilerParams(vmem_limit_bytes=32 << 20),
        name="stencil",
    )(primal, adjoint, rad_a, rad_b, azi_l, azi_r, ax_a, ax_b, ax_s, row)

    data = lax.all_to_all(send, AXES, 0, 0, tiled=True)

    cost, load = pl.pallas_call(
        functools.partial(final_kernel, n_loc, per_ax),
        out_shape=(f32((per_rad, per_azi, per_ax)), f32((1, 1, 1))),
        in_specs=[vmem],
        out_specs=(vmem, vmem),
        name="blocks",
    )(data)
    return indicator, cost, load


def solution(mesh):
    spec = P("rad", "azi", "ax")
    field = P(None, "rad", "azi", "ax")
    return jax.shard_map(
        on_device,
        mesh=mesh,
        in_specs=(field, field, spec, spec, spec, P("rad", "azi", "ax", None)),
        out_specs=(spec, spec, spec),
        check_vma=False,
    )
```

```python
import functools

import jax
import jax.numpy as jnp
from jax import lax
from jax.experimental import pallas as pl
from jax.experimental.pallas import tpu as pltpu
from jax.sharding import PartitionSpec as P

BLK = 16
F = 5
AXES = ("rad", "azi", "ax")


def line_pairs(count, first):
    pairs = []
    for i in range(first, count - 1, 2):
        pairs += [(i, i + 1), (i + 1, i)]
    return pairs


def ring(count, step):
    return [(i, (i + step) % count) for i in range(count)]


def edge_kernel(dims, prim, adj, rad_a, rad_b, azi_s, sems):
    nr, na, nx = dims
    odd = lax.rem(lax.axis_index("rad"), 2)
    first = jnp.where(odd == 0, nr - 2, 0)
    copies = []
    for t, src in enumerate((prim, adj)):
        rows = pl.ds(t * F, F)
        for i, (a, b) in enumerate(
            (
                (src.at[:, pl.ds(first, 2)], rad_a.at[rows]),
                (src.at[:, pl.ds(nr - 2 - first, 2)], rad_b.at[rows]),
                (src.at[:, :, pl.ds(0, 2)], azi_s.at[rows, :, pl.ds(0, 2)]),
                (src.at[:, :, pl.ds(na - 2, 2)], azi_s.at[rows, :, pl.ds(2, 2)]),
            )
        ):
            copies.append(pltpu.make_async_copy(a, b, sems.at[t, i]))
    for c in copies:
        c.start()
    for c in copies:
        c.wait()


def lane_kernel(dims, prim, adj, ax_s):
    nr, na, nx = dims
    slot = lax.broadcasted_iota(jnp.int32, (8, nx), 1) >> 2
    tiles = na // 8
    per = nx // 4
    for t, src in enumerate((prim, adj)):
        for f in range(F):
            for h in range(nr * tiles // per):
                acc = jnp.zeros((8, nx), jnp.float32)
                for j in range(per):
                    k = h * per + j
                    x = src[f, k // tiles, pl.ds(8 * (k % tiles), 8), :]
                    acc = jnp.where(slot == j, pltpu.roll(x, (4 * j + 2) % nx, 1), acc)
                ax_s[t * F + f, h] = acc


def flux(s, along):
    inv = 1.0 / s[0]
    v = s[1 + along] * inv
    kin = (s[1] * s[1] + s[2] * s[2] + s[3] * s[3]) * inv
    p = 0.4 * s[4] - 0.2 * kin
    out = [s[1 + along], s[1] * v, s[2] * v, s[3] * v, (s[4] + p) * v]
    out[1 + along] = out[1 + along] + p
    return out


def face(m1, c, p1, p2):
    return 7.0 * (c + p1) - (m1 + p2)


def split3(x):
    hi = x.astype(jnp.bfloat16)
    x = x - hi.astype(jnp.float32)
    mid = x.astype(jnp.bfloat16)
    x = x - mid.astype(jnp.float32)
    return hi, mid, x.astype(jnp.bfloat16)


def taps(rows, cols, table):
    out = jnp.zeros(rows.shape, jnp.float32)
    for step, value in table.items():
        out = jnp.where(rows - cols == step, value, out)
    return out


UPPER = {-1: -1.0, 0: 7.0, 1: 7.0, 2: -1.0}
LOWER = {-2: -1.0, -1: 7.0, 0: 7.0, 1: -1.0}
FOURTH = {-2: 1.0, -1: -4.0, 0: 6.0, 1: -4.0, 2: 1.0}


def axial_kernel(dims, n_ax, prim, adj, ax_a, ax_b, bw, got, lhs, rhs, sums):
    nr, na, nx = dims
    i_ax = lax.axis_index("ax")
    even_ax = lax.rem(i_ax, 2) == 0
    lane = lax.broadcasted_iota(jnp.int32, (8, nx), 1)
    part = lane & 3
    slot = lane >> 2
    tiles = na // 8
    per = nx // 4
    halves = nr * tiles // per
    size = nr * na

    i = lax.broadcasted_iota(jnp.int32, (nx, nx), 0)
    c = lax.broadcasted_iota(jnp.int32, (nx, nx), 1)
    p = i & 3
    halo = jnp.where(p < 2, p - 2, p - 2 + nx)
    for n, table in enumerate((UPPER, LOWER, FOURTH)):
        own = taps(i, c, table).astype(jnp.bfloat16)
        far = taps(halo, c, table).astype(jnp.bfloat16)
        for k in range(3):
            rhs[pl.ds(2 * k * nx, nx), pl.ds(n * nx, nx)] = own
            rhs[pl.ds((2 * k + 1) * nx, nx), pl.ds(n * nx, nx)] = far

    for h in range(halves):
        for f in range(2 * F):
            a, b = ax_a[f, h], ax_b[f, h]
            g = jnp.where(part < 2, jnp.where(even_ax, b, a), jnp.where(even_ax, a, b))
            for k, x in enumerate(split3(g)):
                got[k, f, h] = x.astype(jnp.float32)

    def build(t, src, f):
        g0 = t * F + f
        for r in range(nr):
            h, j0 = r * tiles // per, r * tiles % per
            rows = pl.ds(pl.multiple_of(g0 * size, size) + r * na, na)
            for k, x in enumerate(split3(src[f, r])):
                lhs[rows, pl.ds(2 * k * nx, nx)] = x
                g = got[k, g0, h]
                y = [jnp.where(slot == j0 + a, g, 0.0) for a in range(tiles)]
                lhs[rows, pl.ds((2 * k + 1) * nx, nx)] = jnp.concatenate(y, axis=0).astype(jnp.bfloat16)

    for t, src in enumerate((prim, adj)):
        lax.fori_loop(0, F, lambda f, c, t=t, src=src: (build(t, src, f), c)[1], 0)
    sums[...] = jnp.dot(
        lhs[0:F * size, :], rhs[:, 0:2 * nx], preferred_element_type=jnp.float32
    )
    bw[F:2 * F] = jnp.dot(
        lhs[F * size:2 * F * size, :], rhs[:, 2 * nx:3 * nx], preferred_element_type=jnp.float32
    ).reshape(F, nr, na, nx)

    def body(r, carry):
        for a in range(tiles):
            at = [pl.ds(f * size + pl.multiple_of(r * na, na) + 8 * a, 8) for f in range(F)]
            up = flux([sums[q, 0:nx] for q in at], 2)
            low = flux([sums[q, nx:2 * nx] for q in at], 2)
            for f in range(F):
                bw[f, r, pl.ds(8 * a, 8), :] = up[f] - low[f]
        return carry

    lax.fori_loop(0, nr, body, 0)


def main_kernel(
    dims, prim, adj, bw, rad_a, rad_b, azi_l, azi_r, row, ind, send, far, low, top, frad, fazi
):
    nr, na, nx = dims
    odd = lax.rem(lax.axis_index("rad"), 2)
    tiles = na // 8
    last = 8 * (tiles - 1)
    lane = lax.broadcasted_iota(jnp.int32, (8, nx), 1)
    for f in range(2 * F):
        for i in range(2):
            a, b = rad_a[f, i], rad_b[f, i]
            far[f, i] = jnp.where(odd == 0, b, a)
            far[f, 2 + i] = jnp.where(odd == 0, a, b)

    def edges(r, carry):
        for t, src in enumerate((prim, adj)):
            for f in range(F):
                g = t * F + f
                low[g, r, 14:16, :] = azi_l[g, r, 2:4, :]
                low[g, r, 16:24, :] = src[f, r, 0:8, :]
                top[g, r, 0:8, :] = src[f, r, last:last + 8, :]
                top[g, r, 8:10, :] = azi_r[g, r, 0:2, :]
        return carry

    lax.fori_loop(0, nr, edges, 0)

    def cell(g, r, a, dr=0, da=0):
        if isinstance(r, int):
            if r + dr < 0:
                return far[g, 2 + r + dr, pl.ds(8 * a, 8), :]
            if r + dr >= nr:
                return far[g, 2 + r + dr - nr, pl.ds(8 * a, 8), :]
        if da < 0 and a == 0:
            return low[g, r, pl.ds(16 + da, 8), :]
        if da > 0 and a == tiles - 1:
            return top[g, r, pl.ds(da, 8), :]
        src = (prim, adj)[g // F]
        return src[g % F, r + dr, pl.ds(8 * a + da, 8), :]

    def rad_flux(r, a):
        return flux([face(*(cell(f, r, a, dr=o) for o in (-1, 0, 1, 2))) for f in range(F)], 0)

    def azi_flux(r, a):
        return flux([face(*(cell(f, r, a, da=o) for o in (-1, 0, 1, 2))) for f in range(F)], 1)

    def low_flux(r):
        return flux([face(*(low[f, r, pl.ds(8 + o, 8), :] for o in (-1, 0, 1, 2))) for f in range(F)], 1)

    for a in range(tiles):
        for f, x in enumerate(rad_flux(-1, a)):
            frad[f, a] = x

    def plane(r, sums):
        for f, x in enumerate(low_flux(r)):
            fazi[f, 0:8, :] = x
        for a in range(tiles):
            for f, x in enumerate(azi_flux(r, a)):
                fazi[f, pl.ds(8 + 8 * a, 8), :] = x
        out = []
        for a in range(tiles):
            mine = pl.ds(8 * a, 8)
            up = rad_flux(r, a)
            total = None
            for f in range(F):
                bal = bw[f, r, mine, :] + (up[f] - frad[f, a])
                frad[f, a] = up[f]
                bal = bal + (fazi[f, pl.ds(8 * a + 8, 8), :] - fazi[f, pl.ds(8 * a + 7, 8), :])
                g = F + f
                two = (cell(g, r, a, dr=-2) + cell(g, r, a, dr=2)) + (
                    cell(g, r, a, da=-2) + cell(g, r, a, da=2)
                )
                one = (cell(g, r, a, dr=-1) + cell(g, r, a, dr=1)) + (
                    cell(g, r, a, da=-1) + cell(g, r, a, da=1)
                )
                w = (two - 4.0 * one + 12.0 * cell(g, r, a) + bw[g, r, mine, :]) * bal
                total = w if total is None else total + w
            total = jnp.abs(total) * (1.0 / 144.0)
            ind[r, mine, :] = total
            out.append(sums[a] + total)
        return tuple(out)

    sums = tuple(jnp.zeros((8, nx), jnp.float32) for _ in range(tiles))
    for r in (0, 1):
        sums = plane(r, sums)
    sums = lax.fori_loop(2, nr - 2, plane, sums)
    for r in (nr - 2, nr - 1):
        sums = plane(r, sums)

    groups = nx // BLK
    halves_a = na // BLK
    per_tile = BLK // 8
    means = jnp.zeros((8, nx), jnp.float32)
    for b in range(halves_a):
        t = sums[b * per_tile]
        for i in range(1, per_tile):
            t = t + sums[b * per_tile + i]
        t = jnp.broadcast_to(jnp.sum(t, axis=0, keepdims=True), (8, nx))
        for sh in (8, 4, 2, 1):
            t = t + pltpu.roll(t, nx - sh, 1)
        t = jnp.take_along_axis(t, (lane % groups) * BLK, axis=1)
        means = jnp.where(lane // groups == b, t, means)
    means = means * (1.0 / BLK**3)
    head = jnp.broadcast_to(row[:, 0:nx], (8, nx))
    head = jnp.where(lane < groups * halves_a, means, head)
    tail = jnp.broadcast_to(row[:, nx:2 * nx], (8, nx))
    for d in range(send.shape[0] // 8):
        send[pl.ds(8 * d, 8), 0:nx] = head
        send[pl.ds(8 * d, 8), nx:2 * nx] = tail


def final_kernel(n_loc, per_ax, data, cost, load):
    n_dev = data.shape[0]
    nx = data.shape[1] // 2
    me = (lax.axis_index("rad") * lax.axis_size("azi") + lax.axis_index("azi")) * lax.axis_size(
        "ax"
    ) + lax.axis_index("ax")
    lane = lax.broadcasted_iota(jnp.int32, (8, nx), 1)
    sub = lax.broadcasted_iota(jnp.int32, (8, nx), 0)

    def group(g, carry):
        acc_load, acc_cost = carry
        rows = pl.ds(pl.multiple_of(8 * g, 8), 8)
        head = data[rows, 0:nx]
        tail = data[rows, nx:2 * nx]
        spot = head.astype(jnp.int32)
        dev = spot // n_loc
        pos = spot - dev * n_loc

        def look(d8, acc):
            table = data[pl.ds(pl.multiple_of(8 * d8, 8), 8), 0:nx]
            for i in range(8):
                t = jnp.broadcast_to(table[i:i + 1, :], (8, nx))
                v = jnp.take_along_axis(t, pos, axis=1)
                acc = jnp.where(dev == d8 * 8 + i, v, acc)
            return acc

        val = lax.fori_loop(0, n_dev // 8, look, jnp.zeros((8, nx), jnp.float32), unroll=n_dev <= 32)
        beside = None
        for j in range(6):
            x = pltpu.roll(val, nx - n_loc * (1 + j), 1)
            beside = x if beside is None else beside + x
        smooth = 0.5 * head + (0.5 / 6.0) * beside
        refine = pltpu.roll(head, nx - 7 * n_loc, 1)
        owner = tail.astype(jnp.int32)
        weight = pltpu.roll(tail, nx - n_loc, 1)
        home = sub + 8 * g
        c = smooth * (1.0 + 7.0 * refine) + jnp.where(owner != home, 0.25 * weight, 0.0)
        ok = lane < n_loc
        acc_load = acc_load + jnp.where(ok & (owner == me), c, 0.0)
        acc_cost = acc_cost + jnp.where(home == me, c, 0.0)
        return acc_load, acc_cost

    zero = jnp.zeros((8, nx), jnp.float32)
    acc_load, acc_cost = lax.fori_loop(0, n_dev // 8, group, (zero, zero), unroll=n_dev <= 32)
    own = jnp.sum(acc_cost, axis=0, keepdims=True)
    for b in range(n_loc // per_ax):
        x = own if b == 0 else pltpu.roll(own, nx - b * per_ax, 1)
        cost[0, pl.ds(b, 1), :] = x[:, 0:per_ax]
    total = jnp.sum(jnp.sum(acc_load, axis=0, keepdims=True), axis=1, keepdims=True) * (1.0 / n_loc)
    load[0] = total


def on_device(primal, adjoint, refine_flag, owner_map, migrate_weight, neighbor_list):
    _, nr, na, nx = primal.shape
    dims = (nr, na, nx)
    n_rad, n_azi, n_ax = (lax.axis_size(a) for a in AXES)
    n_dev = n_rad * n_azi * n_ax
    tiles = na // 8
    halves = nr * tiles // (nx // 4)
    f32 = functools.partial(jax.ShapeDtypeStruct, dtype=jnp.float32)
    anyspec = pl.BlockSpec(memory_space=pl.ANY)
    hbm = pl.BlockSpec(memory_space=pltpu.HBM)
    vmem = pl.BlockSpec(memory_space=pltpu.VMEM)

    rad_a, rad_b, azi_s = pl.pallas_call(
        functools.partial(edge_kernel, dims),
        out_shape=(f32((2 * F, 2, na, nx)), f32((2 * F, 2, na, nx)), f32((2 * F, nr, 4, nx))),
        in_specs=[hbm, hbm],
        out_specs=(vmem, vmem, vmem),
        scratch_shapes=[pltpu.SemaphoreType.DMA((2, 4))],
        name="edges",
    )(primal, adjoint)
    ax_s = pl.pallas_call(
        functools.partial(lane_kernel, dims),
        out_shape=f32((2 * F, halves, 8, nx)),
        in_specs=[vmem, vmem],
        out_specs=vmem,
        compiler_params=pltpu.CompilerParams(vmem_limit_bytes=16 << 20),
        name="lanes",
    )(primal, adjoint)

    ax_a = lax.ppermute(ax_s, "ax", line_pairs(n_ax, 0))
    ax_b = lax.ppermute(ax_s, "ax", line_pairs(n_ax, 1))
    azi_l = lax.ppermute(azi_s, "azi", ring(n_azi, 1))
    azi_r = azi_l if n_azi == 2 else lax.ppermute(azi_s, "azi", ring(n_azi, -1))
    rad_a = lax.ppermute(rad_a, "rad", line_pairs(n_rad, 0))
    rad_b = lax.ppermute(rad_b, "rad", line_pairs(n_rad, 1))

    per_rad, per_azi, per_ax = nr // BLK, na // BLK, nx // BLK
    n_loc = per_rad * per_azi * per_ax
    blocks_azi, blocks_ax = per_azi * n_azi, per_ax * n_ax
    b_rad = neighbor_list // (blocks_azi * blocks_ax)
    b_azi = neighbor_list // blocks_ax % blocks_azi
    b_ax = neighbor_list % blocks_ax
    device = (b_rad // per_rad * n_azi + b_azi // per_azi) * n_ax + b_ax // per_ax
    local = (b_rad % per_rad * per_azi + b_azi % per_azi) * per_ax + b_ax % per_ax
    spot = (device * n_loc + local).reshape(n_loc, 6).T.reshape(-1)
    row = jnp.concatenate(
        [
            jnp.zeros((n_loc,), jnp.int32),
            spot,
            refine_flag.reshape(-1),
            owner_map.reshape(-1),
            migrate_weight.reshape(-1),
        ]
    ).astype(jnp.float32)
    row = jnp.pad(row, (0, 2 * nx - row.shape[0]))[None]

    bw = pl.pallas_call(
        functools.partial(axial_kernel, dims, n_ax),
        out_shape=f32((2 * F, nr, na, nx)),
        in_specs=[vmem] * 4,
        out_specs=vmem,
        scratch_shapes=[
            pltpu.VMEM((3, 2 * F, halves, 8, nx), jnp.float32),
            pltpu.VMEM((2 * F * nr * na, 6 * nx), jnp.bfloat16),
            pltpu.VMEM((6 * nx, 3 * nx), jnp.bfloat16),
            pltpu.VMEM((F * nr * na, 2 * nx), jnp.float32),
        ],
        compiler_params=pltpu.CompilerParams(vmem_limit_bytes=40 << 20),
        name="axial",
    )(primal, adjoint, ax_a, ax_b)

    indicator, send = pl.pallas_call(
        functools.partial(main_kernel, dims),
        out_shape=(f32(dims), f32((n_dev, 2 * nx))),
        in_specs=[vmem] * 8,
        out_specs=(vmem, vmem),
        scratch_shapes=[
            pltpu.VMEM((2 * F, 4, na, nx), jnp.float32),
            pltpu.VMEM((2 * F, nr, 24, nx), jnp.float32),
            pltpu.VMEM((2 * F, nr, 16, nx), jnp.float32),
            pltpu.VMEM((F, tiles, 8, nx), jnp.float32),
            pltpu.VMEM((F, 8 + na, nx), jnp.float32),
        ],
        compiler_params=pltpu.CompilerParams(vmem_limit_bytes=32 << 20),
        name="stencil",
    )(primal, adjoint, bw, rad_a, rad_b, azi_l, azi_r, row)

    data = lax.all_to_all(send, AXES, 0, 0, tiled=True)

    cost, load = pl.pallas_call(
        functools.partial(final_kernel, n_loc, per_ax),
        out_shape=(f32((per_rad, per_azi, per_ax)), f32((1, 1, 1))),
        in_specs=[vmem],
        out_specs=(vmem, vmem),
        name="blocks",
    )(data)
    return indicator, cost, load


def solution(mesh):
    spec = P("rad", "azi", "ax")
    field = P(None, "rad", "azi", "ax")
    return jax.shard_map(
        on_device,
        mesh=mesh,
        in_specs=(field, field, spec, spec, spec, P("rad", "azi", "ax", None)),
        out_specs=(spec, spec, spec),
        check_vma=False,
    )
```

```python
import functools

import jax
import jax.numpy as jnp
from jax import lax
from jax.experimental import pallas as pl
from jax.experimental.pallas import tpu as pltpu
from jax.sharding import PartitionSpec as P

BLK = 16
F = 5
AXES = ("rad", "azi", "ax")


def pair_round(sizes, along, first):
    n = sizes[along]
    step = [sizes[1] * sizes[2], sizes[2], 1]
    used = range(first, n - 1, 2)
    partner = {i: i + 1 for i in used} | {i + 1: i for i in used}
    idle = [i for i in range(n) if i not in partner]
    if along == 2 and len(idle) == 2:
        partner |= {idle[0]: idle[1], idle[1]: idle[0]}
    pairs = []
    for me in range(sizes[0] * step[0]):
        i = me // step[along] % n
        if i in partner:
            pairs.append((me, me + (partner[i] - i) * step[along]))
        elif along != 2 and sizes[2] % 2 == 0:
            pairs.append((me, me ^ 1))
    return pairs


def ring(count, step):
    return [(i, (i + step) % count) for i in range(count)]


def edge_kernel(dims, prim, adj, rad_a, rad_b, azi_s, sems):
    nr, na, nx = dims
    odd = lax.rem(lax.axis_index("rad"), 2)
    first = jnp.where(odd == 0, nr - 2, 0)
    copies = []
    for t, src in enumerate((prim, adj)):
        rows = pl.ds(t * F, F)
        for i, (a, b) in enumerate(
            (
                (src.at[:, pl.ds(first, 2)], rad_a.at[rows]),
                (src.at[:, pl.ds(nr - 2 - first, 2)], rad_b.at[rows]),
                (src.at[:, :, pl.ds(0, 2)], azi_s.at[rows, :, pl.ds(0, 2)]),
                (src.at[:, :, pl.ds(na - 2, 2)], azi_s.at[rows, :, pl.ds(2, 2)]),
            )
        ):
            copies.append(pltpu.make_async_copy(a, b, sems.at[t, i]))
    for c in copies:
        c.start()
    for c in copies:
        c.wait()


def lane_kernel(dims, prim, adj, ax_s):
    nr, na, nx = dims
    slot = lax.broadcasted_iota(jnp.int32, (8, nx), 1) >> 2
    tiles = na // 8
    per = nx // 4
    for t, src in enumerate((prim, adj)):
        for f in range(F):
            for h in range(nr * tiles // per):
                acc = jnp.zeros((8, nx), jnp.float32)
                for j in range(per):
                    k = h * per + j
                    x = src[f, k // tiles, pl.ds(8 * (k % tiles), 8), :]
                    acc = jnp.where(slot == j, pltpu.roll(x, (4 * j + 2) % nx, 1), acc)
                ax_s[t * F + f, h] = acc


def flux(s, along):
    inv = 1.0 / s[0]
    v = s[1 + along] * inv
    kin = (s[1] * s[1] + s[2] * s[2] + s[3] * s[3]) * inv
    p = 0.4 * s[4] - 0.2 * kin
    out = [s[1 + along], s[1] * v, s[2] * v, s[3] * v, (s[4] + p) * v]
    out[1 + along] = out[1 + along] + p
    return out


def face(m1, c, p1, p2):
    return 7.0 * (c + p1) - (m1 + p2)


def split3(x):
    hi = x.astype(jnp.bfloat16)
    x = x - hi.astype(jnp.float32)
    mid = x.astype(jnp.bfloat16)
    x = x - mid.astype(jnp.float32)
    return hi, mid, x.astype(jnp.bfloat16)


def taps(rows, cols, table):
    out = jnp.zeros(rows.shape, jnp.float32)
    for step, value in table.items():
        out = jnp.where(rows - cols == step, value, out)
    return out


UPPER = {-1: -1.0, 0: 7.0, 1: 7.0, 2: -1.0}
LOWER = {-2: -1.0, -1: 7.0, 0: 7.0, 1: -1.0}
FOURTH = {-2: 1.0, -1: -4.0, 0: 6.0, 1: -4.0, 2: 1.0}


def axial_kernel(dims, n_ax, prim, adj, ax_a, ax_b, bw, got, lhs, rhs, sums):
    nr, na, nx = dims
    i_ax = lax.axis_index("ax")
    even_ax = lax.rem(i_ax, 2) == 0
    lane = lax.broadcasted_iota(jnp.int32, (8, nx), 1)
    part = lane & 3
    slot = lane >> 2
    tiles = na // 8
    per = nx // 4
    halves = nr * tiles // per
    size = nr * na

    i = lax.broadcasted_iota(jnp.int32, (nx, nx), 0)
    c = lax.broadcasted_iota(jnp.int32, (nx, nx), 1)
    p = i & 3
    halo = jnp.where(p < 2, p - 2, p - 2 + nx)
    for n, table in enumerate((UPPER, LOWER, FOURTH)):
        own = taps(i, c, table).astype(jnp.bfloat16)
        far = taps(halo, c, table).astype(jnp.bfloat16)
        for k in range(3):
            rhs[pl.ds(2 * k * nx, nx), pl.ds(n * nx, nx)] = own
            rhs[pl.ds((2 * k + 1) * nx, nx), pl.ds(n * nx, nx)] = far

    for h in range(halves):
        for f in range(2 * F):
            a, b = ax_a[f, h], ax_b[f, h]
            left = jnp.where(i_ax == 0, 0.0, jnp.where(even_ax, b, a))
            right = jnp.where(i_ax == n_ax - 1, 0.0, jnp.where(even_ax, a, b))
            g = jnp.where(part < 2, left, right)
            for k, x in enumerate(split3(g)):
                got[k, f, h] = x.astype(jnp.float32)

    def build(t, src, f):
        g0 = t * F + f
        for r in range(nr):
            h, j0 = r * tiles // per, r * tiles % per
            rows = pl.ds(pl.multiple_of(g0 * size, size) + r * na, na)
            for k, x in enumerate(split3(src[f, r])):
                lhs[rows, pl.ds(2 * k * nx, nx)] = x
                g = got[k, g0, h]
                y = [jnp.where(slot == j0 + a, g, 0.0) for a in range(tiles)]
                lhs[rows, pl.ds((2 * k + 1) * nx, nx)] = jnp.concatenate(y, axis=0).astype(jnp.bfloat16)

    for t, src in enumerate((prim, adj)):
        lax.fori_loop(0, F, lambda f, c, t=t, src=src: (build(t, src, f), c)[1], 0)
    sums[...] = jnp.dot(
        lhs[0:F * size, :], rhs[:, 0:2 * nx], preferred_element_type=jnp.float32
    )
    bw[F:2 * F] = jnp.dot(
        lhs[F * size:2 * F * size, :], rhs[:, 2 * nx:3 * nx], preferred_element_type=jnp.float32
    ).reshape(F, nr, na, nx)

    def body(r, carry):
        for a in range(tiles):
            at = [pl.ds(f * size + pl.multiple_of(r * na, na) + 8 * a, 8) for f in range(F)]
            up = flux([sums[q, 0:nx] for q in at], 2)
            low = flux([sums[q, nx:2 * nx] for q in at], 2)
            for f in range(F):
                bw[f, r, pl.ds(8 * a, 8), :] = up[f] - low[f]
        return carry

    lax.fori_loop(0, nr, body, 0)


def main_kernel(
    dims, n_rad, prim, adj, bw, rad_a, rad_b, azi_l, azi_r, row, ind, send, far, low, top, frad, fazi
):
    nr, na, nx = dims
    i_rad = lax.axis_index("rad")
    odd = lax.rem(i_rad, 2)
    tiles = na // 8
    last = 8 * (tiles - 1)
    lane = lax.broadcasted_iota(jnp.int32, (8, nx), 1)
    for f in range(2 * F):
        for i in range(2):
            a, b = rad_a[f, i], rad_b[f, i]
            far[f, i] = jnp.where(i_rad == 0, 0.0, jnp.where(odd == 0, b, a))
            far[f, 2 + i] = jnp.where(i_rad == n_rad - 1, 0.0, jnp.where(odd == 0, a, b))

    def edges(r, carry):
        for t, src in enumerate((prim, adj)):
            for f in range(F):
                g = t * F + f
                low[g, r, 14:16, :] = azi_l[g, r, 2:4, :]
                low[g, r, 16:24, :] = src[f, r, 0:8, :]
                top[g, r, 0:8, :] = src[f, r, last:last + 8, :]
                top[g, r, 8:10, :] = azi_r[g, r, 0:2, :]
        return carry

    lax.fori_loop(0, nr, edges, 0)

    def cell(g, r, a, dr=0, da=0):
        if isinstance(r, int):
            if r + dr < 0:
                return far[g, 2 + r + dr, pl.ds(8 * a, 8), :]
            if r + dr >= nr:
                return far[g, 2 + r + dr - nr, pl.ds(8 * a, 8), :]
        if da < 0 and a == 0:
            return low[g, r, pl.ds(16 + da, 8), :]
        if da > 0 and a == tiles - 1:
            return top[g, r, pl.ds(da, 8), :]
        src = (prim, adj)[g // F]
        return src[g % F, r + dr, pl.ds(8 * a + da, 8), :]

    def rad_flux(r, a):
        return flux([face(*(cell(f, r, a, dr=o) for o in (-1, 0, 1, 2))) for f in range(F)], 0)

    def azi_flux(r, a):
        return flux([face(*(cell(f, r, a, da=o) for o in (-1, 0, 1, 2))) for f in range(F)], 1)

    def low_flux(r):
        return flux([face(*(low[f, r, pl.ds(8 + o, 8), :] for o in (-1, 0, 1, 2))) for f in range(F)], 1)

    for a in range(tiles):
        for f, x in enumerate(rad_flux(-1, a)):
            frad[f, a] = x

    def plane(r, sums):
        for f, x in enumerate(low_flux(r)):
            fazi[f, 0:8, :] = x
        for a in range(tiles):
            for f, x in enumerate(azi_flux(r, a)):
                fazi[f, pl.ds(8 + 8 * a, 8), :] = x
        out = []
        for a in range(tiles):
            mine = pl.ds(8 * a, 8)
            up = rad_flux(r, a)
            total = None
            for f in range(F):
                bal = bw[f, r, mine, :] + (up[f] - frad[f, a])
                frad[f, a] = up[f]
                bal = bal + (fazi[f, pl.ds(8 * a + 8, 8), :] - fazi[f, pl.ds(8 * a + 7, 8), :])
                g = F + f
                two = (cell(g, r, a, dr=-2) + cell(g, r, a, dr=2)) + (
                    cell(g, r, a, da=-2) + cell(g, r, a, da=2)
                )
                one = (cell(g, r, a, dr=-1) + cell(g, r, a, dr=1)) + (
                    cell(g, r, a, da=-1) + cell(g, r, a, da=1)
                )
                w = (two - 4.0 * one + 12.0 * cell(g, r, a) + bw[g, r, mine, :]) * bal
                total = w if total is None else total + w
            total = jnp.abs(total) * (1.0 / 144.0)
            ind[r, mine, :] = total
            out.append(sums[a] + total)
        return tuple(out)

    sums = tuple(jnp.zeros((8, nx), jnp.float32) for _ in range(tiles))
    for r in (0, 1):
        sums = plane(r, sums)
    sums = lax.fori_loop(2, nr - 2, plane, sums)
    for r in (nr - 2, nr - 1):
        sums = plane(r, sums)

    groups = nx // BLK
    halves_a = na // BLK
    per_tile = BLK // 8
    means = jnp.zeros((8, nx), jnp.float32)
    for b in range(halves_a):
        t = sums[b * per_tile]
        for i in range(1, per_tile):
            t = t + sums[b * per_tile + i]
        t = jnp.broadcast_to(jnp.sum(t, axis=0, keepdims=True), (8, nx))
        for sh in (8, 4, 2, 1):
            t = t + pltpu.roll(t, nx - sh, 1)
        t = jnp.take_along_axis(t, (lane % groups) * BLK, axis=1)
        means = jnp.where(lane // groups == b, t, means)
    means = means * (1.0 / BLK**3)
    head = jnp.broadcast_to(row[:, 0:nx], (8, nx))
    head = jnp.where(lane < groups * halves_a, means, head)
    tail = jnp.broadcast_to(row[:, nx:2 * nx], (8, nx))
    both = jnp.where(lax.broadcasted_iota(jnp.int32, (8, nx), 0) & 1 == 0, head, tail)
    for d in range(send.shape[0] // 8):
        send[pl.ds(8 * d, 8), :] = both


def final_kernel(n_loc, per_ax, data, cost, load, means):
    n_dev, nx = data.shape[0] // 2, data.shape[1]
    me = (lax.axis_index("rad") * lax.axis_size("azi") + lax.axis_index("azi")) * lax.axis_size(
        "ax"
    ) + lax.axis_index("ax")
    lane = lax.broadcasted_iota(jnp.int32, (8, nx), 1)
    sub = lax.broadcasted_iota(jnp.int32, (8, nx), 0)
    small = n_dev <= 32
    groups = n_dev // 8
    ok = lane < n_loc

    def rows(g, part):
        return data[pl.ds(16 * g + part, 8, stride=2), :]

    def table(g, carry):
        x = jnp.where(ok, rows(g, 0), 0.0)
        x = pltpu.roll(x, 0, 1, stride=n_loc, stride_axis=0)
        means[g] = jnp.broadcast_to(jnp.sum(x, axis=0, keepdims=True), (8, nx))
        return carry

    lax.fori_loop(0, groups, table, 0, unroll=small)

    def group(g, carry):
        acc_load, acc_cost = carry
        head = rows(g, 0)
        tail = rows(g, 1)
        spot = head.astype(jnp.int32)
        pos = spot & (nx - 1)
        line = spot >> (nx.bit_length() - 1)

        def look(q, acc):
            return jnp.where(line == q, jnp.take_along_axis(means[q], pos, axis=1), acc)

        val = lax.fori_loop(0, groups, look, jnp.zeros((8, nx), jnp.float32), unroll=small)
        beside = None
        for j in range(6):
            x = pltpu.roll(val, nx - n_loc * (1 + j), 1)
            beside = x if beside is None else beside + x
        smooth = 0.5 * head + (0.5 / 6.0) * beside
        refine = pltpu.roll(head, nx - 7 * n_loc, 1)
        owner = tail.astype(jnp.int32)
        weight = pltpu.roll(tail, nx - n_loc, 1)
        home = sub + 8 * g
        c = smooth * (1.0 + 7.0 * refine) + jnp.where(owner != home, 0.25 * weight, 0.0)
        acc_load = acc_load + jnp.where(ok & (owner == me), c, 0.0)
        acc_cost = acc_cost + jnp.where(home == me, c, 0.0)
        return acc_load, acc_cost

    zero = jnp.zeros((8, nx), jnp.float32)
    acc_load, acc_cost = lax.fori_loop(0, groups, group, (zero, zero), unroll=small)
    own = jnp.sum(acc_cost, axis=0, keepdims=True)
    for b in range(n_loc // per_ax):
        x = own if b == 0 else pltpu.roll(own, nx - b * per_ax, 1)
        cost[0, pl.ds(b, 1), :] = x[:, 0:per_ax]
    total = jnp.sum(jnp.sum(acc_load, axis=0, keepdims=True), axis=1, keepdims=True) * (1.0 / n_loc)
    load[0] = total


def on_device(primal, adjoint, refine_flag, owner_map, migrate_weight, neighbor_list):
    _, nr, na, nx = primal.shape
    dims = (nr, na, nx)
    sizes = n_rad, n_azi, n_ax = tuple(lax.axis_size(a) for a in AXES)
    n_dev = n_rad * n_azi * n_ax
    tiles = na // 8
    halves = nr * tiles // (nx // 4)
    f32 = functools.partial(jax.ShapeDtypeStruct, dtype=jnp.float32)
    anyspec = pl.BlockSpec(memory_space=pl.ANY)
    hbm = pl.BlockSpec(memory_space=pltpu.HBM)
    vmem = pl.BlockSpec(memory_space=pltpu.VMEM)

    rad_a, rad_b, azi_s = pl.pallas_call(
        functools.partial(edge_kernel, dims),
        out_shape=(f32((2 * F, 2, na, nx)), f32((2 * F, 2, na, nx)), f32((2 * F, nr, 4, nx))),
        in_specs=[hbm, hbm],
        out_specs=(vmem, vmem, vmem),
        scratch_shapes=[pltpu.SemaphoreType.DMA((2, 4))],
        name="edges",
    )(primal, adjoint)
    ax_s = pl.pallas_call(
        functools.partial(lane_kernel, dims),
        out_shape=f32((2 * F, halves, 8, nx)),
        in_specs=[vmem, vmem],
        out_specs=vmem,
        compiler_params=pltpu.CompilerParams(vmem_limit_bytes=16 << 20),
        name="lanes",
    )(primal, adjoint)

    ax_a = lax.ppermute(ax_s, AXES, pair_round(sizes, 2, 0))
    ax_b = lax.ppermute(ax_s, AXES, pair_round(sizes, 2, 1))
    azi_l = lax.ppermute(azi_s, "azi", ring(n_azi, 1))
    azi_r = azi_l if n_azi == 2 else lax.ppermute(azi_s, "azi", ring(n_azi, -1))
    rad_a = lax.ppermute(rad_a, AXES, pair_round(sizes, 0, 0))
    rad_b = lax.ppermute(rad_b, AXES, pair_round(sizes, 0, 1))

    per_rad, per_azi, per_ax = nr // BLK, na // BLK, nx // BLK
    n_loc = per_rad * per_azi * per_ax
    blocks_azi, blocks_ax = per_azi * n_azi, per_ax * n_ax
    b_rad = neighbor_list // (blocks_azi * blocks_ax)
    b_azi = neighbor_list // blocks_ax % blocks_azi
    b_ax = neighbor_list % blocks_ax
    device = (b_rad // per_rad * n_azi + b_azi // per_azi) * n_ax + b_ax // per_ax
    local = (b_rad % per_rad * per_azi + b_azi % per_azi) * per_ax + b_ax % per_ax
    spot = (device * n_loc + local).reshape(n_loc, 6).T.reshape(-1)
    row = jnp.concatenate(
        [
            jnp.zeros((n_loc,), jnp.int32),
            spot,
            refine_flag.reshape(-1),
            owner_map.reshape(-1),
            migrate_weight.reshape(-1),
        ]
    ).astype(jnp.float32)
    row = jnp.pad(row, (0, 2 * nx - row.shape[0]))[None]

    bw = pl.pallas_call(
        functools.partial(axial_kernel, dims, n_ax),
        out_shape=f32((2 * F, nr, na, nx)),
        in_specs=[vmem] * 4,
        out_specs=vmem,
        scratch_shapes=[
            pltpu.VMEM((3, 2 * F, halves, 8, nx), jnp.float32),
            pltpu.VMEM((2 * F * nr * na, 6 * nx), jnp.bfloat16),
            pltpu.VMEM((6 * nx, 3 * nx), jnp.bfloat16),
            pltpu.VMEM((F * nr * na, 2 * nx), jnp.float32),
        ],
        compiler_params=pltpu.CompilerParams(vmem_limit_bytes=40 << 20),
        name="axial",
    )(primal, adjoint, ax_a, ax_b)

    indicator, send = pl.pallas_call(
        functools.partial(main_kernel, dims, n_rad),
        out_shape=(f32(dims), f32((2 * n_dev, nx))),
        in_specs=[vmem] * 8,
        out_specs=(vmem, vmem),
        scratch_shapes=[
            pltpu.VMEM((2 * F, 4, na, nx), jnp.float32),
            pltpu.VMEM((2 * F, nr, 24, nx), jnp.float32),
            pltpu.VMEM((2 * F, nr, 16, nx), jnp.float32),
            pltpu.VMEM((F, tiles, 8, nx), jnp.float32),
            pltpu.VMEM((F, 8 + na, nx), jnp.float32),
        ],
        compiler_params=pltpu.CompilerParams(vmem_limit_bytes=32 << 20),
        name="stencil",
    )(primal, adjoint, bw, rad_a, rad_b, azi_l, azi_r, row)

    data = lax.all_to_all(send, AXES, 0, 0, tiled=True)

    cost, load = pl.pallas_call(
        functools.partial(final_kernel, n_loc, per_ax),
        out_shape=(f32((per_rad, per_azi, per_ax)), f32((1, 1, 1))),
        in_specs=[vmem],
        out_specs=(vmem, vmem),
        scratch_shapes=[pltpu.VMEM((n_dev // 8, 8, nx), jnp.float32)],
        name="blocks",
    )(data)
    return indicator, cost, load


def solution(mesh):
    spec = P("rad", "azi", "ax")
    field = P(None, "rad", "azi", "ax")
    return jax.shard_map(
        on_device,
        mesh=mesh,
        in_specs=(field, field, spec, spec, spec, P("rad", "azi", "ax", None)),
        out_specs=(spec, spec, spec),
        check_vma=False,
    )
```

```python
import functools

import jax
import jax.numpy as jnp
from jax import lax
from jax.experimental import pallas as pl
from jax.experimental.pallas import tpu as pltpu
from jax.sharding import PartitionSpec as P

BLK = 16
F = 5
AXES = ("rad", "azi", "ax")


def pair_round(sizes, along, first):
    n = sizes[along]
    step = [sizes[1] * sizes[2], sizes[2], 1]
    used = range(first, n - 1, 2)
    partner = {i: i + 1 for i in used} | {i + 1: i for i in used}
    idle = [i for i in range(n) if i not in partner]
    if along == 2 and len(idle) == 2:
        partner |= {idle[0]: idle[1], idle[1]: idle[0]}
    pairs = []
    for me in range(sizes[0] * step[0]):
        i = me // step[along] % n
        if i in partner:
            pairs.append((me, me + (partner[i] - i) * step[along]))
        elif along != 2 and sizes[2] % 2 == 0:
            pairs.append((me, me ^ 1))
    return pairs


def ring(count, step):
    return [(i, (i + step) % count) for i in range(count)]


def edge_kernel(dims, prim, adj, rad_a, rad_b, azi_s, sems):
    nr, na, nx = dims
    odd = lax.rem(lax.axis_index("rad"), 2)
    first = jnp.where(odd == 0, nr - 2, 0)
    copies = []
    for t, src in enumerate((prim, adj)):
        rows = pl.ds(t * F, F)
        for i, (a, b) in enumerate(
            (
                (src.at[:, pl.ds(first, 2)], rad_a.at[rows]),
                (src.at[:, pl.ds(nr - 2 - first, 2)], rad_b.at[rows]),
                (src.at[:, :, pl.ds(0, 2)], azi_s.at[rows, :, pl.ds(0, 2)]),
                (src.at[:, :, pl.ds(na - 2, 2)], azi_s.at[rows, :, pl.ds(2, 2)]),
            )
        ):
            copies.append(pltpu.make_async_copy(a, b, sems.at[t, i]))
    for c in copies:
        c.start()
    for c in copies:
        c.wait()


def lane_kernel(dims, prim, adj, ax_s):
    nr, na, nx = dims
    slot = lax.broadcasted_iota(jnp.int32, (8, nx), 1) >> 2
    tiles = na // 8
    per = nx // 4
    for t, src in enumerate((prim, adj)):
        for f in range(F):
            for h in range(nr * tiles // per):
                acc = jnp.zeros((8, nx), jnp.float32)
                for j in range(per):
                    k = h * per + j
                    x = src[f, k // tiles, pl.ds(8 * (k % tiles), 8), :]
                    acc = jnp.where(slot == j, pltpu.roll(x, (4 * j + 2) % nx, 1), acc)
                ax_s[t * F + f, h] = acc


def flux(s, along):
    inv = 1.0 / s[0]
    v = s[1 + along] * inv
    kin = (s[1] * s[1] + s[2] * s[2] + s[3] * s[3]) * inv
    p = 0.4 * s[4] - 0.2 * kin
    out = [s[1 + along], s[1] * v, s[2] * v, s[3] * v, (s[4] + p) * v]
    out[1 + along] = out[1 + along] + p
    return out


def face(m1, c, p1, p2):
    return 7.0 * (c + p1) - (m1 + p2)


def split3(x):
    hi = x.astype(jnp.bfloat16)
    x = x - hi.astype(jnp.float32)
    mid = x.astype(jnp.bfloat16)
    x = x - mid.astype(jnp.float32)
    return hi, mid, x.astype(jnp.bfloat16)


def taps(rows, cols, table):
    out = jnp.zeros(rows.shape, jnp.float32)
    for step, value in table.items():
        out = jnp.where(rows - cols == step, value, out)
    return out


UPPER = {-1: -1.0, 0: 7.0, 1: 7.0, 2: -1.0}
LOWER = {-2: -1.0, -1: 7.0, 0: 7.0, 1: -1.0}
FOURTH = {-2: 1.0, -1: -4.0, 0: 6.0, 1: -4.0, 2: 1.0}


def block_row(grid, near, refine, owner, weight, nx):
    (per_rad, per_azi, per_ax), (n_azi, n_ax) = grid
    n_loc = per_rad * per_azi * per_ax
    blocks_azi, blocks_ax = per_azi * n_azi, per_ax * n_ax
    lane = lax.broadcasted_iota(jnp.int32, (per_azi, nx), 1)

    def place(number):
        b_rad = lax.div(number, blocks_azi * blocks_ax)
        b_azi = lax.rem(lax.div(number, blocks_ax), blocks_azi)
        b_ax = lax.rem(number, blocks_ax)
        device = (lax.div(b_rad, per_rad) * n_azi + lax.div(b_azi, per_azi)) * n_ax + lax.div(b_ax, per_ax)
        local = (lax.rem(b_rad, per_rad) * per_azi + lax.rem(b_azi, per_azi)) * per_ax + lax.rem(b_ax, per_ax)
        return device * n_loc + local

    def spread(x, at):
        x = jnp.concatenate([x, jnp.zeros((per_azi, nx - per_ax), jnp.int32)], axis=1)
        x = jnp.where(lane < per_ax, x, 0).astype(jnp.float32)
        rows = [x[b:b + 1] if at + b * per_ax == 0 else pltpu.roll(x[b:b + 1], at + b * per_ax, 1) for b in range(per_azi)]
        return sum(rows[1:], rows[0])

    head = spread(refine[0], 7 * n_loc)
    for j in range(6):
        head = head + spread(place(near[0, j]), (1 + j) * n_loc)
    tail = spread(owner[0], 0) + spread(weight[0], n_loc)
    return head, tail


def own_kernel(
    dims, grid, prim, adj, ax_s, near, refine, owner, weight, sums, fourth, row, lhs, rhs
):
    del ax_s
    nr, na, nx = dims
    head, tail = block_row(grid, near, refine, owner, weight, nx)
    row[:, 0:nx] = head
    row[:, nx:2 * nx] = tail
    size = nr * na
    i = lax.broadcasted_iota(jnp.int32, (nx, nx), 0)
    c = lax.broadcasted_iota(jnp.int32, (nx, nx), 1)
    for n, table in enumerate((UPPER, LOWER, FOURTH)):
        own = taps(i, c, table).astype(jnp.bfloat16)
        for k in range(3):
            rhs[pl.ds(k * nx, nx), pl.ds(n * nx, nx)] = own

    def build(t, src, f):
        for r in range(nr):
            rows = pl.ds(pl.multiple_of((t * F + f) * size, size) + r * na, na)
            for k, x in enumerate(split3(src[f, r])):
                lhs[rows, pl.ds(k * nx, nx)] = x

    for t, src in enumerate((prim, adj)):
        lax.fori_loop(0, F, lambda f, c, t=t, src=src: (build(t, src, f), c)[1], 0)
    sums[...] = jnp.dot(
        lhs[0:F * size, :], rhs[:, 0:2 * nx], preferred_element_type=jnp.float32
    )
    fourth[...] = jnp.dot(
        lhs[F * size:2 * F * size, :], rhs[:, 2 * nx:3 * nx], preferred_element_type=jnp.float32
    )


def axial_kernel(dims, n_ax, sums, fourth, ax_a, ax_b, bw, got, lhs, rhs, far):
    nr, na, nx = dims
    i_ax = lax.axis_index("ax")
    even_ax = lax.rem(i_ax, 2) == 0
    lane = lax.broadcasted_iota(jnp.int32, (8, nx), 1)
    part = lane & 3
    slot = lane >> 2
    tiles = na // 8
    per = nx // 4
    halves = nr * tiles // per
    size = nr * na
    third = per // 3

    i = lax.broadcasted_iota(jnp.int32, (nx, nx), 0) & 3
    c = lax.broadcasted_iota(jnp.int32, (nx, nx), 1)
    cells = jnp.where(i < 2, i - 2, i - 2 + nx)
    for n, table in enumerate((UPPER, LOWER, FOURTH)):
        rhs[:, pl.ds(n * nx, nx)] = taps(cells, c, table).astype(jnp.bfloat16)

    for h in range(halves):
        for f in range(2 * F):
            a, b = ax_a[f, h], ax_b[f, h]
            left = jnp.where(i_ax == 0, 0.0, jnp.where(even_ax, b, a))
            right = jnp.where(i_ax == n_ax - 1, 0.0, jnp.where(even_ax, a, b))
            for k, x in enumerate(split3(jnp.where(part < 2, left, right))):
                x = x.astype(jnp.float32)
                got[k, f, h] = pltpu.roll(x, 4 * third * k, 1) if k else x

    def build(g, carry):
        for r in range(nr):
            h, j0 = r * tiles // per, r * tiles % per
            rows = pl.ds(pl.multiple_of(g * size, size) + r * na, na)
            y = []
            for a in range(tiles):
                x = jnp.zeros((8, nx), jnp.float32)
                for k in range(3):
                    x = jnp.where(slot == (j0 + a + third * k) % per, got[k, g, h], x)
                y.append(x)
            lhs[rows, :] = jnp.concatenate(y, axis=0).astype(jnp.bfloat16)
        return carry

    lax.fori_loop(0, 2 * F, build, 0)
    far[...] = jnp.dot(lhs[0:F * size, :], rhs[:, 0:2 * nx], preferred_element_type=jnp.float32)
    bw[F:2 * F] = (
        fourth[...]
        + jnp.dot(
            lhs[F * size:2 * F * size, :], rhs[:, 2 * nx:3 * nx], preferred_element_type=jnp.float32
        )
    ).reshape(F, nr, na, nx)

    def body(r, carry):
        for a in range(tiles):
            at = [pl.ds(f * size + pl.multiple_of(r * na, na) + 8 * a, 8) for f in range(F)]
            up = flux([sums[q, 0:nx] + far[q, 0:nx] for q in at], 2)
            low = flux([sums[q, nx:2 * nx] + far[q, nx:2 * nx] for q in at], 2)
            for f in range(F):
                bw[f, r, pl.ds(8 * a, 8), :] = up[f] - low[f]
        return carry

    lax.fori_loop(0, nr, body, 0)


def main_kernel(
    dims, n_rad, prim, adj, bw, rad_a, rad_b, azi_l, azi_r, row, ind, send, far, low, top, frad, fazi
):
    nr, na, nx = dims
    i_rad = lax.axis_index("rad")
    odd = lax.rem(i_rad, 2)
    tiles = na // 8
    last = 8 * (tiles - 1)
    lane = lax.broadcasted_iota(jnp.int32, (8, nx), 1)
    for f in range(2 * F):
        for i in range(2):
            a, b = rad_a[f, i], rad_b[f, i]
            far[f, i] = jnp.where(i_rad == 0, 0.0, jnp.where(odd == 0, b, a))
            far[f, 2 + i] = jnp.where(i_rad == n_rad - 1, 0.0, jnp.where(odd == 0, a, b))

    def edges(r, carry):
        for t, src in enumerate((prim, adj)):
            for f in range(F):
                g = t * F + f
                low[g, r, 14:16, :] = azi_l[g, r, 2:4, :]
                low[g, r, 16:24, :] = src[f, r, 0:8, :]
                top[g, r, 0:8, :] = src[f, r, last:last + 8, :]
                top[g, r, 8:10, :] = azi_r[g, r, 0:2, :]
        return carry

    lax.fori_loop(0, nr, edges, 0)

    def cell(g, r, a, dr=0, da=0):
        if isinstance(r, int):
            if r + dr < 0:
                return far[g, 2 + r + dr, pl.ds(8 * a, 8), :]
            if r + dr >= nr:
                return far[g, 2 + r + dr - nr, pl.ds(8 * a, 8), :]
        if da < 0 and a == 0:
            return low[g, r, pl.ds(16 + da, 8), :]
        if da > 0 and a == tiles - 1:
            return top[g, r, pl.ds(da, 8), :]
        src = (prim, adj)[g // F]
        return src[g % F, r + dr, pl.ds(8 * a + da, 8), :]

    def rad_flux(r, a):
        return flux([face(*(cell(f, r, a, dr=o) for o in (-1, 0, 1, 2))) for f in range(F)], 0)

    def azi_flux(r, a):
        return flux([face(*(cell(f, r, a, da=o) for o in (-1, 0, 1, 2))) for f in range(F)], 1)

    def low_flux(r):
        return flux([face(*(low[f, r, pl.ds(8 + o, 8), :] for o in (-1, 0, 1, 2))) for f in range(F)], 1)

    for a in range(tiles):
        for f, x in enumerate(rad_flux(-1, a)):
            frad[f, a] = x

    def plane(r, sums):
        for f, x in enumerate(low_flux(r)):
            fazi[f, 0:8, :] = x
        for a in range(tiles):
            for f, x in enumerate(azi_flux(r, a)):
                fazi[f, pl.ds(8 + 8 * a, 8), :] = x
        out = []
        for a in range(tiles):
            mine = pl.ds(8 * a, 8)
            up = rad_flux(r, a)
            total = None
            for f in range(F):
                bal = bw[f, r, mine, :] + (up[f] - frad[f, a])
                frad[f, a] = up[f]
                bal = bal + (fazi[f, pl.ds(8 * a + 8, 8), :] - fazi[f, pl.ds(8 * a + 7, 8), :])
                g = F + f
                two = (cell(g, r, a, dr=-2) + cell(g, r, a, dr=2)) + (
                    cell(g, r, a, da=-2) + cell(g, r, a, da=2)
                )
                one = (cell(g, r, a, dr=-1) + cell(g, r, a, dr=1)) + (
                    cell(g, r, a, da=-1) + cell(g, r, a, da=1)
                )
                w = (two - 4.0 * one + 12.0 * cell(g, r, a) + bw[g, r, mine, :]) * bal
                total = w if total is None else total + w
            total = jnp.abs(total) * (1.0 / 144.0)
            ind[r, mine, :] = total
            out.append(sums[a] + total)
        return tuple(out)

    sums = tuple(jnp.zeros((8, nx), jnp.float32) for _ in range(tiles))
    for r in (0, 1):
        sums = plane(r, sums)
    sums = lax.fori_loop(2, nr - 2, plane, sums)
    for r in (nr - 2, nr - 1):
        sums = plane(r, sums)

    groups = nx // BLK
    halves_a = na // BLK
    per_tile = BLK // 8
    means = jnp.zeros((8, nx), jnp.float32)
    for b in range(halves_a):
        t = sums[b * per_tile]
        for i in range(1, per_tile):
            t = t + sums[b * per_tile + i]
        t = jnp.broadcast_to(jnp.sum(t, axis=0, keepdims=True), (8, nx))
        for sh in (8, 4, 2, 1):
            t = t + pltpu.roll(t, nx - sh, 1)
        t = jnp.take_along_axis(t, (lane % groups) * BLK, axis=1)
        means = jnp.where(lane // groups == b, t, means)
    means = means * (1.0 / BLK**3)
    head = jnp.broadcast_to(row[:, 0:nx], (8, nx))
    head = jnp.where(lane < groups * halves_a, means, head)
    tail = jnp.broadcast_to(row[:, nx:2 * nx], (8, nx))
    both = jnp.where(lax.broadcasted_iota(jnp.int32, (8, nx), 0) & 1 == 0, head, tail)
    for d in range(send.shape[0] // 8):
        send[pl.ds(8 * d, 8), :] = both


def final_kernel(n_loc, per_ax, data, cost, load, means):
    n_dev, nx = data.shape[0] // 2, data.shape[1]
    me = (lax.axis_index("rad") * lax.axis_size("azi") + lax.axis_index("azi")) * lax.axis_size(
        "ax"
    ) + lax.axis_index("ax")
    lane = lax.broadcasted_iota(jnp.int32, (8, nx), 1)
    sub = lax.broadcasted_iota(jnp.int32, (8, nx), 0)
    small = n_dev <= 32
    groups = n_dev // 8
    ok = lane < n_loc

    def rows(g, part):
        return data[pl.ds(16 * g + part, 8, stride=2), :]

    def table(g, carry):
        x = jnp.where(ok, rows(g, 0), 0.0)
        x = pltpu.roll(x, 0, 1, stride=n_loc, stride_axis=0)
        means[g] = jnp.broadcast_to(jnp.sum(x, axis=0, keepdims=True), (8, nx))
        return carry

    lax.fori_loop(0, groups, table, 0, unroll=small)

    def group(g, carry):
        acc_load, acc_cost = carry
        head = rows(g, 0)
        tail = rows(g, 1)
        spot = head.astype(jnp.int32)
        pos = spot & (nx - 1)
        line = spot >> (nx.bit_length() - 1)

        def look(q, acc):
            return jnp.where(line == q, jnp.take_along_axis(means[q], pos, axis=1), acc)

        val = lax.fori_loop(0, groups, look, jnp.zeros((8, nx), jnp.float32), unroll=small)
        beside = None
        for j in range(6):
            x = pltpu.roll(val, nx - n_loc * (1 + j), 1)
            beside = x if beside is None else beside + x
        smooth = 0.5 * head + (0.5 / 6.0) * beside
        refine = pltpu.roll(head, nx - 7 * n_loc, 1)
        owner = tail.astype(jnp.int32)
        weight = pltpu.roll(tail, nx - n_loc, 1)
        home = sub + 8 * g
        c = smooth * (1.0 + 7.0 * refine) + jnp.where(owner != home, 0.25 * weight, 0.0)
        acc_load = acc_load + jnp.where(ok & (owner == me), c, 0.0)
        acc_cost = acc_cost + jnp.where(home == me, c, 0.0)
        return acc_load, acc_cost

    zero = jnp.zeros((8, nx), jnp.float32)
    acc_load, acc_cost = lax.fori_loop(0, groups, group, (zero, zero), unroll=small)
    own = jnp.sum(acc_cost, axis=0, keepdims=True)
    for b in range(n_loc // per_ax):
        x = own if b == 0 else pltpu.roll(own, nx - b * per_ax, 1)
        cost[0, pl.ds(b, 1), :] = x[:, 0:per_ax]
    total = jnp.sum(jnp.sum(acc_load, axis=0, keepdims=True), axis=1, keepdims=True) * (1.0 / n_loc)
    load[0] = total


def on_device(primal, adjoint, refine_flag, owner_map, migrate_weight, neighbor_list):
    _, nr, na, nx = primal.shape
    dims = (nr, na, nx)
    sizes = n_rad, n_azi, n_ax = tuple(lax.axis_size(a) for a in AXES)
    n_dev = n_rad * n_azi * n_ax
    tiles = na // 8
    halves = nr * tiles // (nx // 4)
    f32 = functools.partial(jax.ShapeDtypeStruct, dtype=jnp.float32)
    anyspec = pl.BlockSpec(memory_space=pl.ANY)
    hbm = pl.BlockSpec(memory_space=pltpu.HBM)
    vmem = pl.BlockSpec(memory_space=pltpu.VMEM)

    rad_a, rad_b, azi_s = pl.pallas_call(
        functools.partial(edge_kernel, dims),
        out_shape=(f32((2 * F, 2, na, nx)), f32((2 * F, 2, na, nx)), f32((2 * F, nr, 4, nx))),
        in_specs=[hbm, hbm],
        out_specs=(vmem, vmem, vmem),
        scratch_shapes=[pltpu.SemaphoreType.DMA((2, 4))],
        compiler_params=pltpu.CompilerParams(vmem_limit_bytes=60 << 20),
        name="edges",
    )(primal, adjoint)
    ax_s = pl.pallas_call(
        functools.partial(lane_kernel, dims),
        out_shape=f32((2 * F, halves, 8, nx)),
        in_specs=[vmem, vmem],
        out_specs=vmem,
        compiler_params=pltpu.CompilerParams(vmem_limit_bytes=16 << 20),
        name="lanes",
    )(primal, adjoint)

    ax_a = lax.ppermute(ax_s, AXES, pair_round(sizes, 2, 0))
    ax_b = lax.ppermute(ax_s, AXES, pair_round(sizes, 2, 1))
    azi_l = lax.ppermute(azi_s, "azi", ring(n_azi, 1))
    azi_r = azi_l if n_azi == 2 else lax.ppermute(azi_s, "azi", ring(n_azi, -1))
    rad_a = lax.ppermute(rad_a, AXES, pair_round(sizes, 0, 0))
    rad_b = lax.ppermute(rad_b, AXES, pair_round(sizes, 0, 1))

    per_rad, per_azi, per_ax = nr // BLK, na // BLK, nx // BLK
    n_loc = per_rad * per_azi * per_ax
    near = neighbor_list.transpose(0, 3, 1, 2)
    cells = F * nr * na
    sums, fourth, row = pl.pallas_call(
        functools.partial(own_kernel, dims, ((per_rad, per_azi, per_ax), (n_azi, n_ax))),
        out_shape=(f32((cells, 2 * nx)), f32((cells, nx)), f32((1, 2 * nx))),
        in_specs=[vmem] * 7,
        out_specs=(vmem, vmem, vmem),
        scratch_shapes=[
            pltpu.VMEM((2 * cells, 3 * nx), jnp.bfloat16),
            pltpu.VMEM((3 * nx, 3 * nx), jnp.bfloat16),
        ],
        compiler_params=pltpu.CompilerParams(vmem_limit_bytes=16 << 20),
        name="own",
    )(primal, adjoint, ax_s, near, refine_flag, owner_map, migrate_weight)
    bw = pl.pallas_call(
        functools.partial(axial_kernel, dims, n_ax),
        out_shape=f32((2 * F, nr, na, nx)),
        in_specs=[vmem] * 4,
        out_specs=vmem,
        scratch_shapes=[
            pltpu.VMEM((3, 2 * F, halves, 8, nx), jnp.float32),
            pltpu.VMEM((2 * cells, nx), jnp.bfloat16),
            pltpu.VMEM((nx, 3 * nx), jnp.bfloat16),
            pltpu.VMEM((cells, 2 * nx), jnp.float32),
        ],
        compiler_params=pltpu.CompilerParams(vmem_limit_bytes=16 << 20),
        name="axial",
    )(sums, fourth, ax_a, ax_b)

    indicator, send = pl.pallas_call(
        functools.partial(main_kernel, dims, n_rad),
        out_shape=(f32(dims), f32((2 * n_dev, nx))),
        in_specs=[vmem] * 8,
        out_specs=(vmem, vmem),
        scratch_shapes=[
            pltpu.VMEM((2 * F, 4, na, nx), jnp.float32),
            pltpu.VMEM((2 * F, nr, 24, nx), jnp.float32),
            pltpu.VMEM((2 * F, nr, 16, nx), jnp.float32),
            pltpu.VMEM((F, tiles, 8, nx), jnp.float32),
            pltpu.VMEM((F, 8 + na, nx), jnp.float32),
        ],
        compiler_params=pltpu.CompilerParams(vmem_limit_bytes=32 << 20),
        name="stencil",
    )(primal, adjoint, bw, rad_a, rad_b, azi_l, azi_r, row)

    data = lax.all_to_all(send, AXES, 0, 0, tiled=True)

    cost, load = pl.pallas_call(
        functools.partial(final_kernel, n_loc, per_ax),
        out_shape=(f32((per_rad, per_azi, per_ax)), f32((1, 1, 1))),
        in_specs=[vmem],
        out_specs=(vmem, vmem),
        scratch_shapes=[pltpu.VMEM((n_dev // 8, 8, nx), jnp.float32)],
        compiler_params=pltpu.CompilerParams(vmem_limit_bytes=4 << 20),
        name="blocks",
    )(data)
    return indicator, cost, load


def solution(mesh):
    spec = P("rad", "azi", "ax")
    field = P(None, "rad", "azi", "ax")
    return jax.shard_map(
        on_device,
        mesh=mesh,
        in_specs=(field, field, spec, spec, spec, P("rad", "azi", "ax", None)),
        out_specs=(spec, spec, spec),
        check_vma=False,
    )
```

```python
import functools

import jax
import jax.numpy as jnp
from jax import lax
from jax.experimental import pallas as pl
from jax.experimental.pallas import tpu as pltpu
from jax.sharding import PartitionSpec as P

BLK = 16
F = 5
AXES = ("rad", "azi", "ax")


def pair_round(sizes, along, first):
    n = sizes[along]
    step = [sizes[1] * sizes[2], sizes[2], 1]
    used = range(first, n - 1, 2)
    partner = {i: i + 1 for i in used} | {i + 1: i for i in used}
    idle = [i for i in range(n) if i not in partner]
    if along == 2 and len(idle) == 2:
        partner |= {idle[0]: idle[1], idle[1]: idle[0]}
    pairs = []
    for me in range(sizes[0] * step[0]):
        i = me // step[along] % n
        if i in partner:
            pairs.append((me, me + (partner[i] - i) * step[along]))
        elif along != 2 and sizes[2] % 2 == 0:
            pairs.append((me, me ^ 1))
    return pairs


def ring(count, step):
    return [(i, (i + step) % count) for i in range(count)]


def edge_kernel(dims, prim, adj, rad_a, rad_b, azi_s, sems):
    nr, na, nx = dims
    odd = lax.rem(lax.axis_index("rad"), 2)
    first = jnp.where(odd == 0, nr - 2, 0)
    copies = []
    for t, src in enumerate((prim, adj)):
        rows = pl.ds(t * F, F)
        for i, (a, b) in enumerate(
            (
                (src.at[:, pl.ds(first, 2)], rad_a.at[rows]),
                (src.at[:, pl.ds(nr - 2 - first, 2)], rad_b.at[rows]),
                (src.at[:, :, pl.ds(0, 2)], azi_s.at[rows, :, pl.ds(0, 2)]),
                (src.at[:, :, pl.ds(na - 2, 2)], azi_s.at[rows, :, pl.ds(2, 2)]),
            )
        ):
            copies.append(pltpu.make_async_copy(a, b, sems.at[t, i]))
    for c in copies:
        c.start()
    for c in copies:
        c.wait()


def lane_kernel(dims, prim, adj, ax_s):
    nr, na, nx = dims
    slot = lax.broadcasted_iota(jnp.int32, (8, nx), 1) >> 2
    tiles = na // 8
    per = nx // 4
    for t, src in enumerate((prim, adj)):
        for f in range(F):
            for h in range(nr * tiles // per):
                acc = jnp.zeros((8, nx), jnp.float32)
                for j in range(per):
                    k = h * per + j
                    x = src[f, k // tiles, pl.ds(8 * (k % tiles), 8), :]
                    acc = jnp.where(slot == j, pltpu.roll(x, (4 * j + 2) % nx, 1), acc)
                ax_s[t * F + f, h] = acc


def flux(s, along):
    inv = 1.0 / s[0]
    v = s[1 + along] * inv
    kin = (s[1] * s[1] + s[2] * s[2] + s[3] * s[3]) * inv
    p = 0.4 * s[4] - 0.2 * kin
    out = [s[1 + along], s[1] * v, s[2] * v, s[3] * v, (s[4] + p) * v]
    out[1 + along] = out[1 + along] + p
    return out


def face(m1, c, p1, p2):
    return 7.0 * (c + p1) - (m1 + p2)


def split3(x):
    hi = x.astype(jnp.bfloat16)
    x = x - hi.astype(jnp.float32)
    mid = x.astype(jnp.bfloat16)
    x = x - mid.astype(jnp.float32)
    return hi, mid, x.astype(jnp.bfloat16)


def taps(rows, cols, table):
    out = jnp.zeros(rows.shape, jnp.float32)
    for step, value in table.items():
        out = jnp.where(rows - cols == step, value, out)
    return out


UPPER = {-1: -1.0, 0: 7.0, 1: 7.0, 2: -1.0}
LOWER = {-2: -1.0, -1: 7.0, 0: 7.0, 1: -1.0}
FOURTH = {-2: 1.0, -1: -4.0, 0: 6.0, 1: -4.0, 2: 1.0}


def block_row(grid, near, refine, owner, weight, nx):
    (per_rad, per_azi, per_ax), (n_azi, n_ax) = grid
    n_loc = per_rad * per_azi * per_ax
    blocks_azi, blocks_ax = per_azi * n_azi, per_ax * n_ax
    lane = lax.broadcasted_iota(jnp.int32, (per_azi, nx), 1)

    def place(number):
        b_rad = lax.div(number, blocks_azi * blocks_ax)
        b_azi = lax.rem(lax.div(number, blocks_ax), blocks_azi)
        b_ax = lax.rem(number, blocks_ax)
        device = (lax.div(b_rad, per_rad) * n_azi + lax.div(b_azi, per_azi)) * n_ax + lax.div(b_ax, per_ax)
        local = (lax.rem(b_rad, per_rad) * per_azi + lax.rem(b_azi, per_azi)) * per_ax + lax.rem(b_ax, per_ax)
        return device * n_loc + local

    def spread(x, at):
        x = jnp.concatenate([x, jnp.zeros((per_azi, nx - per_ax), jnp.int32)], axis=1)
        x = jnp.where(lane < per_ax, x, 0).astype(jnp.float32)
        rows = [x[b:b + 1] if at + b * per_ax == 0 else pltpu.roll(x[b:b + 1], at + b * per_ax, 1) for b in range(per_azi)]
        return sum(rows[1:], rows[0])

    head = spread(refine[0], 7 * n_loc)
    for j in range(6):
        head = head + spread(place(near[0, j]), (1 + j) * n_loc)
    tail = spread(owner[0], 0) + spread(weight[0], n_loc)
    return head, tail


def own_kernel(
    dims, grid, prim, adj, ax_s, near, refine, owner, weight, sums, fourth, row, lhs, rhs
):
    del ax_s
    nr, na, nx = dims
    head, tail = block_row(grid, near, refine, owner, weight, nx)
    row[:, 0:nx] = head
    row[:, nx:2 * nx] = tail
    size = nr * na
    i = lax.broadcasted_iota(jnp.int32, (nx, nx), 0)
    c = lax.broadcasted_iota(jnp.int32, (nx, nx), 1)
    for n, table in enumerate((UPPER, LOWER, FOURTH)):
        own = taps(i, c, table).astype(jnp.bfloat16)
        for k in range(3):
            rhs[pl.ds(k * nx, nx), pl.ds(n * nx, nx)] = own

    def build(t, src, f):
        for r in range(nr):
            rows = pl.ds(pl.multiple_of((t * F + f) * size, size) + r * na, na)
            for k, x in enumerate(split3(src[f, r])):
                lhs[rows, pl.ds(k * nx, nx)] = x

    for t, src in enumerate((prim, adj)):
        lax.fori_loop(0, F, lambda f, c, t=t, src=src: (build(t, src, f), c)[1], 0)
    sums[...] = jnp.dot(
        lhs[0:F * size, :], rhs[:, 0:2 * nx], preferred_element_type=jnp.float32
    )
    fourth[...] = jnp.dot(
        lhs[F * size:2 * F * size, :], rhs[:, 2 * nx:3 * nx], preferred_element_type=jnp.float32
    )


def axial_kernel(dims, n_ax, sums, fourth, part_bw, ax_a, ax_b, bw, done, got, lhs, rhs, far, far_w):
    nr, na, nx = dims
    i_ax = lax.axis_index("ax")
    even_ax = lax.rem(i_ax, 2) == 0
    lane = lax.broadcasted_iota(jnp.int32, (8, nx), 1)
    part = lane & 3
    slot = lane >> 2
    tiles = na // 8
    per = nx // 4
    halves = nr * tiles // per
    size = nr * na
    third = per // 3

    i = lax.broadcasted_iota(jnp.int32, (nx, nx), 0) & 3
    c = lax.broadcasted_iota(jnp.int32, (nx, nx), 1)
    cells = jnp.where(i < 2, i - 2, i - 2 + nx)
    for n, table in enumerate((UPPER, LOWER, FOURTH)):
        rhs[:, pl.ds(n * nx, nx)] = taps(cells, c, table).astype(jnp.bfloat16)

    for h in range(halves):
        for f in range(2 * F):
            a, b = ax_a[f, h], ax_b[f, h]
            left = jnp.where(i_ax == 0, 0.0, jnp.where(even_ax, b, a))
            right = jnp.where(i_ax == n_ax - 1, 0.0, jnp.where(even_ax, a, b))
            for k, x in enumerate(split3(jnp.where(part < 2, left, right))):
                x = x.astype(jnp.float32)
                got[k, f, h] = pltpu.roll(x, 4 * third * k, 1) if k else x

    def build(g, carry):
        for r in range(nr):
            h, j0 = r * tiles // per, r * tiles % per
            rows = pl.ds(pl.multiple_of(g * size, size) + r * na, na)
            y = []
            for a in range(tiles):
                x = jnp.zeros((8, nx), jnp.float32)
                for k in range(3):
                    x = jnp.where(slot == (j0 + a + third * k) % per, got[k, g, h], x)
                y.append(x)
            lhs[rows, :] = jnp.concatenate(y, axis=0).astype(jnp.bfloat16)
        return carry

    lax.fori_loop(0, 2 * F, build, 0)
    far[...] = jnp.dot(lhs[0:F * size, :], rhs[:, 0:2 * nx], preferred_element_type=jnp.float32)
    far_w[...] = jnp.dot(
        lhs[F * size:2 * F * size, :], rhs[:, 2 * nx:3 * nx], preferred_element_type=jnp.float32
    )

    def tile(r, a, whole):
        mine = pl.ds(8 * a, 8)
        at = [pl.ds(f * size + r * na + 8 * a, 8) for f in range(F)]
        up = flux([sums[q, 0:nx] + far[q, 0:nx] for q in at], 2)
        low = flux([sums[q, nx:2 * nx] + far[q, nx:2 * nx] for q in at], 2)
        total = None
        for f in range(F):
            bal = part_bw[f, r, mine, :] + (up[f] - low[f])
            w = part_bw[F + f, r, mine, :] + (fourth[at[f], :] + far_w[at[f], :])
            if whole:
                total = w * bal if total is None else total + w * bal
            else:
                bw[f, r, mine, :] = bal
                bw[F + f, r, mine, :] = w
        if whole:
            done[r, mine, :] = jnp.abs(total) * (1.0 / 144.0)

    def body(r, carry):
        for a in range(tiles):
            tile(r, a, 0 < a < tiles - 1)
        return carry

    for r in (0, 1, nr - 2, nr - 1):
        for a in range(tiles):
            tile(r, a, False)
    lax.fori_loop(2, nr - 2, body, 0)


def shifted(src, f, r, a, tiles, da):
    if da < 0 and a == 0 or da > 0 and a == tiles - 1:
        return pltpu.roll(src[f, r, pl.ds(8 * a, 8), :], -da % 8, 0)
    return src[f, r, pl.ds(8 * a + da, 8), :]


def inner_kernel(dims, prim, adj, dep, bw, frad, fazi):
    del dep
    nr, na, nx = dims
    tiles = na // 8
    sub = lax.broadcasted_iota(jnp.int32, (8, nx), 0)
    zero = jnp.zeros((8, nx), jnp.float32)

    def rad_flux(r, a):
        rows = pl.ds(8 * a, 8)
        return flux([face(*(prim[f, r + o, rows, :] for o in (-1, 0, 1, 2))) for f in range(F)], 0)

    def azi_flux(r, a):
        x = flux([face(*(shifted(prim, f, r, a, tiles, o) for o in (-1, 0, 1, 2))) for f in range(F)], 1)
        if a == 0:
            x = [jnp.where(sub < 1, 0.0, t) for t in x]
        if a == tiles - 1:
            x = [jnp.where(sub > 5, 0.0, t) for t in x]
        return x

    for f in range(F):
        fazi[f, 0:8, :] = zero

    def plane(r, carry):
        here = not isinstance(r, int) or 1 <= r <= nr - 3
        before = not isinstance(r, int) or 1 <= r - 1 <= nr - 3
        for a in range(tiles):
            for f, x in enumerate(azi_flux(r, a)):
                fazi[f, pl.ds(8 + 8 * a, 8), :] = x
        for a in range(tiles):
            mine = pl.ds(8 * a, 8)
            up = rad_flux(r, a) if here else None
            for f in range(F):
                bal = fazi[f, pl.ds(8 * a + 8, 8), :] - fazi[f, pl.ds(8 * a + 7, 8), :]
                if before:
                    bal = bal - frad[f, a]
                if here:
                    bal = bal + up[f]
                    frad[f, a] = up[f]
                bw[f, r, mine, :] = bal

                def row(da):
                    x = shifted(adj, f, r, a, tiles, da)
                    if da < 0 and a == 0:
                        x = jnp.where(sub < -da, 0.0, x)
                    if da > 0 and a == tiles - 1:
                        x = jnp.where(sub > 7 - da, 0.0, x)
                    return x

                def layer(dr):
                    if isinstance(r, int) and not 0 <= r + dr < nr:
                        return None
                    return adj[f, r + dr, mine, :]

                two, one = row(-2) + row(2), row(-1) + row(1)
                for dr in (-2, 2):
                    x = layer(dr)
                    two = two if x is None else two + x
                for dr in (-1, 1):
                    x = layer(dr)
                    one = one if x is None else one + x
                bw[F + f, r, mine, :] = two - 4.0 * one + 12.0 * adj[f, r, mine, :]
        return carry

    for r in (0, 1):
        plane(r, 0)
    lax.fori_loop(2, nr - 2, plane, 0)
    for r in (nr - 2, nr - 1):
        plane(r, 0)


def edge_terms(dims, n_rad, prim, adj, rad_a, rad_b, azi_l, azi_r):
    nr, na, nx = dims
    i_rad = lax.axis_index("rad")
    odd = lax.rem(i_rad, 2) == 1
    tiles = na // 8
    sub = lax.broadcasted_iota(jnp.int32, (8, nx), 0)

    def before(g, i, rows):
        return jnp.where(i_rad == 0, 0.0, jnp.where(odd, rad_a[g, i, rows, :], rad_b[g, i, rows, :]))

    def after(g, i, rows):
        x = jnp.where(odd, rad_b[g, i, rows, :], rad_a[g, i, rows, :])
        return jnp.where(i_rad == n_rad - 1, 0.0, x)

    def radial(a):
        rows = pl.ds(8 * a, 8)
        low, high = [], []
        for f in range(F):
            b0, b1, h0, h1 = (before(f, 0, rows), before(f, 1, rows), after(f, 0, rows), after(f, 1, rows))
            u0, u1, u2 = (prim[f, i, rows, :] for i in range(3))
            v2, v1, v0 = (prim[f, nr - i, rows, :] for i in (3, 2, 1))
            low.append((face(b0, b1, u0, u1), face(b1, u0, u1, u2)))
            high.append((face(v2, v1, v0, h0), face(v1, v0, h0, h1)))
        p, q = (flux([x[i] for x in low], 0) for i in range(2))
        s, t = (flux([x[i] for x in high], 0) for i in range(2))
        bal = {
            0: [y - x for x, y in zip(p, q)],
            1: [-y for y in q],
            nr - 2: s,
            nr - 1: [y - x for x, y in zip(s, t)],
        }
        w = {0: [], 1: [], nr - 2: [], nr - 1: []}
        for f in range(F):
            g = F + f
            b0, b1, h0, h1 = (before(g, 0, rows), before(g, 1, rows), after(g, 0, rows), after(g, 1, rows))
            w[0].append(b0 - 4.0 * b1)
            w[1].append(b1)
            w[nr - 2].append(h0)
            w[nr - 1].append(h1 - 4.0 * h0)
        return bal, w

    def azimuthal(r, a):
        if a == 0:
            def layer(g, i):
                return jnp.broadcast_to(azi_l[g, r, 2 + i:3 + i, :], (8, nx))

            s = []
            for f in range(F):
                x = prim[f, r, 0:8, :]
                l0, l1 = layer(f, 0), layer(f, 1)
                s.append(
                    face(
                        jnp.where(sub == 0, l0, jnp.where(sub == 1, l1, pltpu.roll(x, 2, 0))),
                        jnp.where(sub == 0, l1, pltpu.roll(x, 1, 0)),
                        x,
                        prim[f, r, 1:9, :],
                    )
                )
            bal = [
                jnp.where(sub == 0, pltpu.roll(x, 7, 0) - x, jnp.where(sub == 1, -x, 0.0))
                for x in flux(s, 1)
            ]
            w = []
            for f in range(F):
                l0, l1 = layer(F + f, 0), layer(F + f, 1)
                w.append(jnp.where(sub == 0, l0 - 4.0 * l1, jnp.where(sub == 1, l1, 0.0)))
            return bal, w

        def layer(g, i):
            return jnp.broadcast_to(azi_r[g, r, i:i + 1, :], (8, nx))

        s = []
        for f in range(F):
            x = prim[f, r, na - 8:na, :]
            h0, h1 = layer(f, 0), layer(f, 1)
            s.append(
                face(
                    prim[f, r, na - 9:na - 1, :],
                    x,
                    jnp.where(sub == 7, h0, pltpu.roll(x, 7, 0)),
                    jnp.where(sub == 7, h1, jnp.where(sub == 6, h0, pltpu.roll(x, 6, 0))),
                )
            )
        bal = [
            jnp.where(sub == 7, x - pltpu.roll(x, 1, 0), jnp.where(sub == 6, x, 0.0)) for x in flux(s, 1)
        ]
        w = []
        for f in range(F):
            h0, h1 = layer(F + f, 0), layer(F + f, 1)
            w.append(jnp.where(sub == 7, h1 - 4.0 * h0, jnp.where(sub == 6, h0, 0.0)))
        return bal, w

    return radial, azimuthal


def main_kernel(dims, n_rad, prim, adj, bw, done, rad_a, rad_b, azi_l, azi_r, row, ind, send):
    nr, na, nx = dims
    tiles = na // 8
    lane = lax.broadcasted_iota(jnp.int32, (8, nx), 1)
    radial, azimuthal = edge_terms(dims, n_rad, prim, adj, rad_a, rad_b, azi_l, azi_r)

    def outer(r, a, extra):
        mine = pl.ds(8 * a, 8)
        bal = [bw[f, r, mine, :] for f in range(F)]
        w = [bw[F + f, r, mine, :] for f in range(F)]
        for more_bal, more_w in extra:
            bal = [x + y for x, y in zip(bal, more_bal)]
            w = [x + y for x, y in zip(w, more_w)]
        total = w[0] * bal[0]
        for f in range(1, F):
            total = total + w[f] * bal[f]
        total = jnp.abs(total) * (1.0 / 144.0)
        ind[r, mine, :] = total
        return total

    ends = (0, 1, nr - 2, nr - 1)
    sums = [jnp.zeros((8, nx), jnp.float32) for _ in range(tiles)]
    for a in range(tiles):
        bal, w = radial(a)
        for r in ends:
            extra = [(bal[r], w[r])]
            if a in (0, tiles - 1):
                extra.append(azimuthal(r, a))
            sums[a] = sums[a] + outer(r, a, extra)

    def plane(r, sums):
        out = []
        for a in range(tiles):
            if a in (0, tiles - 1):
                x = outer(r, a, [azimuthal(r, a)])
            else:
                x = done[r, pl.ds(8 * a, 8), :]
                ind[r, pl.ds(8 * a, 8), :] = x
            out.append(sums[a] + x)
        return tuple(out)

    sums = lax.fori_loop(2, nr - 2, plane, tuple(sums))

    groups = nx // BLK
    halves_a = na // BLK
    per_tile = BLK // 8
    means = jnp.zeros((8, nx), jnp.float32)
    for b in range(halves_a):
        t = sums[b * per_tile]
        for i in range(1, per_tile):
            t = t + sums[b * per_tile + i]
        t = jnp.broadcast_to(jnp.sum(t, axis=0, keepdims=True), (8, nx))
        for sh in (8, 4, 2, 1):
            t = t + pltpu.roll(t, nx - sh, 1)
        t = jnp.take_along_axis(t, (lane % groups) * BLK, axis=1)
        means = jnp.where(lane // groups == b, t, means)
    means = means * (1.0 / BLK**3)
    head = jnp.broadcast_to(row[:, 0:nx], (8, nx))
    head = jnp.where(lane < groups * halves_a, means, head)
    tail = jnp.broadcast_to(row[:, nx:2 * nx], (8, nx))
    both = jnp.where(lax.broadcasted_iota(jnp.int32, (8, nx), 0) & 1 == 0, head, tail)
    for d in range(send.shape[0] // 8):
        send[pl.ds(8 * d, 8), :] = both


def final_kernel(n_loc, per_ax, data, cost, load, means):
    n_dev, nx = data.shape[0] // 2, data.shape[1]
    me = (lax.axis_index("rad") * lax.axis_size("azi") + lax.axis_index("azi")) * lax.axis_size(
        "ax"
    ) + lax.axis_index("ax")
    lane = lax.broadcasted_iota(jnp.int32, (8, nx), 1)
    sub = lax.broadcasted_iota(jnp.int32, (8, nx), 0)
    small = n_dev <= 32
    groups = n_dev // 8
    ok = lane < n_loc

    def rows(g, part):
        return data[pl.ds(16 * g + part, 8, stride=2), :]

    def table(g, carry):
        x = jnp.where(ok, rows(g, 0), 0.0)
        x = pltpu.roll(x, 0, 1, stride=n_loc, stride_axis=0)
        means[g] = jnp.broadcast_to(jnp.sum(x, axis=0, keepdims=True), (8, nx))
        return carry

    lax.fori_loop(0, groups, table, 0, unroll=small)

    def group(g, carry):
        acc_load, acc_cost = carry
        head = rows(g, 0)
        tail = rows(g, 1)
        spot = head.astype(jnp.int32)
        pos = spot & (nx - 1)
        line = spot >> (nx.bit_length() - 1)

        def look(q, acc):
            return jnp.where(line == q, jnp.take_along_axis(means[q], pos, axis=1), acc)

        val = lax.fori_loop(0, groups, look, jnp.zeros((8, nx), jnp.float32), unroll=small)
        beside = None
        for j in range(6):
            x = pltpu.roll(val, nx - n_loc * (1 + j), 1)
            beside = x if beside is None else beside + x
        smooth = 0.5 * head + (0.5 / 6.0) * beside
        refine = pltpu.roll(head, nx - 7 * n_loc, 1)
        owner = tail.astype(jnp.int32)
        weight = pltpu.roll(tail, nx - n_loc, 1)
        home = sub + 8 * g
        c = smooth * (1.0 + 7.0 * refine) + jnp.where(owner != home, 0.25 * weight, 0.0)
        acc_load = acc_load + jnp.where(ok & (owner == me), c, 0.0)
        acc_cost = acc_cost + jnp.where(home == me, c, 0.0)
        return acc_load, acc_cost

    zero = jnp.zeros((8, nx), jnp.float32)
    acc_load, acc_cost = lax.fori_loop(0, groups, group, (zero, zero), unroll=small)
    own = jnp.sum(acc_cost, axis=0, keepdims=True)
    for b in range(n_loc // per_ax):
        x = own if b == 0 else pltpu.roll(own, nx - b * per_ax, 1)
        cost[0, pl.ds(b, 1), :] = x[:, 0:per_ax]
    total = jnp.sum(jnp.sum(acc_load, axis=0, keepdims=True), axis=1, keepdims=True) * (1.0 / n_loc)
    load[0] = total


def on_device(primal, adjoint, refine_flag, owner_map, migrate_weight, neighbor_list):
    _, nr, na, nx = primal.shape
    dims = (nr, na, nx)
    sizes = n_rad, n_azi, n_ax = tuple(lax.axis_size(a) for a in AXES)
    n_dev = n_rad * n_azi * n_ax
    tiles = na // 8
    halves = nr * tiles // (nx // 4)
    f32 = functools.partial(jax.ShapeDtypeStruct, dtype=jnp.float32)
    anyspec = pl.BlockSpec(memory_space=pl.ANY)
    hbm = pl.BlockSpec(memory_space=pltpu.HBM)
    vmem = pl.BlockSpec(memory_space=pltpu.VMEM)

    rad_a, rad_b, azi_s = pl.pallas_call(
        functools.partial(edge_kernel, dims),
        out_shape=(f32((2 * F, 2, na, nx)), f32((2 * F, 2, na, nx)), f32((2 * F, nr, 4, nx))),
        in_specs=[hbm, hbm],
        out_specs=(vmem, vmem, vmem),
        scratch_shapes=[pltpu.SemaphoreType.DMA((2, 4))],
        compiler_params=pltpu.CompilerParams(vmem_limit_bytes=60 << 20),
        name="edges",
    )(primal, adjoint)
    ax_s = pl.pallas_call(
        functools.partial(lane_kernel, dims),
        out_shape=f32((2 * F, halves, 8, nx)),
        in_specs=[vmem, vmem],
        out_specs=vmem,
        compiler_params=pltpu.CompilerParams(vmem_limit_bytes=16 << 20),
        name="lanes",
    )(primal, adjoint)

    ax_a = lax.ppermute(ax_s, AXES, pair_round(sizes, 2, 0))
    ax_b = lax.ppermute(ax_s, AXES, pair_round(sizes, 2, 1))
    azi_l = lax.ppermute(azi_s, "azi", ring(n_azi, 1))
    azi_r = azi_l if n_azi == 2 else lax.ppermute(azi_s, "azi", ring(n_azi, -1))
    rad_a = lax.ppermute(rad_a, AXES, pair_round(sizes, 0, 0))
    rad_b = lax.ppermute(rad_b, AXES, pair_round(sizes, 0, 1))

    per_rad, per_azi, per_ax = nr // BLK, na // BLK, nx // BLK
    n_loc = per_rad * per_azi * per_ax
    near = neighbor_list.transpose(0, 3, 1, 2)
    cells = F * nr * na
    sums, fourth, row = pl.pallas_call(
        functools.partial(own_kernel, dims, ((per_rad, per_azi, per_ax), (n_azi, n_ax))),
        out_shape=(f32((cells, 2 * nx)), f32((cells, nx)), f32((1, 2 * nx))),
        in_specs=[vmem] * 7,
        out_specs=(vmem, vmem, vmem),
        scratch_shapes=[
            pltpu.VMEM((2 * cells, 3 * nx), jnp.bfloat16),
            pltpu.VMEM((3 * nx, 3 * nx), jnp.bfloat16),
        ],
        compiler_params=pltpu.CompilerParams(vmem_limit_bytes=16 << 20),
        name="own",
    )(primal, adjoint, ax_s, near, refine_flag, owner_map, migrate_weight)
    part_bw = pl.pallas_call(
        functools.partial(inner_kernel, dims),
        out_shape=f32((2 * F, nr, na, nx)),
        in_specs=[vmem] * 3,
        out_specs=vmem,
        scratch_shapes=[
            pltpu.VMEM((F, tiles, 8, nx), jnp.float32),
            pltpu.VMEM((F, 8 + na, nx), jnp.float32),
        ],
        compiler_params=pltpu.CompilerParams(vmem_limit_bytes=16 << 20),
        name="inner",
    )(primal, adjoint, row)
    bw, done = pl.pallas_call(
        functools.partial(axial_kernel, dims, n_ax),
        out_shape=(f32((2 * F, nr, na, nx)), f32(dims)),
        in_specs=[vmem] * 5,
        out_specs=(vmem, vmem),
        scratch_shapes=[
            pltpu.VMEM((3, 2 * F, halves, 8, nx), jnp.float32),
            pltpu.VMEM((2 * cells, nx), jnp.bfloat16),
            pltpu.VMEM((nx, 3 * nx), jnp.bfloat16),
            pltpu.VMEM((cells, 2 * nx), jnp.float32),
            pltpu.VMEM((cells, nx), jnp.float32),
        ],
        compiler_params=pltpu.CompilerParams(vmem_limit_bytes=16 << 20),
        name="axial",
    )(sums, fourth, part_bw, ax_a, ax_b)

    indicator, send = pl.pallas_call(
        functools.partial(main_kernel, dims, n_rad),
        out_shape=(f32(dims), f32((2 * n_dev, nx))),
        in_specs=[vmem] * 9,
        out_specs=(vmem, vmem),
        compiler_params=pltpu.CompilerParams(vmem_limit_bytes=16 << 20),
        name="stencil",
    )(primal, adjoint, bw, done, rad_a, rad_b, azi_l, azi_r, row)

    data = lax.all_to_all(send, AXES, 0, 0, tiled=True)

    cost, load = pl.pallas_call(
        functools.partial(final_kernel, n_loc, per_ax),
        out_shape=(f32((per_rad, per_azi, per_ax)), f32((1, 1, 1))),
        in_specs=[vmem],
        out_specs=(vmem, vmem),
        scratch_shapes=[pltpu.VMEM((n_dev // 8, 8, nx), jnp.float32)],
        compiler_params=pltpu.CompilerParams(vmem_limit_bytes=4 << 20),
        name="blocks",
    )(data)
    return indicator, cost, load


def solution(mesh):
    spec = P("rad", "azi", "ax")
    field = P(None, "rad", "azi", "ax")
    return jax.shard_map(
        on_device,
        mesh=mesh,
        in_specs=(field, field, spec, spec, spec, P("rad", "azi", "ax", None)),
        out_specs=(spec, spec, spec),
        check_vma=False,
    )
```

```python
import functools

import jax
import jax.numpy as jnp
from jax import lax
from jax.experimental import pallas as pl
from jax.experimental.pallas import tpu as pltpu
from jax.sharding import PartitionSpec as P

BLK = 16
F = 5
AXES = ("rad", "azi", "ax")


def pair_round(sizes, along, first):
    n = sizes[along]
    step = [sizes[1] * sizes[2], sizes[2], 1]
    used = range(first, n - 1, 2)
    partner = {i: i + 1 for i in used} | {i + 1: i for i in used}
    idle = [i for i in range(n) if i not in partner]
    if along == 2 and len(idle) == 2:
        partner |= {idle[0]: idle[1], idle[1]: idle[0]}
    pairs = []
    for me in range(sizes[0] * step[0]):
        i = me // step[along] % n
        if i in partner:
            pairs.append((me, me + (partner[i] - i) * step[along]))
        elif along != 2 and sizes[2] % 2 == 0:
            pairs.append((me, me ^ 1))
    return pairs


def ring(count, step):
    return [(i, (i + step) % count) for i in range(count)]


def edge_kernel(dims, prim, adj, rad_a, rad_b, azi_s, sems):
    nr, na, nx = dims
    odd = lax.rem(lax.axis_index("rad"), 2)
    first = jnp.where(odd == 0, nr - 2, 0)
    copies = []
    for t, src in enumerate((prim, adj)):
        rows = pl.ds(t * F, F)
        for i, (a, b) in enumerate(
            (
                (src.at[:, pl.ds(first, 2)], rad_a.at[rows]),
                (src.at[:, pl.ds(nr - 2 - first, 2)], rad_b.at[rows]),
                (src.at[:, :, pl.ds(0, 2)], azi_s.at[rows, :, pl.ds(0, 2)]),
                (src.at[:, :, pl.ds(na - 2, 2)], azi_s.at[rows, :, pl.ds(2, 2)]),
            )
        ):
            copies.append(pltpu.make_async_copy(a, b, sems.at[t, i]))
    for c in copies:
        c.start()
    for c in copies:
        c.wait()


def lane_kernel(dims, prim, adj, ax_s):
    nr, na, nx = dims
    slot = lax.broadcasted_iota(jnp.int32, (8, nx), 1) >> 2
    tiles = na // 8
    per = nx // 4
    for t, src in enumerate((prim, adj)):
        for f in range(F):
            for h in range(nr * tiles // per):
                acc = jnp.zeros((8, nx), jnp.float32)
                for j in range(per):
                    k = h * per + j
                    x = src[f, k // tiles, pl.ds(8 * (k % tiles), 8), :]
                    acc = jnp.where(slot == j, pltpu.roll(x, (4 * j + 2) % nx, 1), acc)
                ax_s[t * F + f, h] = acc


def flux(s, along):
    inv = 1.0 / s[0]
    v = s[1 + along] * inv
    kin = (s[1] * s[1] + s[2] * s[2] + s[3] * s[3]) * inv
    p = 0.4 * s[4] - 0.2 * kin
    out = [s[1 + along], s[1] * v, s[2] * v, s[3] * v, (s[4] + p) * v]
    out[1 + along] = out[1 + along] + p
    return out


def face(m1, c, p1, p2):
    return 7.0 * (c + p1) - (m1 + p2)


def split3(x):
    hi = x.astype(jnp.bfloat16)
    x = x - hi.astype(jnp.float32)
    mid = x.astype(jnp.bfloat16)
    x = x - mid.astype(jnp.float32)
    return hi, mid, x.astype(jnp.bfloat16)


def taps(rows, cols, table):
    out = jnp.zeros(rows.shape, jnp.float32)
    for step, value in table.items():
        out = jnp.where(rows - cols == step, value, out)
    return out


UPPER = {-1: -1.0, 0: 7.0, 1: 7.0, 2: -1.0}
LOWER = {-2: -1.0, -1: 7.0, 0: 7.0, 1: -1.0}
FOURTH = {-2: 1.0, -1: -4.0, 0: 6.0, 1: -4.0, 2: 1.0}


def block_row(grid, near, refine, owner, weight, nx):
    (per_rad, per_azi, per_ax), (n_azi, n_ax) = grid
    n_loc = per_rad * per_azi * per_ax
    blocks_azi, blocks_ax = per_azi * n_azi, per_ax * n_ax
    lane = lax.broadcasted_iota(jnp.int32, (per_azi, nx), 1)

    def place(number):
        b_rad = lax.div(number, blocks_azi * blocks_ax)
        b_azi = lax.rem(lax.div(number, blocks_ax), blocks_azi)
        b_ax = lax.rem(number, blocks_ax)
        device = (lax.div(b_rad, per_rad) * n_azi + lax.div(b_azi, per_azi)) * n_ax + lax.div(b_ax, per_ax)
        local = (lax.rem(b_rad, per_rad) * per_azi + lax.rem(b_azi, per_azi)) * per_ax + lax.rem(b_ax, per_ax)
        return device * n_loc + local

    def spread(x, at):
        x = jnp.concatenate([x, jnp.zeros((per_azi, nx - per_ax), jnp.int32)], axis=1)
        x = jnp.where(lane < per_ax, x, 0).astype(jnp.float32)
        rows = [x[b:b + 1] if at + b * per_ax == 0 else pltpu.roll(x[b:b + 1], at + b * per_ax, 1) for b in range(per_azi)]
        return sum(rows[1:], rows[0])

    head = spread(refine[0], 7 * n_loc)
    for j in range(6):
        head = head + spread(place(near[0, j]), (1 + j) * n_loc)
    tail = spread(owner[0], 0) + spread(weight[0], n_loc)
    return head, tail


def own_kernel(
    dims, grid, prim, adj, ax_s, near, refine, owner, weight, sums, fourth, row, lhs, rhs
):
    del ax_s
    nr, na, nx = dims
    head, tail = block_row(grid, near, refine, owner, weight, nx)
    row[:, 0:nx] = head
    row[:, nx:2 * nx] = tail
    size = nr * na
    i = lax.broadcasted_iota(jnp.int32, (nx, nx), 0)
    c = lax.broadcasted_iota(jnp.int32, (nx, nx), 1)
    for n, table in enumerate((UPPER, LOWER, FOURTH)):
        own = taps(i, c, table).astype(jnp.bfloat16)
        for k in range(3):
            rhs[pl.ds(k * nx, nx), pl.ds(n * nx, nx)] = own

    def build(t, src, f):
        for r in range(nr):
            rows = pl.ds(pl.multiple_of((t * F + f) * size, size) + r * na, na)
            for k, x in enumerate(split3(src[f, r])):
                lhs[rows, pl.ds(k * nx, nx)] = x

    for t, src in enumerate((prim, adj)):
        lax.fori_loop(0, F, lambda f, c, t=t, src=src: (build(t, src, f), c)[1], 0)
    sums[...] = jnp.dot(
        lhs[0:F * size, :], rhs[:, 0:2 * nx], preferred_element_type=jnp.float32
    )
    fourth[...] = jnp.dot(
        lhs[F * size:2 * F * size, :], rhs[:, 2 * nx:3 * nx], preferred_element_type=jnp.float32
    )


def axial_kernel(dims, n_ax, sums, fourth, part_bw, ax_a, ax_b, bw, done, got, lhs, rhs, far, far_w):
    nr, na, nx = dims
    i_ax = lax.axis_index("ax")
    even_ax = lax.rem(i_ax, 2) == 0
    lane = lax.broadcasted_iota(jnp.int32, (8, nx), 1)
    part = lane & 3
    slot = lane >> 2
    tiles = na // 8
    per = nx // 4
    halves = nr * tiles // per
    size = nr * na
    third = per // 3

    i = lax.broadcasted_iota(jnp.int32, (nx, nx), 0) & 3
    c = lax.broadcasted_iota(jnp.int32, (nx, nx), 1)
    cells = jnp.where(i < 2, i - 2, i - 2 + nx)
    for n, table in enumerate((UPPER, LOWER, FOURTH)):
        rhs[:, pl.ds(n * nx, nx)] = taps(cells, c, table).astype(jnp.bfloat16)

    for h in range(halves):
        for f in range(2 * F):
            a, b = ax_a[f, h], ax_b[f, h]
            left = jnp.where(i_ax == 0, 0.0, jnp.where(even_ax, b, a))
            right = jnp.where(i_ax == n_ax - 1, 0.0, jnp.where(even_ax, a, b))
            for k, x in enumerate(split3(jnp.where(part < 2, left, right))):
                x = x.astype(jnp.float32)
                got[k, f, h] = pltpu.roll(x, 4 * third * k, 1) if k else x

    def build(g, carry):
        for r in range(nr):
            h, j0 = r * tiles // per, r * tiles % per
            rows = pl.ds(pl.multiple_of(g * size, size) + r * na, na)
            y = []
            for a in range(tiles):
                x = jnp.zeros((8, nx), jnp.float32)
                for k in range(3):
                    x = jnp.where(slot == (j0 + a + third * k) % per, got[k, g, h], x)
                y.append(x)
            lhs[rows, :] = jnp.concatenate(y, axis=0).astype(jnp.bfloat16)
        return carry

    lax.fori_loop(0, 2 * F, build, 0)
    far[...] = jnp.dot(lhs[0:F * size, :], rhs[:, 0:2 * nx], preferred_element_type=jnp.float32)
    far_w[...] = jnp.dot(
        lhs[F * size:2 * F * size, :], rhs[:, 2 * nx:3 * nx], preferred_element_type=jnp.float32
    )

    def tile(r, a, whole):
        mine = pl.ds(8 * a, 8)
        at = [pl.ds(f * size + r * na + 8 * a, 8) for f in range(F)]
        up = flux([sums[q, 0:nx] + far[q, 0:nx] for q in at], 2)
        low = flux([sums[q, nx:2 * nx] + far[q, nx:2 * nx] for q in at], 2)
        total = None
        for f in range(F):
            bal = part_bw[f, r, mine, :] + (up[f] - low[f])
            w = part_bw[F + f, r, mine, :] + (fourth[at[f], :] + far_w[at[f], :])
            if whole:
                total = w * bal if total is None else total + w * bal
            else:
                bw[f, r, mine, :] = bal
                bw[F + f, r, mine, :] = w
        if whole:
            done[r, mine, :] = jnp.abs(total) * (1.0 / 144.0)

    def body(r, carry):
        for a in range(tiles):
            tile(r, a, 0 < a < tiles - 1)
        return carry

    for r in (0, 1, nr - 2, nr - 1):
        for a in range(tiles):
            tile(r, a, False)
    lax.fori_loop(2, nr - 2, body, 0)


def shifted(src, f, r, a, tiles, da):
    if da < 0 and a == 0 or da > 0 and a == tiles - 1:
        return pltpu.roll(src[f, r, pl.ds(8 * a, 8), :], -da % 8, 0)
    return src[f, r, pl.ds(8 * a + da, 8), :]


def inner_kernel(dims, prim, adj, dep, bw, frad, fazi):
    del dep
    nr, na, nx = dims
    tiles = na // 8
    sub = lax.broadcasted_iota(jnp.int32, (8, nx), 0)
    zero = jnp.zeros((8, nx), jnp.float32)

    def rad_flux(r, a):
        rows = pl.ds(8 * a, 8)
        return flux([face(*(prim[f, r + o, rows, :] for o in (-1, 0, 1, 2))) for f in range(F)], 0)

    def azi_flux(r, a):
        x = flux([face(*(shifted(prim, f, r, a, tiles, o) for o in (-1, 0, 1, 2))) for f in range(F)], 1)
        if a == 0:
            x = [jnp.where(sub < 1, 0.0, t) for t in x]
        if a == tiles - 1:
            x = [jnp.where(sub > 5, 0.0, t) for t in x]
        return x

    for f in range(F):
        fazi[f, 0:8, :] = zero

    def plane(r, carry):
        here = not isinstance(r, int) or 1 <= r <= nr - 3
        before = not isinstance(r, int) or 1 <= r - 1 <= nr - 3
        for a in range(tiles):
            for f, x in enumerate(azi_flux(r, a)):
                fazi[f, pl.ds(8 + 8 * a, 8), :] = x
        for a in range(tiles):
            mine = pl.ds(8 * a, 8)
            up = rad_flux(r, a) if here else None
            for f in range(F):
                bal = fazi[f, pl.ds(8 * a + 8, 8), :] - fazi[f, pl.ds(8 * a + 7, 8), :]
                if before:
                    bal = bal - frad[f, a]
                if here:
                    bal = bal + up[f]
                    frad[f, a] = up[f]
                bw[f, r, mine, :] = bal

                def row(da):
                    x = shifted(adj, f, r, a, tiles, da)
                    if da < 0 and a == 0:
                        x = jnp.where(sub < -da, 0.0, x)
                    if da > 0 and a == tiles - 1:
                        x = jnp.where(sub > 7 - da, 0.0, x)
                    return x

                def layer(dr):
                    if isinstance(r, int) and not 0 <= r + dr < nr:
                        return None
                    return adj[f, r + dr, mine, :]

                two, one = row(-2) + row(2), row(-1) + row(1)
                for dr in (-2, 2):
                    x = layer(dr)
                    two = two if x is None else two + x
                for dr in (-1, 1):
                    x = layer(dr)
                    one = one if x is None else one + x
                bw[F + f, r, mine, :] = two - 4.0 * one + 12.0 * adj[f, r, mine, :]
        return carry

    for r in (0, 1):
        plane(r, 0)
    lax.fori_loop(2, nr - 2, plane, 0)
    for r in (nr - 2, nr - 1):
        plane(r, 0)


def edge_terms(dims, n_rad, prim, adj, rad_a, rad_b, azi_l, azi_r):
    nr, na, nx = dims
    i_rad = lax.axis_index("rad")
    odd = lax.rem(i_rad, 2) == 1
    tiles = na // 8
    sub = lax.broadcasted_iota(jnp.int32, (8, nx), 0)

    def before(g, i, rows):
        return jnp.where(i_rad == 0, 0.0, jnp.where(odd, rad_a[g, i, rows, :], rad_b[g, i, rows, :]))

    def after(g, i, rows):
        x = jnp.where(odd, rad_b[g, i, rows, :], rad_a[g, i, rows, :])
        return jnp.where(i_rad == n_rad - 1, 0.0, x)

    def radial(a):
        rows = pl.ds(8 * a, 8)
        low, high = [], []
        for f in range(F):
            b0, b1, h0, h1 = (before(f, 0, rows), before(f, 1, rows), after(f, 0, rows), after(f, 1, rows))
            u0, u1, u2 = (prim[f, i, rows, :] for i in range(3))
            v2, v1, v0 = (prim[f, nr - i, rows, :] for i in (3, 2, 1))
            low.append((face(b0, b1, u0, u1), face(b1, u0, u1, u2)))
            high.append((face(v2, v1, v0, h0), face(v1, v0, h0, h1)))
        p, q = (flux([x[i] for x in low], 0) for i in range(2))
        s, t = (flux([x[i] for x in high], 0) for i in range(2))
        bal = {
            0: [y - x for x, y in zip(p, q)],
            1: [-y for y in q],
            nr - 2: s,
            nr - 1: [y - x for x, y in zip(s, t)],
        }
        w = {0: [], 1: [], nr - 2: [], nr - 1: []}
        for f in range(F):
            g = F + f
            b0, b1, h0, h1 = (before(g, 0, rows), before(g, 1, rows), after(g, 0, rows), after(g, 1, rows))
            w[0].append(b0 - 4.0 * b1)
            w[1].append(b1)
            w[nr - 2].append(h0)
            w[nr - 1].append(h1 - 4.0 * h0)
        return bal, w

    def azimuthal(r, a):
        if a == 0:
            def layer(g, i):
                return jnp.broadcast_to(azi_l[g, r, 2 + i:3 + i, :], (8, nx))

            s = []
            for f in range(F):
                x = prim[f, r, 0:8, :]
                l0, l1 = layer(f, 0), layer(f, 1)
                s.append(
                    face(
                        jnp.where(sub == 0, l0, jnp.where(sub == 1, l1, pltpu.roll(x, 2, 0))),
                        jnp.where(sub == 0, l1, pltpu.roll(x, 1, 0)),
                        x,
                        prim[f, r, 1:9, :],
                    )
                )
            bal = [
                jnp.where(sub == 0, pltpu.roll(x, 7, 0) - x, jnp.where(sub == 1, -x, 0.0))
                for x in flux(s, 1)
            ]
            w = []
            for f in range(F):
                l0, l1 = layer(F + f, 0), layer(F + f, 1)
                w.append(jnp.where(sub == 0, l0 - 4.0 * l1, jnp.where(sub == 1, l1, 0.0)))
            return bal, w

        def layer(g, i):
            return jnp.broadcast_to(azi_r[g, r, i:i + 1, :], (8, nx))

        s = []
        for f in range(F):
            x = prim[f, r, na - 8:na, :]
            h0, h1 = layer(f, 0), layer(f, 1)
            s.append(
                face(
                    prim[f, r, na - 9:na - 1, :],
                    x,
                    jnp.where(sub == 7, h0, pltpu.roll(x, 7, 0)),
                    jnp.where(sub == 7, h1, jnp.where(sub == 6, h0, pltpu.roll(x, 6, 0))),
                )
            )
        bal = [
            jnp.where(sub == 7, x - pltpu.roll(x, 1, 0), jnp.where(sub == 6, x, 0.0)) for x in flux(s, 1)
        ]
        w = []
        for f in range(F):
            h0, h1 = layer(F + f, 0), layer(F + f, 1)
            w.append(jnp.where(sub == 7, h1 - 4.0 * h0, jnp.where(sub == 6, h0, 0.0)))
        return bal, w

    return radial, azimuthal


def main_kernel(dims, n_rad, prim, adj, bw, done, rad_a, rad_b, azi_l, azi_r, row, ind, send):
    nr, na, nx = dims
    tiles = na // 8
    lane = lax.broadcasted_iota(jnp.int32, (8, nx), 1)
    radial, azimuthal = edge_terms(dims, n_rad, prim, adj, rad_a, rad_b, azi_l, azi_r)

    def outer(r, a, extra):
        mine = pl.ds(8 * a, 8)
        bal = [bw[f, r, mine, :] for f in range(F)]
        w = [bw[F + f, r, mine, :] for f in range(F)]
        for more_bal, more_w in extra:
            bal = [x + y for x, y in zip(bal, more_bal)]
            w = [x + y for x, y in zip(w, more_w)]
        total = w[0] * bal[0]
        for f in range(1, F):
            total = total + w[f] * bal[f]
        total = jnp.abs(total) * (1.0 / 144.0)
        ind[r, mine, :] = total
        return total

    ends = (0, 1, nr - 2, nr - 1)
    sums = [jnp.zeros((8, nx), jnp.float32) for _ in range(tiles)]
    for a in range(tiles):
        bal, w = radial(a)
        for r in ends:
            extra = [(bal[r], w[r])]
            if a in (0, tiles - 1):
                extra.append(azimuthal(r, a))
            sums[a] = sums[a] + outer(r, a, extra)

    def plane(r, sums):
        out = []
        for a in range(tiles):
            if a in (0, tiles - 1):
                x = outer(r, a, [azimuthal(r, a)])
            else:
                x = done[r, pl.ds(8 * a, 8), :]
                ind[r, pl.ds(8 * a, 8), :] = x
            out.append(sums[a] + x)
        return tuple(out)

    sums = lax.fori_loop(2, nr - 2, plane, tuple(sums))

    groups = nx // BLK
    halves_a = na // BLK
    per_tile = BLK // 8
    means = jnp.zeros((8, nx), jnp.float32)
    for b in range(halves_a):
        t = sums[b * per_tile]
        for i in range(1, per_tile):
            t = t + sums[b * per_tile + i]
        t = jnp.broadcast_to(jnp.sum(t, axis=0, keepdims=True), (8, nx))
        for sh in (8, 4, 2, 1):
            t = t + pltpu.roll(t, nx - sh, 1)
        t = jnp.take_along_axis(t, (lane % groups) * BLK, axis=1)
        means = jnp.where(lane // groups == b, t, means)
    means = means * (1.0 / BLK**3)
    head = jnp.broadcast_to(row[:, 0:nx], (8, nx))
    head = jnp.where(lane < groups * halves_a, means, head)
    tail = jnp.broadcast_to(row[:, nx:2 * nx], (8, nx))
    both = jnp.where(lax.broadcasted_iota(jnp.int32, (8, nx), 0) & 1 == 0, head, tail)
    for d in range(send.shape[0] // 8):
        send[pl.ds(8 * d, 8), :] = both


def final_kernel(n_loc, per_ax, data, cost, load, means):
    n_dev, nx = data.shape[0] // 2, data.shape[1]
    me = (lax.axis_index("rad") * lax.axis_size("azi") + lax.axis_index("azi")) * lax.axis_size(
        "ax"
    ) + lax.axis_index("ax")
    lane = lax.broadcasted_iota(jnp.int32, (8, nx), 1)
    sub = lax.broadcasted_iota(jnp.int32, (8, nx), 0)
    small = n_dev <= 32
    groups = n_dev // 8
    ok = lane < n_loc

    def rows(g, part):
        return data[pl.ds(16 * g + part, 8, stride=2), :]

    def table(g, carry):
        x = jnp.where(ok, rows(g, 0), 0.0)
        x = pltpu.roll(x, 0, 1, stride=n_loc, stride_axis=0)
        means[g] = jnp.broadcast_to(jnp.sum(x, axis=0, keepdims=True), (8, nx))
        return carry

    lax.fori_loop(0, groups, table, 0, unroll=small)

    def group(g, carry):
        acc_load, acc_cost = carry
        head = rows(g, 0)
        tail = rows(g, 1)
        spot = head.astype(jnp.int32)
        pos = spot & (nx - 1)
        line = spot >> (nx.bit_length() - 1)

        def look(q, acc):
            return jnp.where(line == q, jnp.take_along_axis(means[q], pos, axis=1), acc)

        val = lax.fori_loop(0, groups, look, jnp.zeros((8, nx), jnp.float32), unroll=small)
        beside = None
        for j in range(6):
            x = pltpu.roll(val, nx - n_loc * (1 + j), 1)
            beside = x if beside is None else beside + x
        smooth = 0.5 * head + (0.5 / 6.0) * beside
        refine = pltpu.roll(head, nx - 7 * n_loc, 1)
        owner = tail.astype(jnp.int32)
        weight = pltpu.roll(tail, nx - n_loc, 1)
        home = sub + 8 * g
        c = smooth * (1.0 + 7.0 * refine) + jnp.where(owner != home, 0.25 * weight, 0.0)
        acc_load = acc_load + jnp.where(ok & (owner == me), c, 0.0)
        acc_cost = acc_cost + jnp.where(home == me, c, 0.0)
        return acc_load, acc_cost

    zero = jnp.zeros((8, nx), jnp.float32)
    acc_load, acc_cost = lax.fori_loop(0, groups, group, (zero, zero), unroll=small)
    own = jnp.sum(acc_cost, axis=0, keepdims=True)
    for b in range(n_loc // per_ax):
        x = own if b == 0 else pltpu.roll(own, nx - b * per_ax, 1)
        cost[0, pl.ds(b, 1), :] = x[:, 0:per_ax]
    total = jnp.sum(jnp.sum(acc_load, axis=0, keepdims=True), axis=1, keepdims=True) * (1.0 / n_loc)
    load[0] = total


def on_device(primal, adjoint, refine_flag, owner_map, migrate_weight, neighbor_list):
    _, nr, na, nx = primal.shape
    dims = (nr, na, nx)
    sizes = n_rad, n_azi, n_ax = tuple(lax.axis_size(a) for a in AXES)
    n_dev = n_rad * n_azi * n_ax
    tiles = na // 8
    halves = nr * tiles // (nx // 4)
    f32 = functools.partial(jax.ShapeDtypeStruct, dtype=jnp.float32)
    anyspec = pl.BlockSpec(memory_space=pl.ANY)
    hbm = pl.BlockSpec(memory_space=pltpu.HBM)
    vmem = pl.BlockSpec(memory_space=pltpu.VMEM)

    rad_a, rad_b, azi_s = pl.pallas_call(
        functools.partial(edge_kernel, dims),
        out_shape=(f32((2 * F, 2, na, nx)), f32((2 * F, 2, na, nx)), f32((2 * F, nr, 4, nx))),
        in_specs=[hbm, hbm],
        out_specs=(vmem, vmem, vmem),
        scratch_shapes=[pltpu.SemaphoreType.DMA((2, 4))],
        compiler_params=pltpu.CompilerParams(vmem_limit_bytes=8 << 20),
        name="edges",
    )(*(pltpu.with_memory_space_constraint(x, pltpu.HBM) for x in (primal, adjoint)))
    ax_s = pl.pallas_call(
        functools.partial(lane_kernel, dims),
        out_shape=f32((2 * F, halves, 8, nx)),
        in_specs=[vmem, vmem],
        out_specs=vmem,
        compiler_params=pltpu.CompilerParams(vmem_limit_bytes=16 << 20),
        name="lanes",
    )(primal, adjoint)

    ax_a = lax.ppermute(ax_s, AXES, pair_round(sizes, 2, 0))
    ax_b = lax.ppermute(ax_s, AXES, pair_round(sizes, 2, 1))
    azi_l = lax.ppermute(azi_s, "azi", ring(n_azi, 1))
    azi_r = azi_l if n_azi == 2 else lax.ppermute(azi_s, "azi", ring(n_azi, -1))
    rad_a = lax.ppermute(rad_a, AXES, pair_round(sizes, 0, 0))
    rad_b = lax.ppermute(rad_b, AXES, pair_round(sizes, 0, 1))

    per_rad, per_azi, per_ax = nr // BLK, na // BLK, nx // BLK
    n_loc = per_rad * per_azi * per_ax
    near = neighbor_list.transpose(0, 3, 1, 2)
    cells = F * nr * na
    sums, fourth, row = pl.pallas_call(
        functools.partial(own_kernel, dims, ((per_rad, per_azi, per_ax), (n_azi, n_ax))),
        out_shape=(f32((cells, 2 * nx)), f32((cells, nx)), f32((1, 2 * nx))),
        in_specs=[vmem] * 7,
        out_specs=(vmem, vmem, vmem),
        scratch_shapes=[
            pltpu.VMEM((2 * cells, 3 * nx), jnp.bfloat16),
            pltpu.VMEM((3 * nx, 3 * nx), jnp.bfloat16),
        ],
        compiler_params=pltpu.CompilerParams(vmem_limit_bytes=16 << 20),
        name="own",
    )(primal, adjoint, ax_s, near, refine_flag, owner_map, migrate_weight)
    part_bw = pl.pallas_call(
        functools.partial(inner_kernel, dims),
        out_shape=f32((2 * F, nr, na, nx)),
        in_specs=[vmem] * 3,
        out_specs=vmem,
        scratch_shapes=[
            pltpu.VMEM((F, tiles, 8, nx), jnp.float32),
            pltpu.VMEM((F, 8 + na, nx), jnp.float32),
        ],
        compiler_params=pltpu.CompilerParams(vmem_limit_bytes=16 << 20),
        name="inner",
    )(primal, adjoint, row)
    bw, done = pl.pallas_call(
        functools.partial(axial_kernel, dims, n_ax),
        out_shape=(f32((2 * F, nr, na, nx)), f32(dims)),
        in_specs=[vmem] * 5,
        out_specs=(vmem, vmem),
        scratch_shapes=[
            pltpu.VMEM((3, 2 * F, halves, 8, nx), jnp.float32),
            pltpu.VMEM((2 * cells, nx), jnp.bfloat16),
            pltpu.VMEM((nx, 3 * nx), jnp.bfloat16),
            pltpu.VMEM((cells, 2 * nx), jnp.float32),
            pltpu.VMEM((cells, nx), jnp.float32),
        ],
        compiler_params=pltpu.CompilerParams(vmem_limit_bytes=16 << 20),
        name="axial",
    )(sums, fourth, part_bw, ax_a, ax_b)

    indicator, send = pl.pallas_call(
        functools.partial(main_kernel, dims, n_rad),
        out_shape=(f32(dims), f32((2 * n_dev, nx))),
        in_specs=[vmem] * 9,
        out_specs=(vmem, vmem),
        compiler_params=pltpu.CompilerParams(vmem_limit_bytes=16 << 20),
        name="stencil",
    )(primal, adjoint, bw, done, rad_a, rad_b, azi_l, azi_r, row)

    data = lax.all_to_all(send, AXES, 0, 0, tiled=True)

    cost, load = pl.pallas_call(
        functools.partial(final_kernel, n_loc, per_ax),
        out_shape=(f32((per_rad, per_azi, per_ax)), f32((1, 1, 1))),
        in_specs=[vmem],
        out_specs=(vmem, vmem),
        scratch_shapes=[pltpu.VMEM((n_dev // 8, 8, nx), jnp.float32)],
        compiler_params=pltpu.CompilerParams(vmem_limit_bytes=4 << 20),
        name="blocks",
    )(data)
    return indicator, cost, load


def solution(mesh):
    spec = P("rad", "azi", "ax")
    field = P(None, "rad", "azi", "ax")
    return jax.shard_map(
        on_device,
        mesh=mesh,
        in_specs=(field, field, spec, spec, spec, P("rad", "azi", "ax", None)),
        out_specs=(spec, spec, spec),
        check_vma=False,
    )
```

```python
import functools

import jax
import jax.numpy as jnp
from jax import lax
from jax.experimental import pallas as pl
from jax.experimental.pallas import tpu as pltpu
from jax.sharding import PartitionSpec as P

BLK = 16
F = 5
AXES = ("rad", "azi", "ax")


def pair_round(sizes, along, first):
    n = sizes[along]
    step = [sizes[1] * sizes[2], sizes[2], 1]
    used = range(first, n - 1, 2)
    partner = {i: i + 1 for i in used} | {i + 1: i for i in used}
    idle = [i for i in range(n) if i not in partner]
    if along == 2 and len(idle) == 2:
        partner |= {idle[0]: idle[1], idle[1]: idle[0]}
    pairs = []
    for me in range(sizes[0] * step[0]):
        i = me // step[along] % n
        if i in partner:
            pairs.append((me, me + (partner[i] - i) * step[along]))
        elif along != 2 and sizes[2] % 2 == 0:
            pairs.append((me, me ^ 1))
    return pairs


def ring(count, step):
    return [(i, (i + step) % count) for i in range(count)]


def edge_kernel(dims, prim, adj, rad_a, rad_b, azi_s, sems):
    nr, na, nx = dims
    odd = lax.rem(lax.axis_index("rad"), 2)
    first = jnp.where(odd == 0, nr - 2, 0)
    copies = []
    for t, src in enumerate((prim, adj)):
        rows = pl.ds(t * F, F)
        for i, (a, b) in enumerate(
            (
                (src.at[:, pl.ds(first, 2)], rad_a.at[rows]),
                (src.at[:, pl.ds(nr - 2 - first, 2)], rad_b.at[rows]),
                (src.at[:, :, pl.ds(0, 2)], azi_s.at[rows, :, pl.ds(0, 2)]),
                (src.at[:, :, pl.ds(na - 2, 2)], azi_s.at[rows, :, pl.ds(2, 2)]),
            )
        ):
            copies.append(pltpu.make_async_copy(a, b, sems.at[t, i]))
    for c in copies:
        c.start()
    for c in copies:
        c.wait()


def lane_kernel(dims, prim, adj, ax_s):
    nr, na, nx = dims
    slot = lax.broadcasted_iota(jnp.int32, (8, nx), 1) >> 2
    tiles = na // 8
    per = nx // 4
    for t, src in enumerate((prim, adj)):
        for f in range(F):
            for h in range(nr * tiles // per):
                acc = jnp.zeros((8, nx), jnp.float32)
                for j in range(per):
                    k = h * per + j
                    x = src[f, k // tiles, pl.ds(8 * (k % tiles), 8), :]
                    acc = jnp.where(slot == j, pltpu.roll(x, (4 * j + 2) % nx, 1), acc)
                ax_s[t * F + f, h] = acc


def flux(s, along):
    inv = 1.0 / s[0]
    v = s[1 + along] * inv
    kin = (s[1] * s[1] + s[2] * s[2] + s[3] * s[3]) * inv
    p = 0.4 * s[4] - 0.2 * kin
    out = [s[1 + along], s[1] * v, s[2] * v, s[3] * v, (s[4] + p) * v]
    out[1 + along] = out[1 + along] + p
    return out


def face(m1, c, p1, p2):
    return 7.0 * (c + p1) - (m1 + p2)


def split3(x):
    hi = x.astype(jnp.bfloat16)
    x = x - hi.astype(jnp.float32)
    mid = x.astype(jnp.bfloat16)
    x = x - mid.astype(jnp.float32)
    return hi, mid, x.astype(jnp.bfloat16)


def taps(rows, cols, table):
    out = jnp.zeros(rows.shape, jnp.float32)
    for step, value in table.items():
        out = jnp.where(rows - cols == step, value, out)
    return out


UPPER = {-1: -1.0, 0: 7.0, 1: 7.0, 2: -1.0}
LOWER = {-2: -1.0, -1: 7.0, 0: 7.0, 1: -1.0}
FOURTH = {-2: 1.0, -1: -4.0, 0: 6.0, 1: -4.0, 2: 1.0}


def block_row(grid, near, refine, owner, weight, nx):
    (per_rad, per_azi, per_ax), (n_azi, n_ax) = grid
    n_loc = per_rad * per_azi * per_ax
    blocks_azi, blocks_ax = per_azi * n_azi, per_ax * n_ax
    lane = lax.broadcasted_iota(jnp.int32, (per_azi, nx), 1)

    def place(number):
        b_rad = lax.div(number, blocks_azi * blocks_ax)
        b_azi = lax.rem(lax.div(number, blocks_ax), blocks_azi)
        b_ax = lax.rem(number, blocks_ax)
        device = (lax.div(b_rad, per_rad) * n_azi + lax.div(b_azi, per_azi)) * n_ax + lax.div(b_ax, per_ax)
        local = (lax.rem(b_rad, per_rad) * per_azi + lax.rem(b_azi, per_azi)) * per_ax + lax.rem(b_ax, per_ax)
        return device * n_loc + local

    def spread(x, at):
        x = jnp.concatenate([x, jnp.zeros((per_azi, nx - per_ax), jnp.int32)], axis=1)
        x = jnp.where(lane < per_ax, x, 0).astype(jnp.float32)
        rows = [x[b:b + 1] if at + b * per_ax == 0 else pltpu.roll(x[b:b + 1], at + b * per_ax, 1) for b in range(per_azi)]
        return sum(rows[1:], rows[0])

    head = spread(refine[0], 7 * n_loc)
    for j in range(6):
        head = head + spread(place(near[0, j]), (1 + j) * n_loc)
    tail = spread(owner[0], 0) + spread(weight[0], n_loc)
    return head, tail


def own_kernel(
    dims, grid, prim, adj, ax_s, near, refine, owner, weight, sums, fourth, row, lhs, rhs
):
    del ax_s
    nr, na, nx = dims
    head, tail = block_row(grid, near, refine, owner, weight, nx)
    row[:, 0:nx] = head
    row[:, nx:2 * nx] = tail
    size = nr * na
    i = lax.broadcasted_iota(jnp.int32, (nx, nx), 0)
    c = lax.broadcasted_iota(jnp.int32, (nx, nx), 1)
    for n, table in enumerate((UPPER, LOWER, FOURTH)):
        own = taps(i, c, table).astype(jnp.bfloat16)
        for k in range(3):
            rhs[pl.ds(k * nx, nx), pl.ds(n * nx, nx)] = own

    def build(t, src, f):
        for r in range(nr):
            rows = pl.ds(pl.multiple_of((t * F + f) * size, size) + r * na, na)
            for k, x in enumerate(split3(src[f, r])):
                lhs[rows, pl.ds(k * nx, nx)] = x

    for t, src in enumerate((prim, adj)):
        lax.fori_loop(0, F, lambda f, c, t=t, src=src: (build(t, src, f), c)[1], 0)
    sums[...] = jnp.dot(
        lhs[0:F * size, :], rhs[:, 0:2 * nx], preferred_element_type=jnp.float32
    )
    fourth[...] = jnp.dot(
        lhs[F * size:2 * F * size, :], rhs[:, 2 * nx:3 * nx], preferred_element_type=jnp.float32
    )


def axial_kernel(dims, n_ax, sums, fourth, part_bw, ax_a, ax_b, bw, done, got, lhs, rhs, far, far_w):
    nr, na, nx = dims
    i_ax = lax.axis_index("ax")
    even_ax = lax.rem(i_ax, 2) == 0
    lane = lax.broadcasted_iota(jnp.int32, (8, nx), 1)
    part = lane & 3
    slot = lane >> 2
    tiles = na // 8
    per = nx // 4
    halves = nr * tiles // per
    size = nr * na
    third = per // 3

    i = lax.broadcasted_iota(jnp.int32, (nx, nx), 0) & 3
    c = lax.broadcasted_iota(jnp.int32, (nx, nx), 1)
    cells = jnp.where(i < 2, i - 2, i - 2 + nx)
    for n, table in enumerate((UPPER, LOWER, FOURTH)):
        rhs[:, pl.ds(n * nx, nx)] = taps(cells, c, table).astype(jnp.bfloat16)

    for h in range(halves):
        for f in range(2 * F):
            a, b = ax_a[f, h], ax_b[f, h]
            left = jnp.where(i_ax == 0, 0.0, jnp.where(even_ax, b, a))
            right = jnp.where(i_ax == n_ax - 1, 0.0, jnp.where(even_ax, a, b))
            for k, x in enumerate(split3(jnp.where(part < 2, left, right))):
                x = x.astype(jnp.float32)
                got[k, f, h] = pltpu.roll(x, 4 * third * k, 1) if k else x

    def build(g, carry):
        for r in range(nr):
            h, j0 = r * tiles // per, r * tiles % per
            rows = pl.ds(pl.multiple_of(g * size, size) + r * na, na)
            y = []
            for a in range(tiles):
                x = jnp.zeros((8, nx), jnp.float32)
                for k in range(3):
                    x = jnp.where(slot == (j0 + a + third * k) % per, got[k, g, h], x)
                y.append(x)
            lhs[rows, :] = jnp.concatenate(y, axis=0).astype(jnp.bfloat16)
        return carry

    lax.fori_loop(0, 2 * F, build, 0)
    far[...] = jnp.dot(lhs[0:F * size, :], rhs[:, 0:2 * nx], preferred_element_type=jnp.float32)
    far_w[...] = jnp.dot(
        lhs[F * size:2 * F * size, :], rhs[:, 2 * nx:3 * nx], preferred_element_type=jnp.float32
    )

    def tile(r, a, whole):
        mine = pl.ds(8 * a, 8)
        at = [pl.ds(f * size + r * na + 8 * a, 8) for f in range(F)]
        up = flux([sums[q, 0:nx] + far[q, 0:nx] for q in at], 2)
        low = flux([sums[q, nx:2 * nx] + far[q, nx:2 * nx] for q in at], 2)
        total = None
        for f in range(F):
            bal = part_bw[f, r, mine, :] + (up[f] - low[f])
            w = part_bw[F + f, r, mine, :] + (fourth[at[f], :] + far_w[at[f], :])
            if whole:
                total = w * bal if total is None else total + w * bal
            else:
                bw[f, r, mine, :] = bal
                bw[F + f, r, mine, :] = w
        if whole:
            done[r, mine, :] = jnp.abs(total) * (1.0 / 144.0)

    def body(r, carry):
        for a in range(tiles):
            tile(r, a, 0 < a < tiles - 1)
        return carry

    for r in (0, 1, nr - 2, nr - 1):
        for a in range(tiles):
            tile(r, a, False)
    lax.fori_loop(2, nr - 2, body, 0)


def shifted(src, f, r, a, tiles, da):
    if da < 0 and a == 0 or da > 0 and a == tiles - 1:
        return pltpu.roll(src[f, r, pl.ds(8 * a, 8), :], -da % 8, 0)
    return src[f, r, pl.ds(8 * a + da, 8), :]


def inner_kernel(dims, prim, adj, dep, bw, frad, fazi):
    del dep
    nr, na, nx = dims
    tiles = na // 8
    sub = lax.broadcasted_iota(jnp.int32, (8, nx), 0)
    zero = jnp.zeros((8, nx), jnp.float32)

    def rad_flux(r, a):
        rows = pl.ds(8 * a, 8)
        return flux([face(*(prim[f, r + o, rows, :] for o in (-1, 0, 1, 2))) for f in range(F)], 0)

    def azi_flux(r, a):
        x = flux([face(*(shifted(prim, f, r, a, tiles, o) for o in (-1, 0, 1, 2))) for f in range(F)], 1)
        if a == 0:
            x = [jnp.where(sub < 1, 0.0, t) for t in x]
        if a == tiles - 1:
            x = [jnp.where(sub > 5, 0.0, t) for t in x]
        return x

    for f in range(F):
        fazi[f, 0:8, :] = zero

    def plane(r, carry):
        here = not isinstance(r, int) or 1 <= r <= nr - 3
        before = not isinstance(r, int) or 1 <= r - 1 <= nr - 3
        for a in range(tiles):
            for f, x in enumerate(azi_flux(r, a)):
                fazi[f, pl.ds(8 + 8 * a, 8), :] = x
        for a in range(tiles):
            mine = pl.ds(8 * a, 8)
            up = rad_flux(r, a) if here else None
            for f in range(F):
                bal = fazi[f, pl.ds(8 * a + 8, 8), :] - fazi[f, pl.ds(8 * a + 7, 8), :]
                if before:
                    bal = bal - frad[f, a]
                if here:
                    bal = bal + up[f]
                    frad[f, a] = up[f]
                bw[f, r, mine, :] = bal

                def row(da):
                    x = shifted(adj, f, r, a, tiles, da)
                    if da < 0 and a == 0:
                        x = jnp.where(sub < -da, 0.0, x)
                    if da > 0 and a == tiles - 1:
                        x = jnp.where(sub > 7 - da, 0.0, x)
                    return x

                def layer(dr):
                    if isinstance(r, int) and not 0 <= r + dr < nr:
                        return None
                    return adj[f, r + dr, mine, :]

                two, one = row(-2) + row(2), row(-1) + row(1)
                for dr in (-2, 2):
                    x = layer(dr)
                    two = two if x is None else two + x
                for dr in (-1, 1):
                    x = layer(dr)
                    one = one if x is None else one + x
                bw[F + f, r, mine, :] = two - 4.0 * one + 12.0 * adj[f, r, mine, :]
        return carry

    for r in (0, 1):
        plane(r, 0)
    lax.fori_loop(2, nr - 2, plane, 0)
    for r in (nr - 2, nr - 1):
        plane(r, 0)


def edge_terms(dims, n_rad, prim, adj, rad_a, rad_b, azi_l, azi_r):
    nr, na, nx = dims
    i_rad = lax.axis_index("rad")
    odd = lax.rem(i_rad, 2) == 1
    tiles = na // 8
    sub = lax.broadcasted_iota(jnp.int32, (8, nx), 0)

    def before(g, i, rows):
        return jnp.where(i_rad == 0, 0.0, jnp.where(odd, rad_a[g, i, rows, :], rad_b[g, i, rows, :]))

    def after(g, i, rows):
        x = jnp.where(odd, rad_b[g, i, rows, :], rad_a[g, i, rows, :])
        return jnp.where(i_rad == n_rad - 1, 0.0, x)

    def radial(a):
        rows = pl.ds(8 * a, 8)
        low, high = [], []
        for f in range(F):
            b0, b1, h0, h1 = (before(f, 0, rows), before(f, 1, rows), after(f, 0, rows), after(f, 1, rows))
            u0, u1, u2 = (prim[f, i, rows, :] for i in range(3))
            v2, v1, v0 = (prim[f, nr - i, rows, :] for i in (3, 2, 1))
            low.append((face(b0, b1, u0, u1), face(b1, u0, u1, u2)))
            high.append((face(v2, v1, v0, h0), face(v1, v0, h0, h1)))
        p, q = (flux([x[i] for x in low], 0) for i in range(2))
        s, t = (flux([x[i] for x in high], 0) for i in range(2))
        bal = {
            0: [y - x for x, y in zip(p, q)],
            1: [-y for y in q],
            nr - 2: s,
            nr - 1: [y - x for x, y in zip(s, t)],
        }
        w = {0: [], 1: [], nr - 2: [], nr - 1: []}
        for f in range(F):
            g = F + f
            b0, b1, h0, h1 = (before(g, 0, rows), before(g, 1, rows), after(g, 0, rows), after(g, 1, rows))
            w[0].append(b0 - 4.0 * b1)
            w[1].append(b1)
            w[nr - 2].append(h0)
            w[nr - 1].append(h1 - 4.0 * h0)
        return bal, w

    def azimuthal(r, a):
        if a == 0:
            def layer(g, i):
                return jnp.broadcast_to(azi_l[g, r, 2 + i:3 + i, :], (8, nx))

            s = []
            for f in range(F):
                x = prim[f, r, 0:8, :]
                l0, l1 = layer(f, 0), layer(f, 1)
                s.append(
                    face(
                        jnp.where(sub == 0, l0, jnp.where(sub == 1, l1, pltpu.roll(x, 2, 0))),
                        jnp.where(sub == 0, l1, pltpu.roll(x, 1, 0)),
                        x,
                        prim[f, r, 1:9, :],
                    )
                )
            bal = [
                jnp.where(sub == 0, pltpu.roll(x, 7, 0) - x, jnp.where(sub == 1, -x, 0.0))
                for x in flux(s, 1)
            ]
            w = []
            for f in range(F):
                l0, l1 = layer(F + f, 0), layer(F + f, 1)
                w.append(jnp.where(sub == 0, l0 - 4.0 * l1, jnp.where(sub == 1, l1, 0.0)))
            return bal, w

        def layer(g, i):
            return jnp.broadcast_to(azi_r[g, r, i:i + 1, :], (8, nx))

        s = []
        for f in range(F):
            x = prim[f, r, na - 8:na, :]
            h0, h1 = layer(f, 0), layer(f, 1)
            s.append(
                face(
                    prim[f, r, na - 9:na - 1, :],
                    x,
                    jnp.where(sub == 7, h0, pltpu.roll(x, 7, 0)),
                    jnp.where(sub == 7, h1, jnp.where(sub == 6, h0, pltpu.roll(x, 6, 0))),
                )
            )
        bal = [
            jnp.where(sub == 7, x - pltpu.roll(x, 1, 0), jnp.where(sub == 6, x, 0.0)) for x in flux(s, 1)
        ]
        w = []
        for f in range(F):
            h0, h1 = layer(F + f, 0), layer(F + f, 1)
            w.append(jnp.where(sub == 7, h1 - 4.0 * h0, jnp.where(sub == 6, h0, 0.0)))
        return bal, w

    return radial, azimuthal


def main_kernel(dims, n_rad, prim, adj, bw, done, azi_l, azi_r, rad_a, rad_b, row, ind, send):
    nr, na, nx = dims
    tiles = na // 8
    lane = lax.broadcasted_iota(jnp.int32, (8, nx), 1)
    radial, azimuthal = edge_terms(dims, n_rad, prim, adj, rad_a, rad_b, azi_l, azi_r)

    def outer(r, a, extra):
        mine = pl.ds(8 * a, 8)
        bal = [bw[f, r, mine, :] for f in range(F)]
        w = [bw[F + f, r, mine, :] for f in range(F)]
        for more_bal, more_w in extra:
            bal = [x + y for x, y in zip(bal, more_bal)]
            w = [x + y for x, y in zip(w, more_w)]
        total = w[0] * bal[0]
        for f in range(1, F):
            total = total + w[f] * bal[f]
        total = jnp.abs(total) * (1.0 / 144.0)
        ind[r, mine, :] = total
        return total

    ends = (0, 1, nr - 2, nr - 1)
    sums = [jnp.zeros((8, nx), jnp.float32) for _ in range(tiles)]
    for a in range(tiles):
        bal, w = radial(a)
        for r in ends:
            extra = [(bal[r], w[r])]
            if a in (0, tiles - 1):
                extra.append(azimuthal(r, a))
            sums[a] = sums[a] + outer(r, a, extra)

    def plane(r, sums):
        out = []
        for a in range(tiles):
            if a in (0, tiles - 1):
                x = outer(r, a, [azimuthal(r, a)])
            else:
                x = done[r, pl.ds(8 * a, 8), :]
                ind[r, pl.ds(8 * a, 8), :] = x
            out.append(sums[a] + x)
        return tuple(out)

    sums = lax.fori_loop(2, nr - 2, plane, tuple(sums))

    groups = nx // BLK
    halves_a = na // BLK
    per_tile = BLK // 8
    means = jnp.zeros((8, nx), jnp.float32)
    for b in range(halves_a):
        t = sums[b * per_tile]
        for i in range(1, per_tile):
            t = t + sums[b * per_tile + i]
        t = jnp.broadcast_to(jnp.sum(t, axis=0, keepdims=True), (8, nx))
        for sh in (8, 4, 2, 1):
            t = t + pltpu.roll(t, nx - sh, 1)
        t = jnp.take_along_axis(t, (lane % groups) * BLK, axis=1)
        means = jnp.where(lane // groups == b, t, means)
    means = means * (1.0 / BLK**3)
    head = jnp.broadcast_to(row[:, 0:nx], (8, nx))
    head = jnp.where(lane < groups * halves_a, means, head)
    tail = jnp.broadcast_to(row[:, nx:2 * nx], (8, nx))
    both = jnp.where(lax.broadcasted_iota(jnp.int32, (8, nx), 0) & 1 == 0, head, tail)
    for d in range(send.shape[0] // 8):
        send[pl.ds(8 * d, 8), :] = both


def final_kernel(n_loc, per_ax, data, ind_in, cost_out, load_out, ind, cost, load, means, sems):
    leave = [pltpu.make_async_copy(ind_in, ind, sems.at[0])]
    leave[0].start()
    n_dev, nx = data.shape[0] // 2, data.shape[1]
    me = (lax.axis_index("rad") * lax.axis_size("azi") + lax.axis_index("azi")) * lax.axis_size(
        "ax"
    ) + lax.axis_index("ax")
    lane = lax.broadcasted_iota(jnp.int32, (8, nx), 1)
    sub = lax.broadcasted_iota(jnp.int32, (8, nx), 0)
    small = n_dev <= 32
    groups = n_dev // 8
    ok = lane < n_loc

    def rows(g, part):
        return data[pl.ds(16 * g + part, 8, stride=2), :]

    def table(g, carry):
        x = jnp.where(ok, rows(g, 0), 0.0)
        x = pltpu.roll(x, 0, 1, stride=n_loc, stride_axis=0)
        means[g] = jnp.broadcast_to(jnp.sum(x, axis=0, keepdims=True), (8, nx))
        return carry

    lax.fori_loop(0, groups, table, 0, unroll=small)

    def group(g, carry):
        acc_load, acc_cost = carry
        head = rows(g, 0)
        tail = rows(g, 1)
        spot = head.astype(jnp.int32)
        pos = spot & (nx - 1)
        line = spot >> (nx.bit_length() - 1)

        def look(q, acc):
            return jnp.where(line == q, jnp.take_along_axis(means[q], pos, axis=1), acc)

        val = lax.fori_loop(0, groups, look, jnp.zeros((8, nx), jnp.float32), unroll=small)
        beside = None
        for j in range(6):
            x = pltpu.roll(val, nx - n_loc * (1 + j), 1)
            beside = x if beside is None else beside + x
        smooth = 0.5 * head + (0.5 / 6.0) * beside
        refine = pltpu.roll(head, nx - 7 * n_loc, 1)
        owner = tail.astype(jnp.int32)
        weight = pltpu.roll(tail, nx - n_loc, 1)
        home = sub + 8 * g
        c = smooth * (1.0 + 7.0 * refine) + jnp.where(owner != home, 0.25 * weight, 0.0)
        acc_load = acc_load + jnp.where(ok & (owner == me), c, 0.0)
        acc_cost = acc_cost + jnp.where(home == me, c, 0.0)
        return acc_load, acc_cost

    zero = jnp.zeros((8, nx), jnp.float32)
    acc_load, acc_cost = lax.fori_loop(0, groups, group, (zero, zero), unroll=small)
    own = jnp.sum(acc_cost, axis=0, keepdims=True)
    for b in range(n_loc // per_ax):
        x = own if b == 0 else pltpu.roll(own, nx - b * per_ax, 1)
        cost[0, pl.ds(b, 1), :] = x[:, 0:per_ax]
    total = jnp.sum(jnp.sum(acc_load, axis=0, keepdims=True), axis=1, keepdims=True) * (1.0 / n_loc)
    load[0] = total
    for i, (x, y) in enumerate(((cost, cost_out), (load, load_out))):
        leave.append(pltpu.make_async_copy(x, y, sems.at[1 + i]))
        leave[-1].start()
    for c in leave:
        c.wait()


def on_device(primal, adjoint, refine_flag, owner_map, migrate_weight, neighbor_list):
    _, nr, na, nx = primal.shape
    dims = (nr, na, nx)
    sizes = n_rad, n_azi, n_ax = tuple(lax.axis_size(a) for a in AXES)
    n_dev = n_rad * n_azi * n_ax
    tiles = na // 8
    halves = nr * tiles // (nx // 4)
    f32 = functools.partial(jax.ShapeDtypeStruct, dtype=jnp.float32)
    anyspec = pl.BlockSpec(memory_space=pl.ANY)
    hbm = pl.BlockSpec(memory_space=pltpu.HBM)
    vmem = pl.BlockSpec(memory_space=pltpu.VMEM)

    rad_a, rad_b, azi_s = pl.pallas_call(
        functools.partial(edge_kernel, dims),
        out_shape=(f32((2 * F, 2, na, nx)), f32((2 * F, 2, na, nx)), f32((2 * F, nr, 4, nx))),
        in_specs=[hbm, hbm],
        out_specs=(vmem, vmem, vmem),
        scratch_shapes=[pltpu.SemaphoreType.DMA((2, 4))],
        compiler_params=pltpu.CompilerParams(vmem_limit_bytes=8 << 20),
        name="edges",
    )(*(pltpu.with_memory_space_constraint(x, pltpu.HBM) for x in (primal, adjoint)))
    ax_s = pl.pallas_call(
        functools.partial(lane_kernel, dims),
        out_shape=f32((2 * F, halves, 8, nx)),
        in_specs=[vmem, vmem],
        out_specs=vmem,
        compiler_params=pltpu.CompilerParams(vmem_limit_bytes=16 << 20),
        name="lanes",
    )(primal, adjoint)

    ax_a = lax.ppermute(ax_s, AXES, pair_round(sizes, 2, 0))
    ax_b = lax.ppermute(ax_s, AXES, pair_round(sizes, 2, 1))
    azi_l = lax.ppermute(azi_s, "azi", ring(n_azi, 1))
    azi_r = azi_l if n_azi == 2 else lax.ppermute(azi_s, "azi", ring(n_azi, -1))
    rad_a = lax.ppermute(rad_a, AXES, pair_round(sizes, 0, 0))
    rad_b = lax.ppermute(rad_b, AXES, pair_round(sizes, 0, 1))

    per_rad, per_azi, per_ax = nr // BLK, na // BLK, nx // BLK
    n_loc = per_rad * per_azi * per_ax
    near = neighbor_list.transpose(0, 3, 1, 2)
    cells = F * nr * na
    sums, fourth, row = pl.pallas_call(
        functools.partial(own_kernel, dims, ((per_rad, per_azi, per_ax), (n_azi, n_ax))),
        out_shape=(f32((cells, 2 * nx)), f32((cells, nx)), f32((1, 2 * nx))),
        in_specs=[vmem] * 7,
        out_specs=(vmem, vmem, vmem),
        scratch_shapes=[
            pltpu.VMEM((2 * cells, 3 * nx), jnp.bfloat16),
            pltpu.VMEM((3 * nx, 3 * nx), jnp.bfloat16),
        ],
        compiler_params=pltpu.CompilerParams(vmem_limit_bytes=16 << 20),
        name="own",
    )(primal, adjoint, ax_s, near, refine_flag, owner_map, migrate_weight)
    part_bw = pl.pallas_call(
        functools.partial(inner_kernel, dims),
        out_shape=f32((2 * F, nr, na, nx)),
        in_specs=[vmem] * 3,
        out_specs=vmem,
        scratch_shapes=[
            pltpu.VMEM((F, tiles, 8, nx), jnp.float32),
            pltpu.VMEM((F, 8 + na, nx), jnp.float32),
        ],
        compiler_params=pltpu.CompilerParams(vmem_limit_bytes=16 << 20),
        name="inner",
    )(primal, adjoint, row)
    bw, done = pl.pallas_call(
        functools.partial(axial_kernel, dims, n_ax),
        out_shape=(f32((2 * F, nr, na, nx)), f32(dims)),
        in_specs=[vmem] * 5,
        out_specs=(vmem, vmem),
        scratch_shapes=[
            pltpu.VMEM((3, 2 * F, halves, 8, nx), jnp.float32),
            pltpu.VMEM((2 * cells, nx), jnp.bfloat16),
            pltpu.VMEM((nx, 3 * nx), jnp.bfloat16),
            pltpu.VMEM((cells, 2 * nx), jnp.float32),
            pltpu.VMEM((cells, nx), jnp.float32),
        ],
        compiler_params=pltpu.CompilerParams(vmem_limit_bytes=16 << 20),
        name="axial",
    )(sums, fourth, part_bw, ax_a, ax_b)

    indicator, send = pl.pallas_call(
        functools.partial(main_kernel, dims, n_rad),
        out_shape=(f32(dims), f32((2 * n_dev, nx))),
        in_specs=[vmem] * 9,
        out_specs=(vmem, vmem),
        compiler_params=pltpu.CompilerParams(vmem_limit_bytes=16 << 20),
        name="stencil",
    )(primal, adjoint, bw, done, azi_l, azi_r, rad_a, rad_b, row)

    data = lax.all_to_all(send, AXES, 0, 0, tiled=True)

    cost, load, indicator = pl.pallas_call(
        functools.partial(final_kernel, n_loc, per_ax),
        out_shape=(f32((per_rad, per_azi, per_ax)), f32((1, 1, 1)), f32(dims)),
        in_specs=[vmem, anyspec],
        out_specs=(anyspec,) * 3,
        scratch_shapes=[
            pltpu.VMEM((per_rad, per_azi, per_ax), jnp.float32),
            pltpu.VMEM((1, 1, 1), jnp.float32),
            pltpu.VMEM((n_dev // 8, 8, nx), jnp.float32),
            pltpu.SemaphoreType.DMA((3,)),
        ],
        compiler_params=pltpu.CompilerParams(vmem_limit_bytes=4 << 20),
        name="blocks",
    )(data, indicator)
    return indicator, cost, load


def solution(mesh):
    spec = P("rad", "azi", "ax")
    field = P(None, "rad", "azi", "ax")
    return jax.shard_map(
        on_device,
        mesh=mesh,
        in_specs=(field, field, spec, spec, spec, P("rad", "azi", "ax", None)),
        out_specs=(spec, spec, spec),
        check_vma=False,
    )
```

```python
import functools

import jax
import jax.numpy as jnp
from jax import lax
from jax.experimental import pallas as pl
from jax.experimental.pallas import tpu as pltpu
from jax.sharding import PartitionSpec as P

BLK = 16
F = 5
AXES = ("rad", "azi", "ax")


def pair_round(sizes, along, first):
    n = sizes[along]
    step = [sizes[1] * sizes[2], sizes[2], 1]
    used = range(first, n - 1, 2)
    partner = {i: i + 1 for i in used} | {i + 1: i for i in used}
    idle = [i for i in range(n) if i not in partner]
    if along == 2 and len(idle) == 2:
        partner |= {idle[0]: idle[1], idle[1]: idle[0]}
    pairs = []
    for me in range(sizes[0] * step[0]):
        i = me // step[along] % n
        if i in partner:
            pairs.append((me, me + (partner[i] - i) * step[along]))
        elif along != 2 and sizes[2] % 2 == 0:
            pairs.append((me, me ^ 1))
    return pairs


def ring(count, step):
    return [(i, (i + step) % count) for i in range(count)]


def edge_kernel(dims, prim, adj, rad_a, rad_b, azi_s, sems):
    nr, na, nx = dims
    odd = lax.rem(lax.axis_index("rad"), 2)
    first = jnp.where(odd == 0, nr - 2, 0)
    copies = []
    for t, src in enumerate((prim, adj)):
        rows = pl.ds(t * F, F)
        for i, (a, b) in enumerate(
            (
                (src.at[:, pl.ds(first, 2)], rad_a.at[rows]),
                (src.at[:, pl.ds(nr - 2 - first, 2)], rad_b.at[rows]),
                (src.at[:, :, pl.ds(0, 2)], azi_s.at[rows, :, pl.ds(0, 2)]),
                (src.at[:, :, pl.ds(na - 2, 2)], azi_s.at[rows, :, pl.ds(2, 2)]),
            )
        ):
            copies.append(pltpu.make_async_copy(a, b, sems.at[t, i]))
    for c in copies:
        c.start()
    for c in copies:
        c.wait()


def lane_kernel(dims, prim, adj, first, second):
    nr, na, nx = dims
    even = lax.rem(lax.axis_index("ax"), 2) == 0
    slot = lax.broadcasted_iota(jnp.int32, (8, nx), 1) >> 1
    tiles = na // 8
    per = nx // 2
    for t, src in enumerate((prim, adj)):
        for f in range(F):
            for h in range(nr * tiles // per):
                upper = lower = jnp.zeros((8, nx), jnp.float32)
                for j in range(per):
                    k = h * per + j
                    x = src[f, k // tiles, pl.ds(8 * (k % tiles), 8), :]
                    x = pltpu.roll(x, (2 * j + 2) % nx, 1)
                    upper = jnp.where(slot == j, x, upper)
                    lower = jnp.where(slot == (j + 1) % per, x, lower)
                first[t * F + f, h] = jnp.where(even, upper, lower)
                second[t * F + f, h] = jnp.where(even, lower, upper)


def flux(s, along):
    inv = 1.0 / s[0]
    v = s[1 + along] * inv
    kin = (s[1] * s[1] + s[2] * s[2] + s[3] * s[3]) * inv
    p = 0.4 * s[4] - 0.2 * kin
    out = [s[1 + along], s[1] * v, s[2] * v, s[3] * v, (s[4] + p) * v]
    out[1 + along] = out[1 + along] + p
    return out


def face(m1, c, p1, p2):
    return 7.0 * (c + p1) - (m1 + p2)


def split3(x):
    hi = x.astype(jnp.bfloat16)
    x = x - hi.astype(jnp.float32)
    mid = x.astype(jnp.bfloat16)
    x = x - mid.astype(jnp.float32)
    return hi, mid, x.astype(jnp.bfloat16)


def taps(rows, cols, table):
    out = jnp.zeros(rows.shape, jnp.float32)
    for step, value in table.items():
        out = jnp.where(rows - cols == step, value, out)
    return out


UPPER = {-1: -1.0, 0: 7.0, 1: 7.0, 2: -1.0}
LOWER = {-2: -1.0, -1: 7.0, 0: 7.0, 1: -1.0}
FOURTH = {-2: 1.0, -1: -4.0, 0: 6.0, 1: -4.0, 2: 1.0}


def block_row(grid, near, refine, owner, weight, nx):
    (per_rad, per_azi, per_ax), (n_azi, n_ax) = grid
    n_loc = per_rad * per_azi * per_ax
    blocks_azi, blocks_ax = per_azi * n_azi, per_ax * n_ax
    lane = lax.broadcasted_iota(jnp.int32, (per_azi, nx), 1)

    def place(number):
        b_rad = lax.div(number, blocks_azi * blocks_ax)
        b_azi = lax.rem(lax.div(number, blocks_ax), blocks_azi)
        b_ax = lax.rem(number, blocks_ax)
        device = (lax.div(b_rad, per_rad) * n_azi + lax.div(b_azi, per_azi)) * n_ax + lax.div(b_ax, per_ax)
        local = (lax.rem(b_rad, per_rad) * per_azi + lax.rem(b_azi, per_azi)) * per_ax + lax.rem(b_ax, per_ax)
        return device * n_loc + local

    def spread(x, at):
        x = jnp.concatenate([x, jnp.zeros((per_azi, nx - per_ax), jnp.int32)], axis=1)
        x = jnp.where(lane < per_ax, x, 0).astype(jnp.float32)
        rows = [x[b:b + 1] if at + b * per_ax == 0 else pltpu.roll(x[b:b + 1], at + b * per_ax, 1) for b in range(per_azi)]
        return sum(rows[1:], rows[0])

    head = spread(refine[0], 7 * n_loc)
    for j in range(6):
        head = head + spread(place(near[0, j]), (1 + j) * n_loc)
    tail = spread(owner[0], 0) + spread(weight[0], n_loc)
    return head, tail


PLANES = 4


def place_of(dims, f, r, a):
    _, na, _ = dims
    group = PLANES * na
    if isinstance(r, int):
        return (r // PLANES * F + f) * group + r % PLANES * na + 8 * a
    return pl.multiple_of((lax.div(r, PLANES) * F + f) * group + lax.rem(r, PLANES) * na, na) + 8 * a


def axial_kernel(dims, n_ax, sums, fourth, part_bw, ax_a, ax_b, bw, done, got, lhs, rhs, far, far_w):
    nr, na, nx = dims
    i_ax = lax.axis_index("ax")
    even_ax = lax.rem(i_ax, 2) == 0
    lane = lax.broadcasted_iota(jnp.int32, (8, nx), 1)
    part = lane & 3
    slot = lane >> 2
    tiles = na // 8
    per = nx // 4
    halves = nr * tiles // per
    size = nr * na
    third = per // 3

    i = lax.broadcasted_iota(jnp.int32, (nx, nx), 0) & 3
    c = lax.broadcasted_iota(jnp.int32, (nx, nx), 1)
    cells = jnp.where(i < 2, i - 2, i - 2 + nx)
    for n, table in enumerate((UPPER, LOWER, FOURTH)):
        rhs[:, pl.ds(n * nx, nx)] = taps(cells, c, table).astype(jnp.bfloat16)

    for h in range(halves):
        for f in range(2 * F):
            a, b = ax_a[f, h // 2], ax_b[f, h // 2]
            left = jnp.where(i_ax == 0, 0.0, jnp.where(even_ax, b, a))
            right = jnp.where(i_ax == n_ax - 1, 0.0, jnp.where(even_ax, a, b))
            at = h % 2 * (nx // 2) + 2 * slot + (lane & 1)
            left = jnp.take_along_axis(left, at, axis=1)
            right = jnp.take_along_axis(right, (at + 2) & (nx - 1), axis=1)
            for k, x in enumerate(split3(jnp.where(part < 2, left, right))):
                x = x.astype(jnp.float32)
                got[k, f, h] = pltpu.roll(x, 4 * third * k, 1) if k else x

    def build(g, carry):
        for r in range(nr):
            h, j0 = r * tiles // per, r * tiles % per
            rows = pl.ds(pl.multiple_of(g * size, size) + r * na, na)
            y = []
            for a in range(tiles):
                x = jnp.zeros((8, nx), jnp.float32)
                for k in range(3):
                    x = jnp.where(slot == (j0 + a + third * k) % per, got[k, g, h], x)
                y.append(x)
            lhs[rows, :] = jnp.concatenate(y, axis=0).astype(jnp.bfloat16)
        return carry

    lax.fori_loop(0, 2 * F, build, 0)
    far[...] = jnp.dot(lhs[0:F * size, :], rhs[:, 0:2 * nx], preferred_element_type=jnp.float32)
    far_w[...] = jnp.dot(
        lhs[F * size:2 * F * size, :], rhs[:, 2 * nx:3 * nx], preferred_element_type=jnp.float32
    )

    def tile(r, a, whole):
        mine = pl.ds(8 * a, 8)
        at = [pl.ds(f * size + r * na + 8 * a, 8) for f in range(F)]
        own = [pl.ds(place_of(dims, f, r, a), 8) for f in range(F)]
        up = flux([sums[p, 0:nx] + far[q, 0:nx] for p, q in zip(own, at)], 2)
        low = flux([sums[p, nx:2 * nx] + far[q, nx:2 * nx] for p, q in zip(own, at)], 2)
        total = None
        for f in range(F):
            bal = part_bw[f, r, mine, :] + (up[f] - low[f])
            w = part_bw[F + f, r, mine, :] + (fourth[own[f], :] + far_w[at[f], :])
            if whole:
                total = w * bal if total is None else total + w * bal
            else:
                bw[f, r, mine, :] = bal
                bw[F + f, r, mine, :] = w
        if whole:
            done[r, mine, :] = jnp.abs(total) * (1.0 / 144.0)

    def body(r, carry):
        for a in range(tiles):
            tile(r, a, 0 < a < tiles - 1)
        return carry

    for r in (0, 1, nr - 2, nr - 1):
        for a in range(tiles):
            tile(r, a, False)
    lax.fori_loop(2, nr - 2, body, 0)


def shifted(src, f, r, a, tiles, da):
    if da < 0 and a == 0 or da > 0 and a == tiles - 1:
        return pltpu.roll(src[f, r, pl.ds(8 * a, 8), :], -da % 8, 0)
    return src[f, r, pl.ds(8 * a + da, 8), :]


def inner_kernel(
    dims, grid, prim, adj, ax_s, near, refine, owner, weight, sums, fourth, row, bw, lhs, rhs, frad, fazi
):
    del ax_s
    nr, na, nx = dims
    tiles = na // 8
    sub = lax.broadcasted_iota(jnp.int32, (8, nx), 0)
    zero = jnp.zeros((8, nx), jnp.float32)
    head, tail = block_row(grid, near, refine, owner, weight, nx)
    row[:, 0:nx] = head
    row[:, nx:2 * nx] = tail
    i = lax.broadcasted_iota(jnp.int32, (nx, nx), 0)
    c = lax.broadcasted_iota(jnp.int32, (nx, nx), 1)
    for n, table in enumerate((UPPER, LOWER, FOURTH)):
        own = taps(i, c, table).astype(jnp.bfloat16)
        for k in range(3):
            rhs[pl.ds(k * nx, nx), pl.ds(n * nx, nx)] = own

    def products(group):
        size = PLANES * na
        for t, src in enumerate((prim, adj)):
            for f in range(F):
                for i in range(PLANES):
                    for k, x in enumerate(split3(src[f, group * PLANES + i])):
                        lhs[group, t, pl.ds(f * size + i * na, na), pl.ds(k * nx, nx)] = x
        rows = pl.ds(group * F * size, F * size)
        sums[rows, :] = jnp.dot(lhs[group, 0], rhs[:, 0:2 * nx], preferred_element_type=jnp.float32)
        fourth[rows, :] = jnp.dot(
            lhs[group, 1], rhs[:, 2 * nx:3 * nx], preferred_element_type=jnp.float32
        )

    def rad_flux(r, a):
        rows = pl.ds(8 * a, 8)
        return flux([face(*(prim[f, r + o, rows, :] for o in (-1, 0, 1, 2))) for f in range(F)], 0)

    def azi_flux(r, a):
        x = flux([face(*(shifted(prim, f, r, a, tiles, o) for o in (-1, 0, 1, 2))) for f in range(F)], 1)
        if a == 0:
            x = [jnp.where(sub < 1, 0.0, t) for t in x]
        if a == tiles - 1:
            x = [jnp.where(sub > 5, 0.0, t) for t in x]
        return x

    for f in range(F):
        fazi[f, 0:8, :] = zero

    def plane(r, carry):
        here = not isinstance(r, int) or 1 <= r <= nr - 3
        before = not isinstance(r, int) or 1 <= r - 1 <= nr - 3
        for a in range(tiles):
            for f, x in enumerate(azi_flux(r, a)):
                fazi[f, pl.ds(8 + 8 * a, 8), :] = x
        for a in range(tiles):
            mine = pl.ds(8 * a, 8)
            up = rad_flux(r, a) if here else None
            for f in range(F):
                bal = fazi[f, pl.ds(8 * a + 8, 8), :] - fazi[f, pl.ds(8 * a + 7, 8), :]
                if before:
                    bal = bal - frad[f, a]
                if here:
                    bal = bal + up[f]
                    frad[f, a] = up[f]
                bw[f, r, mine, :] = bal

                def row(da):
                    x = shifted(adj, f, r, a, tiles, da)
                    if da < 0 and a == 0:
                        x = jnp.where(sub < -da, 0.0, x)
                    if da > 0 and a == tiles - 1:
                        x = jnp.where(sub > 7 - da, 0.0, x)
                    return x

                def layer(dr):
                    if isinstance(r, int) and not 0 <= r + dr < nr:
                        return None
                    return adj[f, r + dr, mine, :]

                two, one = row(-2) + row(2), row(-1) + row(1)
                for dr in (-2, 2):
                    x = layer(dr)
                    two = two if x is None else two + x
                for dr in (-1, 1):
                    x = layer(dr)
                    one = one if x is None else one + x
                bw[F + f, r, mine, :] = two - 4.0 * one + 12.0 * adj[f, r, mine, :]
        return carry

    for group in range(nr // PLANES):
        products(group)
        for i in range(PLANES):
            plane(group * PLANES + i, 0)


def radial_terms(dims, n_rad, prim, rad_a, rad_b):
    nr, na, nx = dims
    i_rad = lax.axis_index("rad")
    odd = lax.rem(i_rad, 2) == 1

    def before(g, i, rows):
        return jnp.where(i_rad == 0, 0.0, jnp.where(odd, rad_a[g, i, rows, :], rad_b[g, i, rows, :]))

    def after(g, i, rows):
        x = jnp.where(odd, rad_b[g, i, rows, :], rad_a[g, i, rows, :])
        return jnp.where(i_rad == n_rad - 1, 0.0, x)

    def radial(a):
        rows = pl.ds(8 * a, 8)
        low, high = [], []
        for f in range(F):
            b0, b1, h0, h1 = (before(f, 0, rows), before(f, 1, rows), after(f, 0, rows), after(f, 1, rows))
            u0, u1, u2 = (prim[f, i, rows, :] for i in range(3))
            v2, v1, v0 = (prim[f, nr - i, rows, :] for i in (3, 2, 1))
            low.append((face(b0, b1, u0, u1), face(b1, u0, u1, u2)))
            high.append((face(v2, v1, v0, h0), face(v1, v0, h0, h1)))
        p, q = (flux([x[i] for x in low], 0) for i in range(2))
        s, t = (flux([x[i] for x in high], 0) for i in range(2))
        bal = {
            0: [y - x for x, y in zip(p, q)],
            1: [-y for y in q],
            nr - 2: s,
            nr - 1: [y - x for x, y in zip(s, t)],
        }
        w = {0: [], 1: [], nr - 2: [], nr - 1: []}
        for f in range(F):
            g = F + f
            b0, b1, h0, h1 = (before(g, 0, rows), before(g, 1, rows), after(g, 0, rows), after(g, 1, rows))
            w[0].append(b0 - 4.0 * b1)
            w[1].append(b1)
            w[nr - 2].append(h0)
            w[nr - 1].append(h1 - 4.0 * h0)
        return bal, w

    return radial


def azimuthal_terms(dims, prim, azi_l, azi_r):
    na, nx = dims[1:]
    sub = lax.broadcasted_iota(jnp.int32, (8, nx), 0)

    def azimuthal(r, a):
        if a == 0:
            def layer(g, i):
                return jnp.broadcast_to(azi_l[g, r, 2 + i:3 + i, :], (8, nx))

            s = []
            for f in range(F):
                x = prim[f, r, 0:8, :]
                l0, l1 = layer(f, 0), layer(f, 1)
                s.append(
                    face(
                        jnp.where(sub == 0, l0, jnp.where(sub == 1, l1, pltpu.roll(x, 2, 0))),
                        jnp.where(sub == 0, l1, pltpu.roll(x, 1, 0)),
                        x,
                        prim[f, r, 1:9, :],
                    )
                )
            bal = [
                jnp.where(sub == 0, pltpu.roll(x, 7, 0) - x, jnp.where(sub == 1, -x, 0.0))
                for x in flux(s, 1)
            ]
            w = []
            for f in range(F):
                l0, l1 = layer(F + f, 0), layer(F + f, 1)
                w.append(jnp.where(sub == 0, l0 - 4.0 * l1, jnp.where(sub == 1, l1, 0.0)))
            return bal, w

        def layer(g, i):
            return jnp.broadcast_to(azi_r[g, r, i:i + 1, :], (8, nx))

        s = []
        for f in range(F):
            x = prim[f, r, na - 8:na, :]
            h0, h1 = layer(f, 0), layer(f, 1)
            s.append(
                face(
                    prim[f, r, na - 9:na - 1, :],
                    x,
                    jnp.where(sub == 7, h0, pltpu.roll(x, 7, 0)),
                    jnp.where(sub == 7, h1, jnp.where(sub == 6, h0, pltpu.roll(x, 6, 0))),
                )
            )
        bal = [
            jnp.where(sub == 7, x - pltpu.roll(x, 1, 0), jnp.where(sub == 6, x, 0.0)) for x in flux(s, 1)
        ]
        w = []
        for f in range(F):
            h0, h1 = layer(F + f, 0), layer(F + f, 1)
            w.append(jnp.where(sub == 7, h1 - 4.0 * h0, jnp.where(sub == 6, h0, 0.0)))
        return bal, w

    return azimuthal


def indicator_of(bal, w):
    total = w[0] * bal[0]
    for f in range(1, F):
        total = total + w[f] * bal[f]
    return jnp.abs(total) * (1.0 / 144.0)


def rows_kernel(dims, prim, bw, done, azi_l, azi_r, ind, ends, part_sums):
    nr, na, nx = dims
    tiles = na // 8
    azimuthal = azimuthal_terms(dims, prim, azi_l, azi_r)

    def outer(r, a):
        mine = pl.ds(8 * a, 8)
        more_bal, more_w = azimuthal(r, a)
        bal = [bw[f, r, mine, :] + more_bal[f] for f in range(F)]
        return bal, [bw[F + f, r, mine, :] + more_w[f] for f in range(F)]

    for i, r in enumerate((0, 1, nr - 2, nr - 1)):
        for a in range(tiles):
            mine = pl.ds(8 * a, 8)
            if a in (0, tiles - 1):
                bal, w = outer(r, a)
                for f in range(F):
                    ends[f, i, mine, :] = bal[f]
                    ends[F + f, i, mine, :] = w[f]
            else:
                for g in range(2 * F):
                    ends[g, i, mine, :] = bw[g, r, mine, :]

    def plane(r, sums):
        out = []
        for a in range(tiles):
            mine = pl.ds(8 * a, 8)
            x = indicator_of(*outer(r, a)) if a in (0, tiles - 1) else done[r, mine, :]
            ind[r, mine, :] = x
            out.append(sums[a] + x)
        return tuple(out)

    zero = jnp.zeros((8, nx), jnp.float32)
    sums = lax.fori_loop(2, nr - 2, plane, (zero,) * tiles)
    for a in range(tiles):
        part_sums[a] = sums[a]


def main_kernel(dims, n_rad, prim, ends, part_sums, rad_a, rad_b, row, ind, send):
    nr, na, nx = dims
    tiles = na // 8
    lane = lax.broadcasted_iota(jnp.int32, (8, nx), 1)
    radial = radial_terms(dims, n_rad, prim, rad_a, rad_b)
    sums = []
    for a in range(tiles):
        mine = pl.ds(8 * a, 8)
        more_bal, more_w = radial(a)
        t = part_sums[a]
        for i, r in enumerate((0, 1, nr - 2, nr - 1)):
            bal = [ends[f, i, mine, :] + more_bal[r][f] for f in range(F)]
            w = [ends[F + f, i, mine, :] + more_w[r][f] for f in range(F)]
            x = indicator_of(bal, w)
            ind[i, mine, :] = x
            t = t + x
        sums.append(t)

    groups = nx // BLK
    halves_a = na // BLK
    per_tile = BLK // 8
    means = jnp.zeros((8, nx), jnp.float32)
    for b in range(halves_a):
        t = sums[b * per_tile]
        for i in range(1, per_tile):
            t = t + sums[b * per_tile + i]
        t = jnp.broadcast_to(jnp.sum(t, axis=0, keepdims=True), (8, nx))
        for sh in (8, 4, 2, 1):
            t = t + pltpu.roll(t, nx - sh, 1)
        t = jnp.take_along_axis(t, (lane % groups) * BLK, axis=1)
        means = jnp.where(lane // groups == b, t, means)
    means = means * (1.0 / BLK**3)
    head = jnp.broadcast_to(row[:, 0:nx], (8, nx))
    head = jnp.where(lane < groups * halves_a, means, head)
    tail = jnp.broadcast_to(row[:, nx:2 * nx], (8, nx))
    both = jnp.where(lax.broadcasted_iota(jnp.int32, (8, nx), 0) & 1 == 0, head, tail)
    for d in range(send.shape[0] // 8):
        send[pl.ds(8 * d, 8), :] = both


def final_kernel(n_loc, per_ax, data, inside, outside, cost_out, load_out, ind, cost, load, means, sems):
    nr = ind.shape[0]
    inner = pl.ds(2, nr - 4)
    leave = [
        pltpu.make_async_copy(inside.at[inner], ind.at[inner], sems.at[0]),
        pltpu.make_async_copy(outside.at[pl.ds(0, 2)], ind.at[pl.ds(0, 2)], sems.at[1]),
        pltpu.make_async_copy(outside.at[pl.ds(2, 2)], ind.at[pl.ds(nr - 2, 2)], sems.at[2]),
    ]
    for c in leave:
        c.start()
    n_dev, nx = data.shape[0] // 2, data.shape[1]
    me = (lax.axis_index("rad") * lax.axis_size("azi") + lax.axis_index("azi")) * lax.axis_size(
        "ax"
    ) + lax.axis_index("ax")
    lane = lax.broadcasted_iota(jnp.int32, (8, nx), 1)
    sub = lax.broadcasted_iota(jnp.int32, (8, nx), 0)
    small = n_dev <= 32
    groups = n_dev // 8
    ok = lane < n_loc

    def rows(g, part):
        return data[pl.ds(16 * g + part, 8, stride=2), :]

    def table(g, carry):
        x = jnp.where(ok, rows(g, 0), 0.0)
        x = pltpu.roll(x, 0, 1, stride=n_loc, stride_axis=0)
        means[g] = jnp.broadcast_to(jnp.sum(x, axis=0, keepdims=True), (8, nx))
        return carry

    lax.fori_loop(0, groups, table, 0, unroll=small)

    def group(g, carry):
        acc_load, acc_cost = carry
        head = rows(g, 0)
        tail = rows(g, 1)
        spot = head.astype(jnp.int32)
        pos = spot & (nx - 1)
        line = spot >> (nx.bit_length() - 1)

        def look(q, acc):
            return jnp.where(line == q, jnp.take_along_axis(means[q], pos, axis=1), acc)

        val = lax.fori_loop(0, groups, look, jnp.zeros((8, nx), jnp.float32), unroll=small)
        beside = None
        for j in range(6):
            x = pltpu.roll(val, nx - n_loc * (1 + j), 1)
            beside = x if beside is None else beside + x
        smooth = 0.5 * head + (0.5 / 6.0) * beside
        refine = pltpu.roll(head, nx - 7 * n_loc, 1)
        owner = tail.astype(jnp.int32)
        weight = pltpu.roll(tail, nx - n_loc, 1)
        home = sub + 8 * g
        c = smooth * (1.0 + 7.0 * refine) + jnp.where(owner != home, 0.25 * weight, 0.0)
        acc_load = acc_load + jnp.where(ok & (owner == me), c, 0.0)
        acc_cost = acc_cost + jnp.where(home == me, c, 0.0)
        return acc_load, acc_cost

    zero = jnp.zeros((8, nx), jnp.float32)
    acc_load, acc_cost = lax.fori_loop(0, groups, group, (zero, zero), unroll=small)
    own = jnp.sum(acc_cost, axis=0, keepdims=True)
    for b in range(n_loc // per_ax):
        x = own if b == 0 else pltpu.roll(own, nx - b * per_ax, 1)
        cost[0, pl.ds(b, 1), :] = x[:, 0:per_ax]
    total = jnp.sum(jnp.sum(acc_load, axis=0, keepdims=True), axis=1, keepdims=True) * (1.0 / n_loc)
    load[0] = total
    for i, (x, y) in enumerate(((cost, cost_out), (load, load_out))):
        leave.append(pltpu.make_async_copy(x, y, sems.at[3 + i]))
        leave[-1].start()
    for c in leave:
        c.wait()


def on_device(primal, adjoint, refine_flag, owner_map, migrate_weight, neighbor_list):
    _, nr, na, nx = primal.shape
    dims = (nr, na, nx)
    sizes = n_rad, n_azi, n_ax = tuple(lax.axis_size(a) for a in AXES)
    n_dev = n_rad * n_azi * n_ax
    tiles = na // 8
    halves = nr * tiles // (nx // 4)
    f32 = functools.partial(jax.ShapeDtypeStruct, dtype=jnp.float32)
    anyspec = pl.BlockSpec(memory_space=pl.ANY)
    hbm = pl.BlockSpec(memory_space=pltpu.HBM)
    vmem = pl.BlockSpec(memory_space=pltpu.VMEM)

    rad_a, rad_b, azi_s = pl.pallas_call(
        functools.partial(edge_kernel, dims),
        out_shape=(f32((2 * F, 2, na, nx)), f32((2 * F, 2, na, nx)), f32((2 * F, nr, 4, nx))),
        in_specs=[hbm, hbm],
        out_specs=(vmem, vmem, vmem),
        scratch_shapes=[pltpu.SemaphoreType.DMA((2, 4))],
        compiler_params=pltpu.CompilerParams(vmem_limit_bytes=8 << 20),
        name="edges",
    )(*(pltpu.with_memory_space_constraint(x, pltpu.HBM) for x in (primal, adjoint)))
    ax_first, ax_second = pl.pallas_call(
        functools.partial(lane_kernel, dims),
        out_shape=(f32((2 * F, halves // 2, 8, nx)),) * 2,
        in_specs=[vmem, vmem],
        out_specs=(vmem, vmem),
        compiler_params=pltpu.CompilerParams(vmem_limit_bytes=16 << 20),
        name="lanes",
    )(primal, adjoint)

    ax_a = lax.ppermute(ax_first, AXES, pair_round(sizes, 2, 0))
    ax_b = lax.ppermute(ax_second, AXES, pair_round(sizes, 2, 1))
    azi_l = lax.ppermute(azi_s, "azi", ring(n_azi, 1))
    azi_r = azi_l if n_azi == 2 else lax.ppermute(azi_s, "azi", ring(n_azi, -1))
    rad_a = lax.ppermute(rad_a, AXES, pair_round(sizes, 0, 0))
    rad_b = lax.ppermute(rad_b, AXES, pair_round(sizes, 0, 1))

    per_rad, per_azi, per_ax = nr // BLK, na // BLK, nx // BLK
    n_loc = per_rad * per_azi * per_ax
    near = neighbor_list.transpose(0, 3, 1, 2)
    cells = F * nr * na
    sums, fourth, row, part_bw = pl.pallas_call(
        functools.partial(inner_kernel, dims, ((per_rad, per_azi, per_ax), (n_azi, n_ax))),
        out_shape=(
            f32((cells, 2 * nx)),
            f32((cells, nx)),
            f32((1, 2 * nx)),
            f32((2 * F, nr, na, nx)),
        ),
        in_specs=[vmem] * 7,
        out_specs=(vmem,) * 4,
        scratch_shapes=[
            pltpu.VMEM((nr // PLANES, 2, F * PLANES * na, 3 * nx), jnp.bfloat16),
            pltpu.VMEM((3 * nx, 3 * nx), jnp.bfloat16),
            pltpu.VMEM((F, tiles, 8, nx), jnp.float32),
            pltpu.VMEM((F, 8 + na, nx), jnp.float32),
        ],
        compiler_params=pltpu.CompilerParams(vmem_limit_bytes=16 << 20),
        name="inner",
    )(primal, adjoint, ax_first, near, refine_flag, owner_map, migrate_weight)
    bw, done = pl.pallas_call(
        functools.partial(axial_kernel, dims, n_ax),
        out_shape=(f32((2 * F, nr, na, nx)), f32(dims)),
        in_specs=[vmem] * 5,
        out_specs=(vmem, vmem),
        scratch_shapes=[
            pltpu.VMEM((3, 2 * F, halves, 8, nx), jnp.float32),
            pltpu.VMEM((2 * cells, nx), jnp.bfloat16),
            pltpu.VMEM((nx, 3 * nx), jnp.bfloat16),
            pltpu.VMEM((cells, 2 * nx), jnp.float32),
            pltpu.VMEM((cells, nx), jnp.float32),
        ],
        compiler_params=pltpu.CompilerParams(vmem_limit_bytes=16 << 20),
        name="axial",
    )(sums, fourth, part_bw, ax_a, ax_b)

    inside, ends, part_sums = pl.pallas_call(
        functools.partial(rows_kernel, dims),
        out_shape=(f32(dims), f32((2 * F, 4, na, nx)), f32((tiles, 8, nx))),
        in_specs=[vmem] * 5,
        out_specs=(vmem,) * 3,
        compiler_params=pltpu.CompilerParams(vmem_limit_bytes=16 << 20),
        name="rows",
    )(primal, bw, done, azi_l, azi_r)
    outside, send = pl.pallas_call(
        functools.partial(main_kernel, dims, n_rad),
        out_shape=(f32((4, na, nx)), f32((2 * n_dev, nx))),
        in_specs=[vmem] * 6,
        out_specs=(vmem, vmem),
        compiler_params=pltpu.CompilerParams(vmem_limit_bytes=16 << 20),
        name="planes",
    )(primal, ends, part_sums, rad_a, rad_b, row)

    data = lax.all_to_all(send, AXES, 0, 0, tiled=True)

    cost, load, indicator = pl.pallas_call(
        functools.partial(final_kernel, n_loc, per_ax),
        out_shape=(f32((per_rad, per_azi, per_ax)), f32((1, 1, 1)), f32(dims)),
        in_specs=[vmem, anyspec, anyspec],
        out_specs=(anyspec,) * 3,
        scratch_shapes=[
            pltpu.VMEM((per_rad, per_azi, per_ax), jnp.float32),
            pltpu.VMEM((1, 1, 1), jnp.float32),
            pltpu.VMEM((n_dev // 8, 8, nx), jnp.float32),
            pltpu.SemaphoreType.DMA((5,)),
        ],
        compiler_params=pltpu.CompilerParams(vmem_limit_bytes=4 << 20),
        name="blocks",
    )(data, inside, outside)
    return indicator, cost, load


def solution(mesh):
    spec = P("rad", "azi", "ax")
    field = P(None, "rad", "azi", "ax")
    return jax.shard_map(
        on_device,
        mesh=mesh,
        in_specs=(field, field, spec, spec, spec, P("rad", "azi", "ax", None)),
        out_specs=(spec, spec, spec),
        check_vma=False,
    )
```

```python
import functools

import jax
import jax.numpy as jnp
from jax import lax
from jax.experimental import pallas as pl
from jax.experimental.pallas import tpu as pltpu
from jax.sharding import PartitionSpec as P

BLK = 16
F = 5
AXES = ("rad", "azi", "ax")


def pair_round(sizes, along, first):
    n = sizes[along]
    step = [sizes[1] * sizes[2], sizes[2], 1]
    used = range(first, n - 1, 2)
    partner = {i: i + 1 for i in used} | {i + 1: i for i in used}
    idle = [i for i in range(n) if i not in partner]
    if along == 2 and len(idle) == 2:
        partner |= {idle[0]: idle[1], idle[1]: idle[0]}
    pairs = []
    for me in range(sizes[0] * step[0]):
        i = me // step[along] % n
        if i in partner:
            pairs.append((me, me + (partner[i] - i) * step[along]))
        elif along != 2 and sizes[2] % 2 == 0:
            pairs.append((me, me ^ 1))
    return pairs


def ring(count, step):
    return [(i, (i + step) % count) for i in range(count)]


def edge_kernel(dims, prim, adj, rad_a, rad_b, azi_s, sems):
    nr, na, nx = dims
    odd = lax.rem(lax.axis_index("rad"), 2)
    first = jnp.where(odd == 0, nr - 2, 0)
    copies = []
    for t, src in enumerate((prim, adj)):
        rows = pl.ds(t * F, F)
        for i, (a, b) in enumerate(
            (
                (src.at[:, pl.ds(first, 2)], rad_a.at[rows]),
                (src.at[:, pl.ds(nr - 2 - first, 2)], rad_b.at[rows]),
                (src.at[:, :, pl.ds(0, 2)], azi_s.at[rows, :, pl.ds(0, 2)]),
                (src.at[:, :, pl.ds(na - 2, 2)], azi_s.at[rows, :, pl.ds(2, 2)]),
            )
        ):
            copies.append(pltpu.make_async_copy(a, b, sems.at[t, i]))
    for c in copies:
        c.start()
    for c in copies:
        c.wait()


def lane_kernel(dims, prim, adj, first, second):
    nr, na, nx = dims
    even = lax.rem(lax.axis_index("ax"), 2) == 0
    slot = lax.broadcasted_iota(jnp.int32, (8, nx), 1) >> 1
    tiles = na // 8
    per = nx // 2
    for t, src in enumerate((prim, adj)):
        for f in range(F):
            for h in range(nr * tiles // per):
                upper = lower = jnp.zeros((8, nx), jnp.float32)
                for j in range(per):
                    k = h * per + j
                    x = src[f, k // tiles, pl.ds(8 * (k % tiles), 8), :]
                    x = pltpu.roll(x, (2 * j + 2) % nx, 1)
                    upper = jnp.where(slot == j, x, upper)
                    lower = jnp.where(slot == (j + 1) % per, x, lower)
                first[t * F + f, h] = jnp.where(even, upper, lower)
                second[t * F + f, h] = jnp.where(even, lower, upper)


def flux(s, along):
    inv = 1.0 / s[0]
    v = s[1 + along] * inv
    kin = (s[1] * s[1] + s[2] * s[2] + s[3] * s[3]) * inv
    p = 0.4 * s[4] - 0.2 * kin
    out = [s[1 + along], s[1] * v, s[2] * v, s[3] * v, (s[4] + p) * v]
    out[1 + along] = out[1 + along] + p
    return out


def face(m1, c, p1, p2):
    return 7.0 * (c + p1) - (m1 + p2)


def split3(x):
    hi = x.astype(jnp.bfloat16)
    x = x - hi.astype(jnp.float32)
    mid = x.astype(jnp.bfloat16)
    x = x - mid.astype(jnp.float32)
    return hi, mid, x.astype(jnp.bfloat16)


def taps(rows, cols, table):
    out = jnp.zeros(rows.shape, jnp.float32)
    for step, value in table.items():
        out = jnp.where(rows - cols == step, value, out)
    return out


UPPER = {-1: -1.0, 0: 7.0, 1: 7.0, 2: -1.0}
LOWER = {-2: -1.0, -1: 7.0, 0: 7.0, 1: -1.0}
FOURTH = {-2: 1.0, -1: -4.0, 0: 6.0, 1: -4.0, 2: 1.0}


def block_row(grid, near, refine, owner, weight, nx):
    (per_rad, per_azi, per_ax), (n_azi, n_ax) = grid
    n_loc = per_rad * per_azi * per_ax
    blocks_azi, blocks_ax = per_azi * n_azi, per_ax * n_ax
    lane = lax.broadcasted_iota(jnp.int32, (per_azi, nx), 1)

    def place(number):
        b_rad = lax.div(number, blocks_azi * blocks_ax)
        b_azi = lax.rem(lax.div(number, blocks_ax), blocks_azi)
        b_ax = lax.rem(number, blocks_ax)
        device = (lax.div(b_rad, per_rad) * n_azi + lax.div(b_azi, per_azi)) * n_ax + lax.div(b_ax, per_ax)
        local = (lax.rem(b_rad, per_rad) * per_azi + lax.rem(b_azi, per_azi)) * per_ax + lax.rem(b_ax, per_ax)
        return device * n_loc + local

    def spread(x, at):
        x = jnp.concatenate([x, jnp.zeros((per_azi, nx - per_ax), jnp.int32)], axis=1)
        x = jnp.where(lane < per_ax, x, 0).astype(jnp.float32)
        rows = [x[b:b + 1] if at + b * per_ax == 0 else pltpu.roll(x[b:b + 1], at + b * per_ax, 1) for b in range(per_azi)]
        return sum(rows[1:], rows[0])

    head = spread(refine[0], 7 * n_loc)
    for j in range(6):
        head = head + spread(place(near[0, j]), (1 + j) * n_loc)
    tail = spread(owner[0], 0) + spread(weight[0], n_loc)
    return head, tail


PLANES = 4


def place_of(dims, f, r, a):
    _, na, _ = dims
    group = PLANES * na
    if isinstance(r, int):
        return (r // PLANES * F + f) * group + r % PLANES * na + 8 * a
    return pl.multiple_of((lax.div(r, PLANES) * F + f) * group + lax.rem(r, PLANES) * na, na) + 8 * a


def axial_kernel(dims, n_ax, sums, fourth, part_bw, ax_a, ax_b, bw, done, got, lhs, rhs, far, far_w):
    nr, na, nx = dims
    i_ax = lax.axis_index("ax")
    even_ax = lax.rem(i_ax, 2) == 0
    lane = lax.broadcasted_iota(jnp.int32, (8, nx), 1)
    part = lane & 3
    slot = lane >> 2
    tiles = na // 8
    per = nx // 4
    halves = nr * tiles // per
    size = nr * na
    third = per // 3

    i = lax.broadcasted_iota(jnp.int32, (nx, nx), 0) & 3
    c = lax.broadcasted_iota(jnp.int32, (nx, nx), 1)
    cells = jnp.where(i < 2, i - 2, i - 2 + nx)
    for n, table in enumerate((UPPER, LOWER, FOURTH)):
        rhs[:, pl.ds(n * nx, nx)] = taps(cells, c, table).astype(jnp.bfloat16)

    for h in range(halves):
        for f in range(2 * F):
            a, b = ax_a[f, h // 2], ax_b[f, h // 2]
            left = jnp.where(i_ax == 0, 0.0, jnp.where(even_ax, b, a))
            right = jnp.where(i_ax == n_ax - 1, 0.0, jnp.where(even_ax, a, b))
            at = h % 2 * (nx // 2) + 2 * slot + (lane & 1)
            left = jnp.take_along_axis(left, at, axis=1)
            right = jnp.take_along_axis(right, (at + 2) & (nx - 1), axis=1)
            for k, x in enumerate(split3(jnp.where(part < 2, left, right))):
                x = x.astype(jnp.float32)
                got[k, f, h] = pltpu.roll(x, 4 * third * k, 1) if k else x

    def build(g, carry):
        for r in range(nr):
            h, j0 = r * tiles // per, r * tiles % per
            rows = pl.ds(pl.multiple_of(g * size, size) + r * na, na)
            y = []
            for a in range(tiles):
                x = jnp.zeros((8, nx), jnp.float32)
                for k in range(3):
                    x = jnp.where(slot == (j0 + a + third * k) % per, got[k, g, h], x)
                y.append(x)
            lhs[rows, :] = jnp.concatenate(y, axis=0).astype(jnp.bfloat16)
        return carry

    lax.fori_loop(0, 2 * F, build, 0)
    far[...] = jnp.dot(lhs[0:F * size, :], rhs[:, 0:2 * nx], preferred_element_type=jnp.float32)
    far_w[...] = jnp.dot(
        lhs[F * size:2 * F * size, :], rhs[:, 2 * nx:3 * nx], preferred_element_type=jnp.float32
    )

    def tile(r, a, whole):
        mine = pl.ds(8 * a, 8)
        at = [pl.ds(f * size + r * na + 8 * a, 8) for f in range(F)]
        own = [pl.ds(place_of(dims, f, r, a), 8) for f in range(F)]
        up = flux([sums[p, 0:nx] + far[q, 0:nx] for p, q in zip(own, at)], 2)
        low = flux([sums[p, nx:2 * nx] + far[q, nx:2 * nx] for p, q in zip(own, at)], 2)
        total = None
        for f in range(F):
            bal = part_bw[f, r, mine, :] + (up[f] - low[f])
            w = part_bw[F + f, r, mine, :] + (fourth[own[f], :] + far_w[at[f], :])
            if whole:
                total = w * bal if total is None else total + w * bal
            else:
                bw[f, r, mine, :] = bal
                bw[F + f, r, mine, :] = w
        if whole:
            done[r, mine, :] = jnp.abs(total) * (1.0 / 144.0)

    def body(r, carry):
        for a in range(tiles):
            tile(r, a, 0 < a < tiles - 1)
        return carry

    for r in (0, 1, nr - 2, nr - 1):
        for a in range(tiles):
            tile(r, a, False)
    lax.fori_loop(2, nr - 2, body, 0, unroll=True)


def shifted(src, f, r, a, tiles, da):
    if da < 0 and a == 0 or da > 0 and a == tiles - 1:
        return pltpu.roll(src[f, r, pl.ds(8 * a, 8), :], -da % 8, 0)
    return src[f, r, pl.ds(8 * a + da, 8), :]


def inner_kernel(
    dims, grid, prim, adj, ax_s, near, refine, owner, weight, sums, fourth, row, bw, lhs, rhs, frad, fazi
):
    del ax_s
    nr, na, nx = dims
    tiles = na // 8
    sub = lax.broadcasted_iota(jnp.int32, (8, nx), 0)
    zero = jnp.zeros((8, nx), jnp.float32)
    head, tail = block_row(grid, near, refine, owner, weight, nx)
    row[:, 0:nx] = head
    row[:, nx:2 * nx] = tail
    i = lax.broadcasted_iota(jnp.int32, (nx, nx), 0)
    c = lax.broadcasted_iota(jnp.int32, (nx, nx), 1)
    for n, table in enumerate((UPPER, LOWER, FOURTH)):
        own = taps(i, c, table).astype(jnp.bfloat16)
        for k in range(3):
            rhs[pl.ds(k * nx, nx), pl.ds(n * nx, nx)] = own

    def products(group):
        size = PLANES * na
        for t, src in enumerate((prim, adj)):
            for f in range(F):
                for i in range(PLANES):
                    for k, x in enumerate(split3(src[f, group * PLANES + i])):
                        lhs[group, t, pl.ds(f * size + i * na, na), pl.ds(k * nx, nx)] = x
        rows = pl.ds(group * F * size, F * size)
        sums[rows, :] = jnp.dot(lhs[group, 0], rhs[:, 0:2 * nx], preferred_element_type=jnp.float32)
        fourth[rows, :] = jnp.dot(
            lhs[group, 1], rhs[:, 2 * nx:3 * nx], preferred_element_type=jnp.float32
        )

    def rad_flux(r, a):
        rows = pl.ds(8 * a, 8)
        return flux([face(*(prim[f, r + o, rows, :] for o in (-1, 0, 1, 2))) for f in range(F)], 0)

    def azi_flux(r, a):
        x = flux([face(*(shifted(prim, f, r, a, tiles, o) for o in (-1, 0, 1, 2))) for f in range(F)], 1)
        if a == 0:
            x = [jnp.where(sub < 1, 0.0, t) for t in x]
        if a == tiles - 1:
            x = [jnp.where(sub > 5, 0.0, t) for t in x]
        return x

    for f in range(F):
        fazi[f, 0:8, :] = zero

    def plane(r, carry):
        here = not isinstance(r, int) or 1 <= r <= nr - 3
        before = not isinstance(r, int) or 1 <= r - 1 <= nr - 3
        for a in range(tiles):
            for f, x in enumerate(azi_flux(r, a)):
                fazi[f, pl.ds(8 + 8 * a, 8), :] = x
        for a in range(tiles):
            mine = pl.ds(8 * a, 8)
            up = rad_flux(r, a) if here else None
            for f in range(F):
                bal = fazi[f, pl.ds(8 * a + 8, 8), :] - fazi[f, pl.ds(8 * a + 7, 8), :]
                if before:
                    bal = bal - frad[f, a]
                if here:
                    bal = bal + up[f]
                    frad[f, a] = up[f]
                bw[f, r, mine, :] = bal

                def row(da):
                    x = shifted(adj, f, r, a, tiles, da)
                    if da < 0 and a == 0:
                        x = jnp.where(sub < -da, 0.0, x)
                    if da > 0 and a == tiles - 1:
                        x = jnp.where(sub > 7 - da, 0.0, x)
                    return x

                def layer(dr):
                    if isinstance(r, int) and not 0 <= r + dr < nr:
                        return None
                    return adj[f, r + dr, mine, :]

                two, one = row(-2) + row(2), row(-1) + row(1)
                for dr in (-2, 2):
                    x = layer(dr)
                    two = two if x is None else two + x
                for dr in (-1, 1):
                    x = layer(dr)
                    one = one if x is None else one + x
                bw[F + f, r, mine, :] = two - 4.0 * one + 12.0 * adj[f, r, mine, :]
        return carry

    for group in range(nr // PLANES):
        products(group)
        for i in range(PLANES):
            plane(group * PLANES + i, 0)


def radial_terms(dims, n_rad, prim, rad_a, rad_b):
    nr, na, nx = dims
    i_rad = lax.axis_index("rad")
    odd = lax.rem(i_rad, 2) == 1

    def before(g, i, rows):
        return jnp.where(i_rad == 0, 0.0, jnp.where(odd, rad_a[g, i, rows, :], rad_b[g, i, rows, :]))

    def after(g, i, rows):
        x = jnp.where(odd, rad_b[g, i, rows, :], rad_a[g, i, rows, :])
        return jnp.where(i_rad == n_rad - 1, 0.0, x)

    def radial(a):
        rows = pl.ds(8 * a, 8)
        low, high = [], []
        for f in range(F):
            b0, b1, h0, h1 = (before(f, 0, rows), before(f, 1, rows), after(f, 0, rows), after(f, 1, rows))
            u0, u1, u2 = (prim[f, i, rows, :] for i in range(3))
            v2, v1, v0 = (prim[f, nr - i, rows, :] for i in (3, 2, 1))
            low.append((face(b0, b1, u0, u1), face(b1, u0, u1, u2)))
            high.append((face(v2, v1, v0, h0), face(v1, v0, h0, h1)))
        p, q = (flux([x[i] for x in low], 0) for i in range(2))
        s, t = (flux([x[i] for x in high], 0) for i in range(2))
        bal = {
            0: [y - x for x, y in zip(p, q)],
            1: [-y for y in q],
            nr - 2: s,
            nr - 1: [y - x for x, y in zip(s, t)],
        }
        w = {0: [], 1: [], nr - 2: [], nr - 1: []}
        for f in range(F):
            g = F + f
            b0, b1, h0, h1 = (before(g, 0, rows), before(g, 1, rows), after(g, 0, rows), after(g, 1, rows))
            w[0].append(b0 - 4.0 * b1)
            w[1].append(b1)
            w[nr - 2].append(h0)
            w[nr - 1].append(h1 - 4.0 * h0)
        return bal, w

    return radial


def azimuthal_terms(dims, prim, azi_l, azi_r):
    na, nx = dims[1:]
    sub = lax.broadcasted_iota(jnp.int32, (8, nx), 0)

    def azimuthal(r, a):
        if a == 0:
            def layer(g, i):
                return jnp.broadcast_to(azi_l[g, r, 2 + i:3 + i, :], (8, nx))

            s = []
            for f in range(F):
                x = prim[f, r, 0:8, :]
                l0, l1 = layer(f, 0), layer(f, 1)
                s.append(
                    face(
                        jnp.where(sub == 0, l0, jnp.where(sub == 1, l1, pltpu.roll(x, 2, 0))),
                        jnp.where(sub == 0, l1, pltpu.roll(x, 1, 0)),
                        x,
                        prim[f, r, 1:9, :],
                    )
                )
            bal = [
                jnp.where(sub == 0, pltpu.roll(x, 7, 0) - x, jnp.where(sub == 1, -x, 0.0))
                for x in flux(s, 1)
            ]
            w = []
            for f in range(F):
                l0, l1 = layer(F + f, 0), layer(F + f, 1)
                w.append(jnp.where(sub == 0, l0 - 4.0 * l1, jnp.where(sub == 1, l1, 0.0)))
            return bal, w

        def layer(g, i):
            return jnp.broadcast_to(azi_r[g, r, i:i + 1, :], (8, nx))

        s = []
        for f in range(F):
            x = prim[f, r, na - 8:na, :]
            h0, h1 = layer(f, 0), layer(f, 1)
            s.append(
                face(
                    prim[f, r, na - 9:na - 1, :],
                    x,
                    jnp.where(sub == 7, h0, pltpu.roll(x, 7, 0)),
                    jnp.where(sub == 7, h1, jnp.where(sub == 6, h0, pltpu.roll(x, 6, 0))),
                )
            )
        bal = [
            jnp.where(sub == 7, x - pltpu.roll(x, 1, 0), jnp.where(sub == 6, x, 0.0)) for x in flux(s, 1)
        ]
        w = []
        for f in range(F):
            h0, h1 = layer(F + f, 0), layer(F + f, 1)
            w.append(jnp.where(sub == 7, h1 - 4.0 * h0, jnp.where(sub == 6, h0, 0.0)))
        return bal, w

    return azimuthal


def indicator_of(bal, w):
    total = w[0] * bal[0]
    for f in range(1, F):
        total = total + w[f] * bal[f]
    return jnp.abs(total) * (1.0 / 144.0)


def rows_kernel(dims, prim, bw, done, azi_l, azi_r, ind, ends, part_sums):
    nr, na, nx = dims
    tiles = na // 8
    azimuthal = azimuthal_terms(dims, prim, azi_l, azi_r)

    def outer(r, a):
        mine = pl.ds(8 * a, 8)
        more_bal, more_w = azimuthal(r, a)
        bal = [bw[f, r, mine, :] + more_bal[f] for f in range(F)]
        return bal, [bw[F + f, r, mine, :] + more_w[f] for f in range(F)]

    for i, r in enumerate((0, 1, nr - 2, nr - 1)):
        for a in range(tiles):
            mine = pl.ds(8 * a, 8)
            if a in (0, tiles - 1):
                bal, w = outer(r, a)
                for f in range(F):
                    ends[f, i, mine, :] = bal[f]
                    ends[F + f, i, mine, :] = w[f]
            else:
                for g in range(2 * F):
                    ends[g, i, mine, :] = bw[g, r, mine, :]

    def plane(r, sums):
        out = []
        for a in range(tiles):
            mine = pl.ds(8 * a, 8)
            x = indicator_of(*outer(r, a)) if a in (0, tiles - 1) else done[r, mine, :]
            ind[r, mine, :] = x
            out.append(sums[a] + x)
        return tuple(out)

    zero = jnp.zeros((8, nx), jnp.float32)
    sums = lax.fori_loop(2, nr - 2, plane, (zero,) * tiles, unroll=True)
    for a in range(tiles):
        part_sums[a] = sums[a]


def main_kernel(dims, n_rad, prim, ends, part_sums, rad_a, rad_b, row, ind, send):
    nr, na, nx = dims
    tiles = na // 8
    lane = lax.broadcasted_iota(jnp.int32, (8, nx), 1)
    radial = radial_terms(dims, n_rad, prim, rad_a, rad_b)
    sums = []
    for a in range(tiles):
        mine = pl.ds(8 * a, 8)
        more_bal, more_w = radial(a)
        t = part_sums[a]
        for i, r in enumerate((0, 1, nr - 2, nr - 1)):
            bal = [ends[f, i, mine, :] + more_bal[r][f] for f in range(F)]
            w = [ends[F + f, i, mine, :] + more_w[r][f] for f in range(F)]
            x = indicator_of(bal, w)
            ind[i, mine, :] = x
            t = t + x
        sums.append(t)

    groups = nx // BLK
    halves_a = na // BLK
    per_tile = BLK // 8
    i = lax.broadcasted_iota(jnp.int32, (nx, nx), 0)
    c = lax.broadcasted_iota(jnp.int32, (nx, nx), 1)
    gather = jnp.where(i // BLK == c % groups, 1.0, 0.0)
    rows = []
    for b in range(halves_a):
        t = sums[b * per_tile]
        for i in range(1, per_tile):
            t = t + sums[b * per_tile + i]
        rows.append(t)
    rows = jnp.dot(
        jnp.concatenate(rows, axis=0),
        gather,
        precision=lax.Precision.HIGHEST,
        preferred_element_type=jnp.float32,
    )
    means = jnp.zeros((8, nx), jnp.float32)
    for b in range(halves_a):
        t = jnp.sum(rows[8 * b:8 * b + 8], axis=0, keepdims=True)
        means = jnp.where(lane // groups == b, jnp.broadcast_to(t, (8, nx)), means)
    means = means * (1.0 / BLK**3)
    head = jnp.broadcast_to(row[:, 0:nx], (8, nx))
    head = jnp.where(lane < groups * halves_a, means, head)
    tail = jnp.broadcast_to(row[:, nx:2 * nx], (8, nx))
    both = jnp.where(lax.broadcasted_iota(jnp.int32, (8, nx), 0) & 1 == 0, head, tail)
    for d in range(send.shape[0] // 8):
        send[pl.ds(8 * d, 8), :] = both


def final_kernel(n_loc, per_ax, data, inside, outside, cost_out, load_out, ind, cost, load, means, sems):
    nr = ind.shape[0]
    inner = pl.ds(2, nr - 4)
    leave = [
        pltpu.make_async_copy(inside.at[inner], ind.at[inner], sems.at[0]),
        pltpu.make_async_copy(outside.at[pl.ds(0, 2)], ind.at[pl.ds(0, 2)], sems.at[1]),
        pltpu.make_async_copy(outside.at[pl.ds(2, 2)], ind.at[pl.ds(nr - 2, 2)], sems.at[2]),
    ]
    for c in leave:
        c.start()
    n_dev, nx = data.shape[0] // 2, data.shape[1]
    me = (lax.axis_index("rad") * lax.axis_size("azi") + lax.axis_index("azi")) * lax.axis_size(
        "ax"
    ) + lax.axis_index("ax")
    lane = lax.broadcasted_iota(jnp.int32, (8, nx), 1)
    sub = lax.broadcasted_iota(jnp.int32, (8, nx), 0)
    small = n_dev <= 32
    groups = n_dev // 8
    ok = lane < n_loc

    def rows(g, part):
        return data[pl.ds(16 * g + part, 8, stride=2), :]

    def table(g, carry):
        x = jnp.where(ok, rows(g, 0), 0.0)
        x = pltpu.roll(x, 0, 1, stride=n_loc, stride_axis=0)
        means[g] = jnp.broadcast_to(jnp.sum(x, axis=0, keepdims=True), (8, nx))
        return carry

    lax.fori_loop(0, groups, table, 0, unroll=small)

    def group(g, carry):
        acc_load, acc_cost = carry
        head = rows(g, 0)
        tail = rows(g, 1)
        spot = head.astype(jnp.int32)
        pos = spot & (nx - 1)
        line = spot >> (nx.bit_length() - 1)

        def look(q, acc):
            return jnp.where(line == q, jnp.take_along_axis(means[q], pos, axis=1), acc)

        val = lax.fori_loop(0, groups, look, jnp.zeros((8, nx), jnp.float32), unroll=small)
        beside = None
        for j in range(6):
            x = pltpu.roll(val, nx - n_loc * (1 + j), 1)
            beside = x if beside is None else beside + x
        smooth = 0.5 * head + (0.5 / 6.0) * beside
        refine = pltpu.roll(head, nx - 7 * n_loc, 1)
        owner = tail.astype(jnp.int32)
        weight = pltpu.roll(tail, nx - n_loc, 1)
        home = sub + 8 * g
        c = smooth * (1.0 + 7.0 * refine) + jnp.where(owner != home, 0.25 * weight, 0.0)
        acc_load = acc_load + jnp.where(ok & (owner == me), c, 0.0)
        acc_cost = acc_cost + jnp.where(home == me, c, 0.0)
        return acc_load, acc_cost

    zero = jnp.zeros((8, nx), jnp.float32)
    acc_load, acc_cost = lax.fori_loop(0, groups, group, (zero, zero), unroll=small)
    own = jnp.sum(acc_cost, axis=0, keepdims=True)
    for b in range(n_loc // per_ax):
        x = own if b == 0 else pltpu.roll(own, nx - b * per_ax, 1)
        cost[0, pl.ds(b, 1), :] = x[:, 0:per_ax]
    total = jnp.sum(jnp.sum(acc_load, axis=0, keepdims=True), axis=1, keepdims=True) * (1.0 / n_loc)
    load[0] = total
    for i, (x, y) in enumerate(((cost, cost_out), (load, load_out))):
        leave.append(pltpu.make_async_copy(x, y, sems.at[3 + i]))
        leave[-1].start()
    for c in leave:
        c.wait()


def on_device(primal, adjoint, refine_flag, owner_map, migrate_weight, neighbor_list):
    _, nr, na, nx = primal.shape
    dims = (nr, na, nx)
    sizes = n_rad, n_azi, n_ax = tuple(lax.axis_size(a) for a in AXES)
    n_dev = n_rad * n_azi * n_ax
    tiles = na // 8
    halves = nr * tiles // (nx // 4)
    f32 = functools.partial(jax.ShapeDtypeStruct, dtype=jnp.float32)
    anyspec = pl.BlockSpec(memory_space=pl.ANY)
    hbm = pl.BlockSpec(memory_space=pltpu.HBM)
    vmem = pl.BlockSpec(memory_space=pltpu.VMEM)

    rad_a, rad_b, azi_s = pl.pallas_call(
        functools.partial(edge_kernel, dims),
        out_shape=(f32((2 * F, 2, na, nx)), f32((2 * F, 2, na, nx)), f32((2 * F, nr, 4, nx))),
        in_specs=[hbm, hbm],
        out_specs=(vmem, vmem, vmem),
        scratch_shapes=[pltpu.SemaphoreType.DMA((2, 4))],
        compiler_params=pltpu.CompilerParams(vmem_limit_bytes=8 << 20),
        name="edges",
    )(*(pltpu.with_memory_space_constraint(x, pltpu.HBM) for x in (primal, adjoint)))
    ax_first, ax_second = pl.pallas_call(
        functools.partial(lane_kernel, dims),
        out_shape=(f32((2 * F, halves // 2, 8, nx)),) * 2,
        in_specs=[vmem, vmem],
        out_specs=(vmem, vmem),
        compiler_params=pltpu.CompilerParams(vmem_limit_bytes=16 << 20),
        name="lanes",
    )(primal, adjoint)

    ax_a = lax.ppermute(ax_first, AXES, pair_round(sizes, 2, 0))
    ax_b = lax.ppermute(ax_second, AXES, pair_round(sizes, 2, 1))
    azi_l = lax.ppermute(azi_s, "azi", ring(n_azi, 1))
    azi_r = azi_l if n_azi == 2 else lax.ppermute(azi_s, "azi", ring(n_azi, -1))
    rad_a = lax.ppermute(rad_a, AXES, pair_round(sizes, 0, 0))
    rad_b = lax.ppermute(rad_b, AXES, pair_round(sizes, 0, 1))

    per_rad, per_azi, per_ax = nr // BLK, na // BLK, nx // BLK
    n_loc = per_rad * per_azi * per_ax
    near = neighbor_list.transpose(0, 3, 1, 2)
    cells = F * nr * na
    sums, fourth, row, part_bw = pl.pallas_call(
        functools.partial(inner_kernel, dims, ((per_rad, per_azi, per_ax), (n_azi, n_ax))),
        out_shape=(
            f32((cells, 2 * nx)),
            f32((cells, nx)),
            f32((1, 2 * nx)),
            f32((2 * F, nr, na, nx)),
        ),
        in_specs=[vmem] * 7,
        out_specs=(vmem,) * 4,
        scratch_shapes=[
            pltpu.VMEM((nr // PLANES, 2, F * PLANES * na, 3 * nx), jnp.bfloat16),
            pltpu.VMEM((3 * nx, 3 * nx), jnp.bfloat16),
            pltpu.VMEM((F, tiles, 8, nx), jnp.float32),
            pltpu.VMEM((F, 8 + na, nx), jnp.float32),
        ],
        compiler_params=pltpu.CompilerParams(vmem_limit_bytes=16 << 20),
        name="inner",
    )(primal, adjoint, ax_first, near, refine_flag, owner_map, migrate_weight)
    bw, done = pl.pallas_call(
        functools.partial(axial_kernel, dims, n_ax),
        out_shape=(f32((2 * F, nr, na, nx)), f32(dims)),
        in_specs=[vmem] * 5,
        out_specs=(vmem, vmem),
        scratch_shapes=[
            pltpu.VMEM((3, 2 * F, halves, 8, nx), jnp.float32),
            pltpu.VMEM((2 * cells, nx), jnp.bfloat16),
            pltpu.VMEM((nx, 3 * nx), jnp.bfloat16),
            pltpu.VMEM((cells, 2 * nx), jnp.float32),
            pltpu.VMEM((cells, nx), jnp.float32),
        ],
        compiler_params=pltpu.CompilerParams(vmem_limit_bytes=16 << 20),
        name="axial",
    )(sums, fourth, part_bw, ax_a, ax_b)

    inside, ends, part_sums = pl.pallas_call(
        functools.partial(rows_kernel, dims),
        out_shape=(f32(dims), f32((2 * F, 4, na, nx)), f32((tiles, 8, nx))),
        in_specs=[vmem] * 5,
        out_specs=(vmem,) * 3,
        compiler_params=pltpu.CompilerParams(vmem_limit_bytes=16 << 20),
        name="rows",
    )(primal, bw, done, azi_l, azi_r)
    outside, send = pl.pallas_call(
        functools.partial(main_kernel, dims, n_rad),
        out_shape=(f32((4, na, nx)), f32((2 * n_dev, nx))),
        in_specs=[vmem] * 6,
        out_specs=(vmem, vmem),
        compiler_params=pltpu.CompilerParams(vmem_limit_bytes=16 << 20),
        name="planes",
    )(primal, ends, part_sums, rad_a, rad_b, row)

    data = lax.all_to_all(send, AXES, 0, 0, tiled=True)

    cost, load, indicator = pl.pallas_call(
        functools.partial(final_kernel, n_loc, per_ax),
        out_shape=(f32((per_rad, per_azi, per_ax)), f32((1, 1, 1)), f32(dims)),
        in_specs=[vmem, anyspec, anyspec],
        out_specs=(anyspec,) * 3,
        scratch_shapes=[
            pltpu.VMEM((per_rad, per_azi, per_ax), jnp.float32),
            pltpu.VMEM((1, 1, 1), jnp.float32),
            pltpu.VMEM((n_dev // 8, 8, nx), jnp.float32),
            pltpu.SemaphoreType.DMA((5,)),
        ],
        compiler_params=pltpu.CompilerParams(vmem_limit_bytes=4 << 20),
        name="blocks",
    )(data, inside, outside)
    return indicator, cost, load


def solution(mesh):
    spec = P("rad", "azi", "ax")
    field = P(None, "rad", "azi", "ax")
    return jax.shard_map(
        on_device,
        mesh=mesh,
        in_specs=(field, field, spec, spec, spec, P("rad", "azi", "ax", None)),
        out_specs=(spec, spec, spec),
        check_vma=False,
    )
```

```python
import functools

import jax
import jax.numpy as jnp
from jax import lax
from jax.experimental import pallas as pl
from jax.experimental.pallas import tpu as pltpu
from jax.sharding import PartitionSpec as P

BLK = 16
F = 5
AXES = ("rad", "azi", "ax")


def pair_round(sizes, along, first):
    n = sizes[along]
    step = [sizes[1] * sizes[2], sizes[2], 1]
    used = range(first, n - 1, 2)
    partner = {i: i + 1 for i in used} | {i + 1: i for i in used}
    idle = [i for i in range(n) if i not in partner]
    if along == 2 and len(idle) == 2:
        partner |= {idle[0]: idle[1], idle[1]: idle[0]}
    pairs = []
    for me in range(sizes[0] * step[0]):
        i = me // step[along] % n
        if i in partner:
            pairs.append((me, me + (partner[i] - i) * step[along]))
        elif along != 2 and sizes[2] % 2 == 0:
            pairs.append((me, me ^ 1))
    return pairs


def ring(count, step):
    return [(i, (i + step) % count) for i in range(count)]


def edge_kernel(dims, prim, adj, rad_a, rad_b, azi_s, sems):
    nr, na, nx = dims
    odd = lax.rem(lax.axis_index("rad"), 2)
    first = jnp.where(odd == 0, nr - 2, 0)
    copies = []
    for t, src in enumerate((prim, adj)):
        rows = pl.ds(t * F, F)
        for i, (a, b) in enumerate(
            (
                (src.at[:, pl.ds(first, 2)], rad_a.at[rows]),
                (src.at[:, pl.ds(nr - 2 - first, 2)], rad_b.at[rows]),
                (src.at[:, :, pl.ds(0, 2)], azi_s.at[rows, :, pl.ds(0, 2)]),
                (src.at[:, :, pl.ds(na - 2, 2)], azi_s.at[rows, :, pl.ds(2, 2)]),
            )
        ):
            copies.append(pltpu.make_async_copy(a, b, sems.at[t, i]))
    for c in copies:
        c.start()
    for c in copies:
        c.wait()


def lane_kernel(dims, prim_in, adj_in, dep, prim, adj, first, second, sems):
    nr, na, nx = dims
    del dep
    loads = {}
    for t, (src, dst) in enumerate(((prim_in, prim), (adj_in, adj))):
        for f in range(F):
            loads[t, f] = pltpu.make_async_copy(src.at[f], dst.at[f], sems.at[t, f])
            loads[t, f].start()
    even = lax.rem(lax.axis_index("ax"), 2) == 0
    slot = lax.broadcasted_iota(jnp.int32, (8, nx), 1) >> 1
    tiles = na // 8
    per = nx // 2
    for t, src in enumerate((prim, adj)):
        for f in range(F):
            loads[t, f].wait()
            for h in range(nr * tiles // per):
                upper = lower = jnp.zeros((8, nx), jnp.float32)
                for j in range(per):
                    k = h * per + j
                    x = src[f, k // tiles, pl.ds(8 * (k % tiles), 8), :]
                    x = pltpu.roll(x, (2 * j + 2) % nx, 1)
                    upper = jnp.where(slot == j, x, upper)
                    lower = jnp.where(slot == (j + 1) % per, x, lower)
                first[t * F + f, h] = jnp.where(even, upper, lower)
                second[t * F + f, h] = jnp.where(even, lower, upper)


def flux(s, along):
    inv = 1.0 / s[0]
    v = s[1 + along] * inv
    kin = (s[1] * s[1] + s[2] * s[2] + s[3] * s[3]) * inv
    p = 0.4 * s[4] - 0.2 * kin
    out = [s[1 + along], s[1] * v, s[2] * v, s[3] * v, (s[4] + p) * v]
    out[1 + along] = out[1 + along] + p
    return out


def face(m1, c, p1, p2):
    return 7.0 * (c + p1) - (m1 + p2)


def split3(x):
    hi = x.astype(jnp.bfloat16)
    x = x - hi.astype(jnp.float32)
    mid = x.astype(jnp.bfloat16)
    x = x - mid.astype(jnp.float32)
    return hi, mid, x.astype(jnp.bfloat16)


def taps(rows, cols, table):
    out = jnp.zeros(rows.shape, jnp.float32)
    for step, value in table.items():
        out = jnp.where(rows - cols == step, value, out)
    return out


UPPER = {-1: -1.0, 0: 7.0, 1: 7.0, 2: -1.0}
LOWER = {-2: -1.0, -1: 7.0, 0: 7.0, 1: -1.0}
FOURTH = {-2: 1.0, -1: -4.0, 0: 6.0, 1: -4.0, 2: 1.0}


def block_row(grid, near, refine, owner, weight, nx):
    (per_rad, per_azi, per_ax), (n_azi, n_ax) = grid
    n_loc = per_rad * per_azi * per_ax
    blocks_azi, blocks_ax = per_azi * n_azi, per_ax * n_ax
    lane = lax.broadcasted_iota(jnp.int32, (per_azi, nx), 1)

    def place(number):
        b_rad = lax.div(number, blocks_azi * blocks_ax)
        b_azi = lax.rem(lax.div(number, blocks_ax), blocks_azi)
        b_ax = lax.rem(number, blocks_ax)
        device = (lax.div(b_rad, per_rad) * n_azi + lax.div(b_azi, per_azi)) * n_ax + lax.div(b_ax, per_ax)
        local = (lax.rem(b_rad, per_rad) * per_azi + lax.rem(b_azi, per_azi)) * per_ax + lax.rem(b_ax, per_ax)
        return device * n_loc + local

    def spread(x, at):
        x = jnp.concatenate([x, jnp.zeros((per_azi, nx - per_ax), jnp.int32)], axis=1)
        x = jnp.where(lane < per_ax, x, 0).astype(jnp.float32)
        rows = [x[b:b + 1] if at + b * per_ax == 0 else pltpu.roll(x[b:b + 1], at + b * per_ax, 1) for b in range(per_azi)]
        return sum(rows[1:], rows[0])

    head = spread(refine[0], 7 * n_loc)
    for j in range(6):
        head = head + spread(place(near[0, j]), (1 + j) * n_loc)
    tail = spread(owner[0], 0) + spread(weight[0], n_loc)
    return head, tail


PLANES = 4


def place_of(dims, f, r, a):
    _, na, _ = dims
    group = PLANES * na
    if isinstance(r, int):
        return (r // PLANES * F + f) * group + r % PLANES * na + 8 * a
    return pl.multiple_of((lax.div(r, PLANES) * F + f) * group + lax.rem(r, PLANES) * na, na) + 8 * a


def axial_kernel(dims, n_ax, sums, fourth, part_bw, ax_a, ax_b, bw, done, got, lhs, rhs, far, far_w):
    nr, na, nx = dims
    i_ax = lax.axis_index("ax")
    even_ax = lax.rem(i_ax, 2) == 0
    lane = lax.broadcasted_iota(jnp.int32, (8, nx), 1)
    part = lane & 3
    slot = lane >> 2
    tiles = na // 8
    per = nx // 4
    halves = nr * tiles // per
    size = nr * na
    third = per // 3

    i = lax.broadcasted_iota(jnp.int32, (nx, nx), 0) & 3
    c = lax.broadcasted_iota(jnp.int32, (nx, nx), 1)
    cells = jnp.where(i < 2, i - 2, i - 2 + nx)
    for n, table in enumerate((UPPER, LOWER, FOURTH)):
        rhs[:, pl.ds(n * nx, nx)] = taps(cells, c, table).astype(jnp.bfloat16)

    for h in range(halves):
        for f in range(2 * F):
            a, b = ax_a[f, h // 2], ax_b[f, h // 2]
            left = jnp.where(i_ax == 0, 0.0, jnp.where(even_ax, b, a))
            right = jnp.where(i_ax == n_ax - 1, 0.0, jnp.where(even_ax, a, b))
            at = h % 2 * (nx // 2) + 2 * slot + (lane & 1)
            left = jnp.take_along_axis(left, at, axis=1)
            right = jnp.take_along_axis(right, (at + 2) & (nx - 1), axis=1)
            for k, x in enumerate(split3(jnp.where(part < 2, left, right))):
                x = x.astype(jnp.float32)
                got[k, f, h] = pltpu.roll(x, 4 * third * k, 1) if k else x

    def build(g, carry):
        for r in range(nr):
            h, j0 = r * tiles // per, r * tiles % per
            rows = pl.ds(pl.multiple_of(g * size, size) + r * na, na)
            y = []
            for a in range(tiles):
                x = jnp.zeros((8, nx), jnp.float32)
                for k in range(3):
                    x = jnp.where(slot == (j0 + a + third * k) % per, got[k, g, h], x)
                y.append(x)
            lhs[rows, :] = jnp.concatenate(y, axis=0).astype(jnp.bfloat16)
        return carry

    lax.fori_loop(0, 2 * F, build, 0)
    far[...] = jnp.dot(lhs[0:F * size, :], rhs[:, 0:2 * nx], preferred_element_type=jnp.float32)
    far_w[...] = jnp.dot(
        lhs[F * size:2 * F * size, :], rhs[:, 2 * nx:3 * nx], preferred_element_type=jnp.float32
    )

    def tile(r, a, whole):
        mine = pl.ds(8 * a, 8)
        at = [pl.ds(f * size + r * na + 8 * a, 8) for f in range(F)]
        own = [pl.ds(place_of(dims, f, r, a), 8) for f in range(F)]
        up = flux([sums[p, 0:nx] + far[q, 0:nx] for p, q in zip(own, at)], 2)
        low = flux([sums[p, nx:2 * nx] + far[q, nx:2 * nx] for p, q in zip(own, at)], 2)
        total = None
        for f in range(F):
            bal = part_bw[f, r, mine, :] + (up[f] - low[f])
            w = part_bw[F + f, r, mine, :] + (fourth[own[f], :] + far_w[at[f], :])
            if whole:
                total = w * bal if total is None else total + w * bal
            else:
                bw[f, r, mine, :] = bal
                bw[F + f, r, mine, :] = w
        if whole:
            done[r, mine, :] = jnp.abs(total) * (1.0 / 144.0)

    def body(r, carry):
        for a in range(tiles):
            tile(r, a, 0 < a < tiles - 1)
        return carry

    for r in (0, 1, nr - 2, nr - 1):
        for a in range(tiles):
            tile(r, a, False)
    lax.fori_loop(2, nr - 2, body, 0, unroll=True)


def shifted(src, f, r, a, tiles, da):
    if da < 0 and a == 0 or da > 0 and a == tiles - 1:
        return pltpu.roll(src[f, r, pl.ds(8 * a, 8), :], -da % 8, 0)
    return src[f, r, pl.ds(8 * a + da, 8), :]


def inner_kernel(
    dims, grid, prim, adj, ax_s, near, refine, owner, weight, sums, fourth, row, bw, lhs, rhs, frad, fazi
):
    del ax_s
    nr, na, nx = dims
    tiles = na // 8
    sub = lax.broadcasted_iota(jnp.int32, (8, nx), 0)
    zero = jnp.zeros((8, nx), jnp.float32)
    head, tail = block_row(grid, near, refine, owner, weight, nx)
    row[:, 0:nx] = head
    row[:, nx:2 * nx] = tail
    i = lax.broadcasted_iota(jnp.int32, (nx, nx), 0)
    c = lax.broadcasted_iota(jnp.int32, (nx, nx), 1)
    for n, table in enumerate((UPPER, LOWER, FOURTH)):
        own = taps(i, c, table).astype(jnp.bfloat16)
        for k in range(3):
            rhs[pl.ds(k * nx, nx), pl.ds(n * nx, nx)] = own

    def products(group):
        size = PLANES * na
        for t, src in enumerate((prim, adj)):
            for f in range(F):
                for i in range(PLANES):
                    for k, x in enumerate(split3(src[f, group * PLANES + i])):
                        lhs[group, t, pl.ds(f * size + i * na, na), pl.ds(k * nx, nx)] = x
        rows = pl.ds(group * F * size, F * size)
        sums[rows, :] = jnp.dot(lhs[group, 0], rhs[:, 0:2 * nx], preferred_element_type=jnp.float32)
        fourth[rows, :] = jnp.dot(
            lhs[group, 1], rhs[:, 2 * nx:3 * nx], preferred_element_type=jnp.float32
        )

    def rad_flux(r, a):
        rows = pl.ds(8 * a, 8)
        return flux([face(*(prim[f, r + o, rows, :] for o in (-1, 0, 1, 2))) for f in range(F)], 0)

    def azi_flux(r, a):
        x = flux([face(*(shifted(prim, f, r, a, tiles, o) for o in (-1, 0, 1, 2))) for f in range(F)], 1)
        if a == 0:
            x = [jnp.where(sub < 1, 0.0, t) for t in x]
        if a == tiles - 1:
            x = [jnp.where(sub > 5, 0.0, t) for t in x]
        return x

    for f in range(F):
        fazi[f, 0:8, :] = zero

    def plane(r, carry):
        here = not isinstance(r, int) or 1 <= r <= nr - 3
        before = not isinstance(r, int) or 1 <= r - 1 <= nr - 3
        for a in range(tiles):
            for f, x in enumerate(azi_flux(r, a)):
                fazi[f, pl.ds(8 + 8 * a, 8), :] = x
        for a in range(tiles):
            mine = pl.ds(8 * a, 8)
            up = rad_flux(r, a) if here else None
            for f in range(F):
                bal = fazi[f, pl.ds(8 * a + 8, 8), :] - fazi[f, pl.ds(8 * a + 7, 8), :]
                if before:
                    bal = bal - frad[f, a]
                if here:
                    bal = bal + up[f]
                    frad[f, a] = up[f]
                bw[f, r, mine, :] = bal

                def row(da):
                    x = shifted(adj, f, r, a, tiles, da)
                    if da < 0 and a == 0:
                        x = jnp.where(sub < -da, 0.0, x)
                    if da > 0 and a == tiles - 1:
                        x = jnp.where(sub > 7 - da, 0.0, x)
                    return x

                def layer(dr):
                    if isinstance(r, int) and not 0 <= r + dr < nr:
                        return None
                    return adj[f, r + dr, mine, :]

                two, one = row(-2) + row(2), row(-1) + row(1)
                for dr in (-2, 2):
                    x = layer(dr)
                    two = two if x is None else two + x
                for dr in (-1, 1):
                    x = layer(dr)
                    one = one if x is None else one + x
                bw[F + f, r, mine, :] = two - 4.0 * one + 12.0 * adj[f, r, mine, :]
        return carry

    for group in range(nr // PLANES):
        products(group)
        for i in range(PLANES):
            plane(group * PLANES + i, 0)


def radial_terms(dims, n_rad, prim, rad_a, rad_b):
    nr, na, nx = dims
    i_rad = lax.axis_index("rad")
    odd = lax.rem(i_rad, 2) == 1

    def before(g, i, rows):
        return jnp.where(i_rad == 0, 0.0, jnp.where(odd, rad_a[g, i, rows, :], rad_b[g, i, rows, :]))

    def after(g, i, rows):
        x = jnp.where(odd, rad_b[g, i, rows, :], rad_a[g, i, rows, :])
        return jnp.where(i_rad == n_rad - 1, 0.0, x)

    def radial(a):
        rows = pl.ds(8 * a, 8)
        low, high = [], []
        for f in range(F):
            b0, b1, h0, h1 = (before(f, 0, rows), before(f, 1, rows), after(f, 0, rows), after(f, 1, rows))
            u0, u1, u2 = (prim[f, i, rows, :] for i in range(3))
            v2, v1, v0 = (prim[f, nr - i, rows, :] for i in (3, 2, 1))
            low.append((face(b0, b1, u0, u1), face(b1, u0, u1, u2)))
            high.append((face(v2, v1, v0, h0), face(v1, v0, h0, h1)))
        p, q = (flux([x[i] for x in low], 0) for i in range(2))
        s, t = (flux([x[i] for x in high], 0) for i in range(2))
        bal = {
            0: [y - x for x, y in zip(p, q)],
            1: [-y for y in q],
            nr - 2: s,
            nr - 1: [y - x for x, y in zip(s, t)],
        }
        w = {0: [], 1: [], nr - 2: [], nr - 1: []}
        for f in range(F):
            g = F + f
            b0, b1, h0, h1 = (before(g, 0, rows), before(g, 1, rows), after(g, 0, rows), after(g, 1, rows))
            w[0].append(b0 - 4.0 * b1)
            w[1].append(b1)
            w[nr - 2].append(h0)
            w[nr - 1].append(h1 - 4.0 * h0)
        return bal, w

    return radial


def azimuthal_terms(dims, prim, azi_l, azi_r):
    na, nx = dims[1:]
    sub = lax.broadcasted_iota(jnp.int32, (8, nx), 0)

    def azimuthal(r, a):
        if a == 0:
            def layer(g, i):
                return jnp.broadcast_to(azi_l[g, r, 2 + i:3 + i, :], (8, nx))

            s = []
            for f in range(F):
                x = prim[f, r, 0:8, :]
                l0, l1 = layer(f, 0), layer(f, 1)
                s.append(
                    face(
                        jnp.where(sub == 0, l0, jnp.where(sub == 1, l1, pltpu.roll(x, 2, 0))),
                        jnp.where(sub == 0, l1, pltpu.roll(x, 1, 0)),
                        x,
                        prim[f, r, 1:9, :],
                    )
                )
            bal = [
                jnp.where(sub == 0, pltpu.roll(x, 7, 0) - x, jnp.where(sub == 1, -x, 0.0))
                for x in flux(s, 1)
            ]
            w = []
            for f in range(F):
                l0, l1 = layer(F + f, 0), layer(F + f, 1)
                w.append(jnp.where(sub == 0, l0 - 4.0 * l1, jnp.where(sub == 1, l1, 0.0)))
            return bal, w

        def layer(g, i):
            return jnp.broadcast_to(azi_r[g, r, i:i + 1, :], (8, nx))

        s = []
        for f in range(F):
            x = prim[f, r, na - 8:na, :]
            h0, h1 = layer(f, 0), layer(f, 1)
            s.append(
                face(
                    prim[f, r, na - 9:na - 1, :],
                    x,
                    jnp.where(sub == 7, h0, pltpu.roll(x, 7, 0)),
                    jnp.where(sub == 7, h1, jnp.where(sub == 6, h0, pltpu.roll(x, 6, 0))),
                )
            )
        bal = [
            jnp.where(sub == 7, x - pltpu.roll(x, 1, 0), jnp.where(sub == 6, x, 0.0)) for x in flux(s, 1)
        ]
        w = []
        for f in range(F):
            h0, h1 = layer(F + f, 0), layer(F + f, 1)
            w.append(jnp.where(sub == 7, h1 - 4.0 * h0, jnp.where(sub == 6, h0, 0.0)))
        return bal, w

    return azimuthal


def indicator_of(bal, w):
    total = w[0] * bal[0]
    for f in range(1, F):
        total = total + w[f] * bal[f]
    return jnp.abs(total) * (1.0 / 144.0)


def rows_kernel(dims, prim, bw, done, azi_l, azi_r, ind, ends, part_sums):
    nr, na, nx = dims
    tiles = na // 8
    azimuthal = azimuthal_terms(dims, prim, azi_l, azi_r)

    def outer(r, a):
        mine = pl.ds(8 * a, 8)
        more_bal, more_w = azimuthal(r, a)
        bal = [bw[f, r, mine, :] + more_bal[f] for f in range(F)]
        return bal, [bw[F + f, r, mine, :] + more_w[f] for f in range(F)]

    for i, r in enumerate((0, 1, nr - 2, nr - 1)):
        for a in range(tiles):
            mine = pl.ds(8 * a, 8)
            if a in (0, tiles - 1):
                bal, w = outer(r, a)
                for f in range(F):
                    ends[f, i, mine, :] = bal[f]
                    ends[F + f, i, mine, :] = w[f]
            else:
                for g in range(2 * F):
                    ends[g, i, mine, :] = bw[g, r, mine, :]

    def plane(r, sums):
        out = []
        for a in range(tiles):
            mine = pl.ds(8 * a, 8)
            x = indicator_of(*outer(r, a)) if a in (0, tiles - 1) else done[r, mine, :]
            ind[r, mine, :] = x
            out.append(sums[a] + x)
        return tuple(out)

    zero = jnp.zeros((8, nx), jnp.float32)
    sums = lax.fori_loop(2, nr - 2, plane, (zero,) * tiles, unroll=True)
    for a in range(tiles):
        part_sums[a] = sums[a]


def main_kernel(dims, n_rad, prim, ends, part_sums, rad_a, rad_b, row, ind, send):
    nr, na, nx = dims
    tiles = na // 8
    lane = lax.broadcasted_iota(jnp.int32, (8, nx), 1)
    radial = radial_terms(dims, n_rad, prim, rad_a, rad_b)
    sums = []
    for a in range(tiles):
        mine = pl.ds(8 * a, 8)
        more_bal, more_w = radial(a)
        t = part_sums[a]
        for i, r in enumerate((0, 1, nr - 2, nr - 1)):
            bal = [ends[f, i, mine, :] + more_bal[r][f] for f in range(F)]
            w = [ends[F + f, i, mine, :] + more_w[r][f] for f in range(F)]
            x = indicator_of(bal, w)
            ind[i, mine, :] = x
            t = t + x
        sums.append(t)

    groups = nx // BLK
    halves_a = na // BLK
    per_tile = BLK // 8
    i = lax.broadcasted_iota(jnp.int32, (nx, nx), 0)
    c = lax.broadcasted_iota(jnp.int32, (nx, nx), 1)
    gather = jnp.where(i // BLK == c % groups, 1.0, 0.0)
    rows = []
    for b in range(halves_a):
        t = sums[b * per_tile]
        for i in range(1, per_tile):
            t = t + sums[b * per_tile + i]
        rows.append(t)
    rows = jnp.dot(
        jnp.concatenate(rows, axis=0),
        gather,
        precision=lax.Precision.HIGHEST,
        preferred_element_type=jnp.float32,
    )
    means = jnp.zeros((8, nx), jnp.float32)
    for b in range(halves_a):
        t = jnp.sum(rows[8 * b:8 * b + 8], axis=0, keepdims=True)
        means = jnp.where(lane // groups == b, jnp.broadcast_to(t, (8, nx)), means)
    means = means * (1.0 / BLK**3)
    head = jnp.broadcast_to(row[:, 0:nx], (8, nx))
    head = jnp.where(lane < groups * halves_a, means, head)
    tail = jnp.broadcast_to(row[:, nx:2 * nx], (8, nx))
    both = jnp.where(lax.broadcasted_iota(jnp.int32, (8, nx), 0) & 1 == 0, head, tail)
    for d in range(send.shape[0] // 8):
        send[pl.ds(8 * d, 8), :] = both


def final_kernel(n_loc, per_ax, data, inside, outside, cost_out, load_out, ind, cost, load, means, sems):
    nr = ind.shape[0]
    inner = pl.ds(2, nr - 4)
    leave = [
        pltpu.make_async_copy(inside.at[inner], ind.at[inner], sems.at[0]),
        pltpu.make_async_copy(outside.at[pl.ds(0, 2)], ind.at[pl.ds(0, 2)], sems.at[1]),
        pltpu.make_async_copy(outside.at[pl.ds(2, 2)], ind.at[pl.ds(nr - 2, 2)], sems.at[2]),
    ]
    for c in leave:
        c.start()
    n_dev, nx = data.shape[0] // 2, data.shape[1]
    me = (lax.axis_index("rad") * lax.axis_size("azi") + lax.axis_index("azi")) * lax.axis_size(
        "ax"
    ) + lax.axis_index("ax")
    lane = lax.broadcasted_iota(jnp.int32, (8, nx), 1)
    sub = lax.broadcasted_iota(jnp.int32, (8, nx), 0)
    small = n_dev <= 32
    groups = n_dev // 8
    ok = lane < n_loc

    def rows(g, part):
        return data[pl.ds(16 * g + part, 8, stride=2), :]

    def table(g, carry):
        x = jnp.where(ok, rows(g, 0), 0.0)
        x = pltpu.roll(x, 0, 1, stride=n_loc, stride_axis=0)
        means[g] = jnp.broadcast_to(jnp.sum(x, axis=0, keepdims=True), (8, nx))
        return carry

    lax.fori_loop(0, groups, table, 0, unroll=small)

    def group(g, carry):
        acc_load, acc_cost = carry
        head = rows(g, 0)
        tail = rows(g, 1)
        spot = head.astype(jnp.int32)
        pos = spot & (nx - 1)
        line = spot >> (nx.bit_length() - 1)

        def look(q, acc):
            return jnp.where(line == q, jnp.take_along_axis(means[q], pos, axis=1), acc)

        val = lax.fori_loop(0, groups, look, jnp.zeros((8, nx), jnp.float32), unroll=small)
        beside = None
        for j in range(6):
            x = pltpu.roll(val, nx - n_loc * (1 + j), 1)
            beside = x if beside is None else beside + x
        smooth = 0.5 * head + (0.5 / 6.0) * beside
        refine = pltpu.roll(head, nx - 7 * n_loc, 1)
        owner = tail.astype(jnp.int32)
        weight = pltpu.roll(tail, nx - n_loc, 1)
        home = sub + 8 * g
        c = smooth * (1.0 + 7.0 * refine) + jnp.where(owner != home, 0.25 * weight, 0.0)
        acc_load = acc_load + jnp.where(ok & (owner == me), c, 0.0)
        acc_cost = acc_cost + jnp.where(home == me, c, 0.0)
        return acc_load, acc_cost

    zero = jnp.zeros((8, nx), jnp.float32)
    acc_load, acc_cost = lax.fori_loop(0, groups, group, (zero, zero), unroll=small)
    own = jnp.sum(acc_cost, axis=0, keepdims=True)
    for b in range(n_loc // per_ax):
        x = own if b == 0 else pltpu.roll(own, nx - b * per_ax, 1)
        cost[0, pl.ds(b, 1), :] = x[:, 0:per_ax]
    total = jnp.sum(jnp.sum(acc_load, axis=0, keepdims=True), axis=1, keepdims=True) * (1.0 / n_loc)
    load[0] = total
    for i, (x, y) in enumerate(((cost, cost_out), (load, load_out))):
        leave.append(pltpu.make_async_copy(x, y, sems.at[3 + i]))
        leave[-1].start()
    for c in leave:
        c.wait()


def on_device(primal, adjoint, refine_flag, owner_map, migrate_weight, neighbor_list):
    _, nr, na, nx = primal.shape
    dims = (nr, na, nx)
    sizes = n_rad, n_azi, n_ax = tuple(lax.axis_size(a) for a in AXES)
    n_dev = n_rad * n_azi * n_ax
    tiles = na // 8
    halves = nr * tiles // (nx // 4)
    f32 = functools.partial(jax.ShapeDtypeStruct, dtype=jnp.float32)
    anyspec = pl.BlockSpec(memory_space=pl.ANY)
    hbm = pl.BlockSpec(memory_space=pltpu.HBM)
    vmem = pl.BlockSpec(memory_space=pltpu.VMEM)

    rad_a, rad_b, azi_s = pl.pallas_call(
        functools.partial(edge_kernel, dims),
        out_shape=(f32((2 * F, 2, na, nx)), f32((2 * F, 2, na, nx)), f32((2 * F, nr, 4, nx))),
        in_specs=[hbm, hbm],
        out_specs=(vmem, vmem, vmem),
        scratch_shapes=[pltpu.SemaphoreType.DMA((2, 4))],
        compiler_params=pltpu.CompilerParams(vmem_limit_bytes=8 << 20),
        name="edges",
    )(*(pltpu.with_memory_space_constraint(x, pltpu.HBM) for x in (primal, adjoint)))
    field = f32(primal.shape)
    primal, adjoint, ax_first, ax_second = pl.pallas_call(
        functools.partial(lane_kernel, dims),
        out_shape=(field, field) + (f32((2 * F, halves // 2, 8, nx)),) * 2,
        in_specs=[hbm, hbm, anyspec],
        out_specs=(vmem,) * 4,
        scratch_shapes=[pltpu.SemaphoreType.DMA((2, F))],
        compiler_params=pltpu.CompilerParams(vmem_limit_bytes=16 << 20),
        name="lanes",
    )(*(pltpu.with_memory_space_constraint(x, pltpu.HBM) for x in (primal, adjoint)), rad_b)

    ax_a = lax.ppermute(ax_first, AXES, pair_round(sizes, 2, 0))
    ax_b = lax.ppermute(ax_second, AXES, pair_round(sizes, 2, 1))
    azi_l = lax.ppermute(azi_s, "azi", ring(n_azi, 1))
    azi_r = azi_l if n_azi == 2 else lax.ppermute(azi_s, "azi", ring(n_azi, -1))
    rad_a = lax.ppermute(rad_a, AXES, pair_round(sizes, 0, 0))
    rad_b = lax.ppermute(rad_b, AXES, pair_round(sizes, 0, 1))

    per_rad, per_azi, per_ax = nr // BLK, na // BLK, nx // BLK
    n_loc = per_rad * per_azi * per_ax
    near = neighbor_list.transpose(0, 3, 1, 2)
    cells = F * nr * na
    sums, fourth, row, part_bw = pl.pallas_call(
        functools.partial(inner_kernel, dims, ((per_rad, per_azi, per_ax), (n_azi, n_ax))),
        out_shape=(
            f32((cells, 2 * nx)),
            f32((cells, nx)),
            f32((1, 2 * nx)),
            f32((2 * F, nr, na, nx)),
        ),
        in_specs=[vmem] * 7,
        out_specs=(vmem,) * 4,
        scratch_shapes=[
            pltpu.VMEM((nr // PLANES, 2, F * PLANES * na, 3 * nx), jnp.bfloat16),
            pltpu.VMEM((3 * nx, 3 * nx), jnp.bfloat16),
            pltpu.VMEM((F, tiles, 8, nx), jnp.float32),
            pltpu.VMEM((F, 8 + na, nx), jnp.float32),
        ],
        compiler_params=pltpu.CompilerParams(vmem_limit_bytes=16 << 20),
        name="inner",
    )(primal, adjoint, ax_first, near, refine_flag, owner_map, migrate_weight)
    bw, done = pl.pallas_call(
        functools.partial(axial_kernel, dims, n_ax),
        out_shape=(f32((2 * F, nr, na, nx)), f32(dims)),
        in_specs=[vmem] * 5,
        out_specs=(vmem, vmem),
        scratch_shapes=[
            pltpu.VMEM((3, 2 * F, halves, 8, nx), jnp.float32),
            pltpu.VMEM((2 * cells, nx), jnp.bfloat16),
            pltpu.VMEM((nx, 3 * nx), jnp.bfloat16),
            pltpu.VMEM((cells, 2 * nx), jnp.float32),
            pltpu.VMEM((cells, nx), jnp.float32),
        ],
        compiler_params=pltpu.CompilerParams(vmem_limit_bytes=16 << 20),
        name="axial",
    )(sums, fourth, part_bw, ax_a, ax_b)

    inside, ends, part_sums = pl.pallas_call(
        functools.partial(rows_kernel, dims),
        out_shape=(f32(dims), f32((2 * F, 4, na, nx)), f32((tiles, 8, nx))),
        in_specs=[vmem] * 5,
        out_specs=(vmem,) * 3,
        compiler_params=pltpu.CompilerParams(vmem_limit_bytes=16 << 20),
        name="rows",
    )(primal, bw, done, azi_l, azi_r)
    outside, send = pl.pallas_call(
        functools.partial(main_kernel, dims, n_rad),
        out_shape=(f32((4, na, nx)), f32((2 * n_dev, nx))),
        in_specs=[vmem] * 6,
        out_specs=(vmem, vmem),
        compiler_params=pltpu.CompilerParams(vmem_limit_bytes=16 << 20),
        name="planes",
    )(primal, ends, part_sums, rad_a, rad_b, row)

    data = lax.all_to_all(send, AXES, 0, 0, tiled=True)

    cost, load, indicator = pl.pallas_call(
        functools.partial(final_kernel, n_loc, per_ax),
        out_shape=(f32((per_rad, per_azi, per_ax)), f32((1, 1, 1)), f32(dims)),
        in_specs=[vmem, anyspec, anyspec],
        out_specs=(anyspec,) * 3,
        scratch_shapes=[
            pltpu.VMEM((per_rad, per_azi, per_ax), jnp.float32),
            pltpu.VMEM((1, 1, 1), jnp.float32),
            pltpu.VMEM((n_dev // 8, 8, nx), jnp.float32),
            pltpu.SemaphoreType.DMA((5,)),
        ],
        compiler_params=pltpu.CompilerParams(vmem_limit_bytes=4 << 20),
        name="blocks",
    )(data, inside, outside)
    return indicator, cost, load


def solution(mesh):
    spec = P("rad", "azi", "ax")
    field = P(None, "rad", "azi", "ax")
    return jax.shard_map(
        on_device,
        mesh=mesh,
        in_specs=(field, field, spec, spec, spec, P("rad", "azi", "ax", None)),
        out_specs=(spec, spec, spec),
        check_vma=False,
    )
```

```python
import functools

import jax
import jax.numpy as jnp
from jax import lax
from jax.experimental import pallas as pl
from jax.experimental.pallas import tpu as pltpu
from jax.sharding import PartitionSpec as P

BLK = 16
F = 5
AXES = ("rad", "azi", "ax")


def pair_round(sizes, along, first):
    n = sizes[along]
    step = [sizes[1] * sizes[2], sizes[2], 1]
    used = range(first, n - 1, 2)
    partner = {i: i + 1 for i in used} | {i + 1: i for i in used}
    idle = [i for i in range(n) if i not in partner]
    if along == 2 and len(idle) == 2:
        partner |= {idle[0]: idle[1], idle[1]: idle[0]}
    pairs = []
    for me in range(sizes[0] * step[0]):
        i = me // step[along] % n
        if i in partner:
            pairs.append((me, me + (partner[i] - i) * step[along]))
        elif along != 2 and sizes[2] % 2 == 0:
            pairs.append((me, me ^ 1))
    return pairs


def ring(count, step):
    return [(i, (i + step) % count) for i in range(count)]


def edge_kernel(dims, n_rad, prim, adj, rad_a, rad_b, azi_s, sems):
    nr, na, nx = dims
    odd = lax.rem(lax.axis_index("rad"), 2)
    first = jnp.where(odd == 0, nr - 2, 0)
    copies = []
    for t, src in enumerate((prim, adj)):
        rows = pl.ds(t * F, F)
        for i, (a, b) in enumerate(
            (
                (src.at[:, pl.ds(first, 2)], rad_a.at[rows]),
                (src.at[:, pl.ds(nr - 2 - first, 2)], rad_b.at[rows]),
                (src.at[:, :, pl.ds(0, 2)], azi_s.at[rows, :, pl.ds(0, 2)]),
                (src.at[:, :, pl.ds(na - 2, 2)], azi_s.at[rows, :, pl.ds(2, 2)]),
            )
        ):
            copies.append((i, pltpu.make_async_copy(a, b, sems.at[t, i])))
    i_rad = lax.axis_index("rad")
    alone = (i_rad == 0) | ((i_rad == n_rad - 1) & (odd == 1))
    for act in ("start", "wait"):
        for i, c in copies:
            if i != 1:
                getattr(c, act)()

        @pl.when(jnp.logical_not(alone))
        def _():
            for i, c in copies:
                if i == 1:
                    getattr(c, act)()


def lane_kernel(dims, prim, adj, first, second):
    nr, na, nx = dims
    even = lax.rem(lax.axis_index("ax"), 2) == 0
    slot = lax.broadcasted_iota(jnp.int32, (8, nx), 1) >> 1
    tiles = na // 8
    per = nx // 2
    for t, src in enumerate((prim, adj)):
        for f in range(F):
            for h in range(nr * tiles // per):
                upper = lower = jnp.zeros((8, nx), jnp.float32)
                for j in range(per):
                    k = h * per + j
                    x = src[f, k // tiles, pl.ds(8 * (k % tiles), 8), :]
                    x = pltpu.roll(x, (2 * j + 2) % nx, 1)
                    upper = jnp.where(slot == j, x, upper)
                    lower = jnp.where(slot == (j + 1) % per, x, lower)
                first[t * F + f, h] = jnp.where(even, upper, lower)
                second[t * F + f, h] = jnp.where(even, lower, upper)


def flux(s, along):
    inv = 1.0 / s[0]
    v = s[1 + along] * inv
    kin = (s[1] * s[1] + s[2] * s[2] + s[3] * s[3]) * inv
    p = 0.4 * s[4] - 0.2 * kin
    out = [s[1 + along], s[1] * v, s[2] * v, s[3] * v, (s[4] + p) * v]
    out[1 + along] = out[1 + along] + p
    return out


def face(m1, c, p1, p2):
    return 7.0 * (c + p1) - (m1 + p2)


def split3(x):
    hi = x.astype(jnp.bfloat16)
    x = x - hi.astype(jnp.float32)
    mid = x.astype(jnp.bfloat16)
    x = x - mid.astype(jnp.float32)
    return hi, mid, x.astype(jnp.bfloat16)


def taps(rows, cols, table):
    out = jnp.zeros(rows.shape, jnp.float32)
    for step, value in table.items():
        out = jnp.where(rows - cols == step, value, out)
    return out


UPPER = {-1: -1.0, 0: 7.0, 1: 7.0, 2: -1.0}
LOWER = {-2: -1.0, -1: 7.0, 0: 7.0, 1: -1.0}
FOURTH = {-2: 1.0, -1: -4.0, 0: 6.0, 1: -4.0, 2: 1.0}


def block_row(grid, near, refine, owner, weight, nx):
    (per_rad, per_azi, per_ax), (n_azi, n_ax) = grid
    n_loc = per_rad * per_azi * per_ax
    blocks_azi, blocks_ax = per_azi * n_azi, per_ax * n_ax
    lane = lax.broadcasted_iota(jnp.int32, (per_azi, nx), 1)

    def place(number):
        b_rad = lax.div(number, blocks_azi * blocks_ax)
        b_azi = lax.rem(lax.div(number, blocks_ax), blocks_azi)
        b_ax = lax.rem(number, blocks_ax)
        device = (lax.div(b_rad, per_rad) * n_azi + lax.div(b_azi, per_azi)) * n_ax + lax.div(b_ax, per_ax)
        local = (lax.rem(b_rad, per_rad) * per_azi + lax.rem(b_azi, per_azi)) * per_ax + lax.rem(b_ax, per_ax)
        return device * n_loc + local

    def spread(x, at):
        x = jnp.concatenate([x, jnp.zeros((per_azi, nx - per_ax), jnp.int32)], axis=1)
        x = jnp.where(lane < per_ax, x, 0).astype(jnp.float32)
        rows = [x[b:b + 1] if at + b * per_ax == 0 else pltpu.roll(x[b:b + 1], at + b * per_ax, 1) for b in range(per_azi)]
        return sum(rows[1:], rows[0])

    head = spread(refine[0], 7 * n_loc)
    for j in range(6):
        head = head + spread(place(near[0, j]), (1 + j) * n_loc)
    tail = spread(owner[0], 0) + spread(weight[0], n_loc)
    return head, tail


PLANES = 4


def place_of(dims, f, r, a):
    _, na, _ = dims
    group = PLANES * na
    if isinstance(r, int):
        return (r // PLANES * F + f) * group + r % PLANES * na + 8 * a
    return pl.multiple_of((lax.div(r, PLANES) * F + f) * group + lax.rem(r, PLANES) * na, na) + 8 * a


def axial_kernel(dims, n_ax, sums, fourth, part_bw, ax_a, ax_b, bw, done, got, lhs, rhs, far, far_w):
    nr, na, nx = dims
    i_ax = lax.axis_index("ax")
    even_ax = lax.rem(i_ax, 2) == 0
    lane = lax.broadcasted_iota(jnp.int32, (8, nx), 1)
    part = lane & 3
    slot = lane >> 2
    tiles = na // 8
    per = nx // 4
    halves = nr * tiles // per
    size = nr * na
    third = per // 3

    i = lax.broadcasted_iota(jnp.int32, (nx, nx), 0) & 3
    c = lax.broadcasted_iota(jnp.int32, (nx, nx), 1)
    cells = jnp.where(i < 2, i - 2, i - 2 + nx)
    for n, table in enumerate((UPPER, LOWER, FOURTH)):
        rhs[:, pl.ds(n * nx, nx)] = taps(cells, c, table).astype(jnp.bfloat16)

    for h in range(halves):
        for f in range(2 * F):
            a, b = ax_a[f, h // 2], ax_b[f, h // 2]
            left = jnp.where(i_ax == 0, 0.0, jnp.where(even_ax, b, a))
            right = jnp.where(i_ax == n_ax - 1, 0.0, jnp.where(even_ax, a, b))
            at = h % 2 * (nx // 2) + 2 * slot + (lane & 1)
            left = jnp.take_along_axis(left, at, axis=1)
            right = jnp.take_along_axis(right, (at + 2) & (nx - 1), axis=1)
            for k, x in enumerate(split3(jnp.where(part < 2, left, right))):
                x = x.astype(jnp.float32)
                got[k, f, h] = pltpu.roll(x, 4 * third * k, 1) if k else x

    def build(g, carry):
        for r in range(nr):
            h, j0 = r * tiles // per, r * tiles % per
            rows = pl.ds(pl.multiple_of(g * size, size) + r * na, na)
            y = []
            for a in range(tiles):
                x = jnp.zeros((8, nx), jnp.float32)
                for k in range(3):
                    x = jnp.where(slot == (j0 + a + third * k) % per, got[k, g, h], x)
                y.append(x)
            lhs[rows, :] = jnp.concatenate(y, axis=0).astype(jnp.bfloat16)
        return carry

    lax.fori_loop(0, 2 * F, build, 0)
    far[...] = jnp.dot(lhs[0:F * size, :], rhs[:, 0:2 * nx], preferred_element_type=jnp.float32)
    far_w[...] = jnp.dot(
        lhs[F * size:2 * F * size, :], rhs[:, 2 * nx:3 * nx], preferred_element_type=jnp.float32
    )

    def tile(r, a, whole):
        mine = pl.ds(8 * a, 8)
        at = [pl.ds(f * size + r * na + 8 * a, 8) for f in range(F)]
        own = [pl.ds(place_of(dims, f, r, a), 8) for f in range(F)]
        up = flux([sums[p, 0:nx] + far[q, 0:nx] for p, q in zip(own, at)], 2)
        low = flux([sums[p, nx:2 * nx] + far[q, nx:2 * nx] for p, q in zip(own, at)], 2)
        total = None
        for f in range(F):
            bal = part_bw[f, r, mine, :] + (up[f] - low[f])
            w = part_bw[F + f, r, mine, :] + (fourth[own[f], :] + far_w[at[f], :])
            if whole:
                total = w * bal if total is None else total + w * bal
            else:
                bw[f, r, mine, :] = bal
                bw[F + f, r, mine, :] = w
        if whole:
            done[r, mine, :] = jnp.abs(total) * (1.0 / 144.0)

    def body(r, carry):
        for a in range(tiles):
            tile(r, a, 0 < a < tiles - 1)
        return carry

    for r in (0, 1, nr - 2, nr - 1):
        for a in range(tiles):
            tile(r, a, False)
    lax.fori_loop(2, nr - 2, body, 0, unroll=True)


def shifted(src, f, r, a, tiles, da):
    if da < 0 and a == 0 or da > 0 and a == tiles - 1:
        return pltpu.roll(src[f, r, pl.ds(8 * a, 8), :], -da % 8, 0)
    return src[f, r, pl.ds(8 * a + da, 8), :]


def inner_kernel(
    dims, grid, prim, adj, ax_s, near, refine, owner, weight, sums, fourth, row, bw, lhs, rhs, frad, fazi
):
    del ax_s
    nr, na, nx = dims
    tiles = na // 8
    sub = lax.broadcasted_iota(jnp.int32, (8, nx), 0)
    zero = jnp.zeros((8, nx), jnp.float32)
    head, tail = block_row(grid, near, refine, owner, weight, nx)
    row[:, 0:nx] = head
    row[:, nx:2 * nx] = tail
    i = lax.broadcasted_iota(jnp.int32, (nx, nx), 0)
    c = lax.broadcasted_iota(jnp.int32, (nx, nx), 1)
    for n, table in enumerate((UPPER, LOWER, FOURTH)):
        own = taps(i, c, table).astype(jnp.bfloat16)
        for k in range(3):
            rhs[pl.ds(k * nx, nx), pl.ds(n * nx, nx)] = own

    def products(group):
        size = PLANES * na
        for t, src in enumerate((prim, adj)):
            for f in range(F):
                for i in range(PLANES):
                    for k, x in enumerate(split3(src[f, group * PLANES + i])):
                        lhs[group, t, pl.ds(f * size + i * na, na), pl.ds(k * nx, nx)] = x
        rows = pl.ds(group * F * size, F * size)
        sums[rows, :] = jnp.dot(lhs[group, 0], rhs[:, 0:2 * nx], preferred_element_type=jnp.float32)
        fourth[rows, :] = jnp.dot(
            lhs[group, 1], rhs[:, 2 * nx:3 * nx], preferred_element_type=jnp.float32
        )

    def rad_flux(r, a):
        rows = pl.ds(8 * a, 8)
        return flux([face(*(prim[f, r + o, rows, :] for o in (-1, 0, 1, 2))) for f in range(F)], 0)

    def azi_flux(r, a):
        x = flux([face(*(shifted(prim, f, r, a, tiles, o) for o in (-1, 0, 1, 2))) for f in range(F)], 1)
        if a == 0:
            x = [jnp.where(sub < 1, 0.0, t) for t in x]
        if a == tiles - 1:
            x = [jnp.where(sub > 5, 0.0, t) for t in x]
        return x

    for f in range(F):
        fazi[f, 0:8, :] = zero

    def plane(r, carry):
        here = not isinstance(r, int) or 1 <= r <= nr - 3
        before = not isinstance(r, int) or 1 <= r - 1 <= nr - 3
        for a in range(tiles):
            for f, x in enumerate(azi_flux(r, a)):
                fazi[f, pl.ds(8 + 8 * a, 8), :] = x
        for a in range(tiles):
            mine = pl.ds(8 * a, 8)
            up = rad_flux(r, a) if here else None
            for f in range(F):
                bal = fazi[f, pl.ds(8 * a + 8, 8), :] - fazi[f, pl.ds(8 * a + 7, 8), :]
                if before:
                    bal = bal - frad[f, a]
                if here:
                    bal = bal + up[f]
                    frad[f, a] = up[f]
                bw[f, r, mine, :] = bal

                def row(da):
                    x = shifted(adj, f, r, a, tiles, da)
                    if da < 0 and a == 0:
                        x = jnp.where(sub < -da, 0.0, x)
                    if da > 0 and a == tiles - 1:
                        x = jnp.where(sub > 7 - da, 0.0, x)
                    return x

                def layer(dr):
                    if isinstance(r, int) and not 0 <= r + dr < nr:
                        return None
                    return adj[f, r + dr, mine, :]

                two, one = row(-2) + row(2), row(-1) + row(1)
                for dr in (-2, 2):
                    x = layer(dr)
                    two = two if x is None else two + x
                for dr in (-1, 1):
                    x = layer(dr)
                    one = one if x is None else one + x
                bw[F + f, r, mine, :] = two - 4.0 * one + 12.0 * adj[f, r, mine, :]
        return carry

    for group in range(nr // PLANES):
        products(group)
        for i in range(PLANES):
            plane(group * PLANES + i, 0)


def radial_terms(dims, n_rad, prim, rad_a, rad_b):
    nr, na, nx = dims
    i_rad = lax.axis_index("rad")
    odd = lax.rem(i_rad, 2) == 1

    def before(g, i, rows):
        return jnp.where(i_rad == 0, 0.0, jnp.where(odd, rad_a[g, i, rows, :], rad_b[g, i, rows, :]))

    def after(g, i, rows):
        x = jnp.where(odd, rad_b[g, i, rows, :], rad_a[g, i, rows, :])
        return jnp.where(i_rad == n_rad - 1, 0.0, x)

    def radial(a):
        rows = pl.ds(8 * a, 8)
        low, high = [], []
        for f in range(F):
            b0, b1, h0, h1 = (before(f, 0, rows), before(f, 1, rows), after(f, 0, rows), after(f, 1, rows))
            u0, u1, u2 = (prim[f, i, rows, :] for i in range(3))
            v2, v1, v0 = (prim[f, nr - i, rows, :] for i in (3, 2, 1))
            low.append((face(b0, b1, u0, u1), face(b1, u0, u1, u2)))
            high.append((face(v2, v1, v0, h0), face(v1, v0, h0, h1)))
        p, q = (flux([x[i] for x in low], 0) for i in range(2))
        s, t = (flux([x[i] for x in high], 0) for i in range(2))
        bal = {
            0: [y - x for x, y in zip(p, q)],
            1: [-y for y in q],
            nr - 2: s,
            nr - 1: [y - x for x, y in zip(s, t)],
        }
        w = {0: [], 1: [], nr - 2: [], nr - 1: []}
        for f in range(F):
            g = F + f
            b0, b1, h0, h1 = (before(g, 0, rows), before(g, 1, rows), after(g, 0, rows), after(g, 1, rows))
            w[0].append(b0 - 4.0 * b1)
            w[1].append(b1)
            w[nr - 2].append(h0)
            w[nr - 1].append(h1 - 4.0 * h0)
        return bal, w

    return radial


def azimuthal_terms(dims, prim, azi_l, azi_r):
    na, nx = dims[1:]
    sub = lax.broadcasted_iota(jnp.int32, (8, nx), 0)

    def azimuthal(r, a):
        if a == 0:
            def layer(g, i):
                return jnp.broadcast_to(azi_l[g, r, 2 + i:3 + i, :], (8, nx))

            s = []
            for f in range(F):
                x = prim[f, r, 0:8, :]
                l0, l1 = layer(f, 0), layer(f, 1)
                s.append(
                    face(
                        jnp.where(sub == 0, l0, jnp.where(sub == 1, l1, pltpu.roll(x, 2, 0))),
                        jnp.where(sub == 0, l1, pltpu.roll(x, 1, 0)),
                        x,
                        prim[f, r, 1:9, :],
                    )
                )
            bal = [
                jnp.where(sub == 0, pltpu.roll(x, 7, 0) - x, jnp.where(sub == 1, -x, 0.0))
                for x in flux(s, 1)
            ]
            w = []
            for f in range(F):
                l0, l1 = layer(F + f, 0), layer(F + f, 1)
                w.append(jnp.where(sub == 0, l0 - 4.0 * l1, jnp.where(sub == 1, l1, 0.0)))
            return bal, w

        def layer(g, i):
            return jnp.broadcast_to(azi_r[g, r, i:i + 1, :], (8, nx))

        s = []
        for f in range(F):
            x = prim[f, r, na - 8:na, :]
            h0, h1 = layer(f, 0), layer(f, 1)
            s.append(
                face(
                    prim[f, r, na - 9:na - 1, :],
                    x,
                    jnp.where(sub == 7, h0, pltpu.roll(x, 7, 0)),
                    jnp.where(sub == 7, h1, jnp.where(sub == 6, h0, pltpu.roll(x, 6, 0))),
                )
            )
        bal = [
            jnp.where(sub == 7, x - pltpu.roll(x, 1, 0), jnp.where(sub == 6, x, 0.0)) for x in flux(s, 1)
        ]
        w = []
        for f in range(F):
            h0, h1 = layer(F + f, 0), layer(F + f, 1)
            w.append(jnp.where(sub == 7, h1 - 4.0 * h0, jnp.where(sub == 6, h0, 0.0)))
        return bal, w

    return azimuthal


def indicator_of(bal, w):
    total = w[0] * bal[0]
    for f in range(1, F):
        total = total + w[f] * bal[f]
    return jnp.abs(total) * (1.0 / 144.0)


def rows_kernel(dims, prim, bw, done, azi_l, azi_r, ind, ends, part_sums):
    nr, na, nx = dims
    tiles = na // 8
    azimuthal = azimuthal_terms(dims, prim, azi_l, azi_r)

    def outer(r, a):
        mine = pl.ds(8 * a, 8)
        more_bal, more_w = azimuthal(r, a)
        bal = [bw[f, r, mine, :] + more_bal[f] for f in range(F)]
        return bal, [bw[F + f, r, mine, :] + more_w[f] for f in range(F)]

    for i, r in enumerate((0, 1, nr - 2, nr - 1)):
        for a in range(tiles):
            mine = pl.ds(8 * a, 8)
            if a in (0, tiles - 1):
                bal, w = outer(r, a)
                for f in range(F):
                    ends[f, i, mine, :] = bal[f]
                    ends[F + f, i, mine, :] = w[f]
            else:
                for g in range(2 * F):
                    ends[g, i, mine, :] = bw[g, r, mine, :]

    def plane(r, sums):
        out = []
        for a in range(tiles):
            mine = pl.ds(8 * a, 8)
            x = indicator_of(*outer(r, a)) if a in (0, tiles - 1) else done[r, mine, :]
            ind[r, mine, :] = x
            out.append(sums[a] + x)
        return tuple(out)

    zero = jnp.zeros((8, nx), jnp.float32)
    sums = lax.fori_loop(2, nr - 2, plane, (zero,) * tiles, unroll=True)
    for a in range(tiles):
        part_sums[a] = sums[a]


def main_kernel(dims, n_rad, prim, ends, part_sums, rad_a, rad_b, row, ind, send):
    nr, na, nx = dims
    tiles = na // 8
    lane = lax.broadcasted_iota(jnp.int32, (8, nx), 1)
    radial = radial_terms(dims, n_rad, prim, rad_a, rad_b)
    sums = []
    for a in range(tiles):
        mine = pl.ds(8 * a, 8)
        more_bal, more_w = radial(a)
        t = part_sums[a]
        for i, r in enumerate((0, 1, nr - 2, nr - 1)):
            bal = [ends[f, i, mine, :] + more_bal[r][f] for f in range(F)]
            w = [ends[F + f, i, mine, :] + more_w[r][f] for f in range(F)]
            x = indicator_of(bal, w)
            ind[i, mine, :] = x
            t = t + x
        sums.append(t)

    groups = nx // BLK
    halves_a = na // BLK
    per_tile = BLK // 8
    i = lax.broadcasted_iota(jnp.int32, (nx, nx), 0)
    c = lax.broadcasted_iota(jnp.int32, (nx, nx), 1)
    gather = jnp.where(i // BLK == c % groups, 1.0, 0.0)
    rows = []
    for b in range(halves_a):
        t = sums[b * per_tile]
        for i in range(1, per_tile):
            t = t + sums[b * per_tile + i]
        rows.append(t)
    rows = jnp.dot(
        jnp.concatenate(rows, axis=0),
        gather,
        precision=lax.Precision.HIGHEST,
        preferred_element_type=jnp.float32,
    )
    means = jnp.zeros((8, nx), jnp.float32)
    for b in range(halves_a):
        t = jnp.sum(rows[8 * b:8 * b + 8], axis=0, keepdims=True)
        means = jnp.where(lane // groups == b, jnp.broadcast_to(t, (8, nx)), means)
    means = means * (1.0 / BLK**3)
    head = jnp.broadcast_to(row[:, 0:nx], (8, nx))
    head = jnp.where(lane < groups * halves_a, means, head)
    tail = jnp.broadcast_to(row[:, nx:2 * nx], (8, nx))
    both = jnp.where(lax.broadcasted_iota(jnp.int32, (8, nx), 0) & 1 == 0, head, tail)
    for d in range(send.shape[0] // 8):
        send[pl.ds(8 * d, 8), :] = both


def final_kernel(n_loc, per_ax, data, inside, outside, cost_out, load_out, ind, cost, load, means, sems):
    nr = ind.shape[0]
    inner = pl.ds(2, nr - 4)
    leave = [
        pltpu.make_async_copy(inside.at[inner], ind.at[inner], sems.at[0]),
        pltpu.make_async_copy(outside.at[pl.ds(0, 2)], ind.at[pl.ds(0, 2)], sems.at[1]),
        pltpu.make_async_copy(outside.at[pl.ds(2, 2)], ind.at[pl.ds(nr - 2, 2)], sems.at[2]),
    ]
    for c in leave:
        c.start()
    n_dev, nx = data.shape[0] // 2, data.shape[1]
    me = (lax.axis_index("rad") * lax.axis_size("azi") + lax.axis_index("azi")) * lax.axis_size(
        "ax"
    ) + lax.axis_index("ax")
    lane = lax.broadcasted_iota(jnp.int32, (8, nx), 1)
    sub = lax.broadcasted_iota(jnp.int32, (8, nx), 0)
    small = n_dev <= 32
    groups = n_dev // 8
    ok = lane < n_loc

    def rows(g, part):
        return data[pl.ds(16 * g + part, 8, stride=2), :]

    def table(g, carry):
        x = jnp.where(ok, rows(g, 0), 0.0)
        x = pltpu.roll(x, 0, 1, stride=n_loc, stride_axis=0)
        means[g] = jnp.broadcast_to(jnp.sum(x, axis=0, keepdims=True), (8, nx))
        return carry

    lax.fori_loop(0, groups, table, 0, unroll=small)

    def group(g, carry):
        acc_load, acc_cost = carry
        head = rows(g, 0)
        tail = rows(g, 1)
        spot = head.astype(jnp.int32)
        pos = spot & (nx - 1)
        line = spot >> (nx.bit_length() - 1)

        def look(q, acc):
            return jnp.where(line == q, jnp.take_along_axis(means[q], pos, axis=1), acc)

        val = lax.fori_loop(0, groups, look, jnp.zeros((8, nx), jnp.float32), unroll=small)
        beside = None
        for j in range(6):
            x = pltpu.roll(val, nx - n_loc * (1 + j), 1)
            beside = x if beside is None else beside + x
        smooth = 0.5 * head + (0.5 / 6.0) * beside
        refine = pltpu.roll(head, nx - 7 * n_loc, 1)
        owner = tail.astype(jnp.int32)
        weight = pltpu.roll(tail, nx - n_loc, 1)
        home = sub + 8 * g
        c = smooth * (1.0 + 7.0 * refine) + jnp.where(owner != home, 0.25 * weight, 0.0)
        acc_load = acc_load + jnp.where(ok & (owner == me), c, 0.0)
        acc_cost = acc_cost + jnp.where(home == me, c, 0.0)
        return acc_load, acc_cost

    zero = jnp.zeros((8, nx), jnp.float32)
    acc_load, acc_cost = lax.fori_loop(0, groups, group, (zero, zero), unroll=small)
    own = jnp.sum(acc_cost, axis=0, keepdims=True)
    for b in range(n_loc // per_ax):
        x = own if b == 0 else pltpu.roll(own, nx - b * per_ax, 1)
        cost[0, pl.ds(b, 1), :] = x[:, 0:per_ax]
    total = jnp.sum(jnp.sum(acc_load, axis=0, keepdims=True), axis=1, keepdims=True) * (1.0 / n_loc)
    load[0] = total
    for i, (x, y) in enumerate(((cost, cost_out), (load, load_out))):
        leave.append(pltpu.make_async_copy(x, y, sems.at[3 + i]))
        leave[-1].start()
    for c in leave:
        c.wait()


def on_device(primal, adjoint, refine_flag, owner_map, migrate_weight, neighbor_list):
    _, nr, na, nx = primal.shape
    dims = (nr, na, nx)
    sizes = n_rad, n_azi, n_ax = tuple(lax.axis_size(a) for a in AXES)
    n_dev = n_rad * n_azi * n_ax
    tiles = na // 8
    halves = nr * tiles // (nx // 4)
    f32 = functools.partial(jax.ShapeDtypeStruct, dtype=jnp.float32)
    anyspec = pl.BlockSpec(memory_space=pl.ANY)
    hbm = pl.BlockSpec(memory_space=pltpu.HBM)
    vmem = pl.BlockSpec(memory_space=pltpu.VMEM)

    rad_a, rad_b, azi_s = pl.pallas_call(
        functools.partial(edge_kernel, dims, n_rad),
        out_shape=(f32((2 * F, 2, na, nx)), f32((2 * F, 2, na, nx)), f32((2 * F, nr, 4, nx))),
        in_specs=[hbm, hbm],
        out_specs=(vmem, vmem, vmem),
        scratch_shapes=[pltpu.SemaphoreType.DMA((2, 4))],
        compiler_params=pltpu.CompilerParams(vmem_limit_bytes=8 << 20),
        name="edges",
    )(*(pltpu.with_memory_space_constraint(x, pltpu.HBM) for x in (primal, adjoint)))
    ax_first, ax_second = pl.pallas_call(
        functools.partial(lane_kernel, dims),
        out_shape=(f32((2 * F, halves // 2, 8, nx)),) * 2,
        in_specs=[vmem, vmem],
        out_specs=(vmem, vmem),
        compiler_params=pltpu.CompilerParams(vmem_limit_bytes=16 << 20),
        name="lanes",
    )(primal, adjoint)

    ax_a = lax.ppermute(ax_first, AXES, pair_round(sizes, 2, 0))
    ax_b = lax.ppermute(ax_second, AXES, pair_round(sizes, 2, 1))
    azi_l = lax.ppermute(azi_s, "azi", ring(n_azi, 1))
    azi_r = azi_l if n_azi == 2 else lax.ppermute(azi_s, "azi", ring(n_azi, -1))
    rad_a = lax.ppermute(rad_a, AXES, pair_round(sizes, 0, 0))
    rad_b = lax.ppermute(rad_b, AXES, pair_round(sizes, 0, 1))

    per_rad, per_azi, per_ax = nr // BLK, na // BLK, nx // BLK
    n_loc = per_rad * per_azi * per_ax
    near = neighbor_list.transpose(0, 3, 1, 2)
    cells = F * nr * na
    sums, fourth, row, part_bw = pl.pallas_call(
        functools.partial(inner_kernel, dims, ((per_rad, per_azi, per_ax), (n_azi, n_ax))),
        out_shape=(
            f32((cells, 2 * nx)),
            f32((cells, nx)),
            f32((1, 2 * nx)),
            f32((2 * F, nr, na, nx)),
        ),
        in_specs=[vmem] * 7,
        out_specs=(vmem,) * 4,
        scratch_shapes=[
            pltpu.VMEM((nr // PLANES, 2, F * PLANES * na, 3 * nx), jnp.bfloat16),
            pltpu.VMEM((3 * nx, 3 * nx), jnp.bfloat16),
            pltpu.VMEM((F, tiles, 8, nx), jnp.float32),
            pltpu.VMEM((F, 8 + na, nx), jnp.float32),
        ],
        compiler_params=pltpu.CompilerParams(vmem_limit_bytes=16 << 20),
        name="inner",
    )(primal, adjoint, ax_first, near, refine_flag, owner_map, migrate_weight)
    bw, done = pl.pallas_call(
        functools.partial(axial_kernel, dims, n_ax),
        out_shape=(f32((2 * F, nr, na, nx)), f32(dims)),
        in_specs=[vmem] * 5,
        out_specs=(vmem, vmem),
        scratch_shapes=[
            pltpu.VMEM((3, 2 * F, halves, 8, nx), jnp.float32),
            pltpu.VMEM((2 * cells, nx), jnp.bfloat16),
            pltpu.VMEM((nx, 3 * nx), jnp.bfloat16),
            pltpu.VMEM((cells, 2 * nx), jnp.float32),
            pltpu.VMEM((cells, nx), jnp.float32),
        ],
        compiler_params=pltpu.CompilerParams(vmem_limit_bytes=16 << 20),
        name="axial",
    )(sums, fourth, part_bw, ax_a, ax_b)

    inside, ends, part_sums = pl.pallas_call(
        functools.partial(rows_kernel, dims),
        out_shape=(f32(dims), f32((2 * F, 4, na, nx)), f32((tiles, 8, nx))),
        in_specs=[vmem] * 5,
        out_specs=(vmem,) * 3,
        compiler_params=pltpu.CompilerParams(vmem_limit_bytes=16 << 20),
        name="rows",
    )(primal, bw, done, azi_l, azi_r)
    outside, send = pl.pallas_call(
        functools.partial(main_kernel, dims, n_rad),
        out_shape=(f32((4, na, nx)), f32((2 * n_dev, nx))),
        in_specs=[vmem] * 6,
        out_specs=(vmem, vmem),
        compiler_params=pltpu.CompilerParams(vmem_limit_bytes=16 << 20),
        name="planes",
    )(primal, ends, part_sums, rad_a, rad_b, row)

    data = lax.all_to_all(send, AXES, 0, 0, tiled=True)

    cost, load, indicator = pl.pallas_call(
        functools.partial(final_kernel, n_loc, per_ax),
        out_shape=(f32((per_rad, per_azi, per_ax)), f32((1, 1, 1)), f32(dims)),
        in_specs=[vmem, anyspec, anyspec],
        out_specs=(anyspec,) * 3,
        scratch_shapes=[
            pltpu.VMEM((per_rad, per_azi, per_ax), jnp.float32),
            pltpu.VMEM((1, 1, 1), jnp.float32),
            pltpu.VMEM((n_dev // 8, 8, nx), jnp.float32),
            pltpu.SemaphoreType.DMA((5,)),
        ],
        compiler_params=pltpu.CompilerParams(vmem_limit_bytes=4 << 20),
        name="blocks",
    )(data, inside, outside)
    return indicator, cost, load


def solution(mesh):
    spec = P("rad", "azi", "ax")
    field = P(None, "rad", "azi", "ax")
    return jax.shard_map(
        on_device,
        mesh=mesh,
        in_specs=(field, field, spec, spec, spec, P("rad", "azi", "ax", None)),
        out_specs=(spec, spec, spec),
        check_vma=False,
    )
```
